512 devices in a mesh: gx: 64 (over z_lo, x, y), gy: 8 (over z_hi, core).
Axes of the slice: x: 4, y: 8, z: 8 (z_hi: 4, z_lo: 2; z = z_hi * 2 + z_lo), core: 2. Of those that a mesh axis runs over, the one named last changes fastest.
Arguments:
- position: float32 [3, 2097152], P(None, ('gx', 'gy')), may hold values from 0.05 to 0.95, as said below
- momentum: float32 [3, 2097152], P(None, ('gx', 'gy')), may hold values from -1.6 to 1.6, as said below
- cell_first: int32 [3, 2097152], P(None, ('gx', 'gy')), may hold values from 0 to 255, as said below
- cell_second: int32 [3, 2097152], P(None, ('gx', 'gy')), may hold values from 0 to 255, as said below
- destination: int32 [2097152], P(('gx', 'gy')), may hold values from 0 to 4, as said below
- slot_index: int32 [2097152], P(('gx', 'gy')), may hold values from 0 to 4095, as said below
- pull_position: float32 [3, 2097152], P(None, ('gx', 'gy')), may hold values from -6 to 6
- pull_momentum: float32 [3, 2097152], P(None, ('gx', 'gy')), may hold values from -6 to 6
Outputs:
- grad_position: float32 [3, 2097152], P(None, ('gx', 'gy'))
- grad_momentum: float32 [3, 2097152], P(None, ('gx', 'gy'))
The draws below stay inside these ranges and needn't reach their ends.
Inputs may be any that keep to these rules, and one draw needn't show every extreme that they name: `destination`: 0: the particle stays on its device; 1 and 2: it moves to the next and to the previous device along gx; 3 and 4: to the next and to the previous device along gy (both axes wrap). From the particles of one device at most 256 go to each of its four neighbours, and in every draw some device sends exactly 256 to one neighbour. Between two neighbouring devices as many particles move one way as the other. A particle that moves to the next (previous) device along an axis lies in the last (first) cell layer of its device along that axis in cell_first. Over all particles the destination device and slot_index fill every index of every device exactly once. `cell_first`: the first component is below 2, the second below 8, the third below 256. `cell_second`: the cell_first of the particle that lands at this index, moved with it: a particle moving along gx goes from the last layer to the first or from the first to the last, likewise along gy; other components stay. The first component is below 2, the second below 8, the third below 256. `position`: A particle's drift_one leaves its cell along an axis exactly where destination sends it across that axis, in that direction. `momentum`: momenta of particles that move carry them across the cell face toward their destination.
All inputs are finite; a program needn't handle non-finite values.
Results may differ from the reference program's by a relative error of at most 0.000058.
Values sent between devices are 32-bit elements; how exact they have to be, the bound alone decides.
No kernel may reach another device: no remote copies, remote signals or barrier semaphores. Data moves between devices by JAX's collectives and lax.ppermute only.
A program may use at most 64 MiB of HBM per device.

```python
import jax
import jax.numpy as jnp
from jax import lax

CX = 2
CY = 8
NZ = 256
PART_DEV = 4096
MOVE_MOST = 256
NX = 128
NY = 64
PARTICLES = 2097152
N_GX = 64
N_GY = 8


def edge_counts(key_pair, key_spot):
    half_most = MOVE_MOST // 2
    counts = half_most + jax.random.randint(key_pair[0], (N_GX, N_GY), 0, MOVE_MOST - half_most + 1)
    counts = jnp.maximum(counts, 1)
    full_spot = jax.random.randint(key_spot, (), 0, N_GX * N_GY)
    return counts.reshape(-1).at[full_spot].set(MOVE_MOST).reshape(N_GX, N_GY)


def shuffled(key, devices):

    def one_order(one_key):
        return jax.random.permutation(one_key, PART_DEV).astype(jnp.int32)
    return jax.vmap(one_order)(jax.random.split(key, devices))


def move_plan(key):
    keys = jax.random.split(jax.random.fold_in(key, 4242), 12)
    devices = N_GX * N_GY
    east_edges = edge_counts(keys[0:2], keys[2])
    north_edges = edge_counts(keys[3:5], keys[5])
    to_east = east_edges.reshape(-1)
    to_west = jnp.roll(east_edges, 1, axis=0).reshape(-1)
    to_north = north_edges.reshape(-1)
    to_south = jnp.roll(north_edges, 1, axis=1).reshape(-1)
    bound_one = to_east[:, None]
    bound_two = bound_one + to_west[:, None]
    bound_three = bound_two + to_north[:, None]
    leaving = bound_three + to_south[:, None]
    ranks = shuffled(keys[6], devices)
    move_code = jnp.where(ranks < bound_one, 1, jnp.where(ranks < bound_two, 2, jnp.where(ranks < bound_three, 3, jnp.where(ranks < leaving, 4, 0))))
    device = jnp.arange(devices, dtype=jnp.int32)[:, None]
    eastward = (move_code == 1).astype(jnp.int32) - (move_code == 2).astype(jnp.int32)
    northward = (move_code == 3).astype(jnp.int32) - (move_code == 4).astype(jnp.int32)
    receiver = (device // N_GY + eastward) % N_GX * N_GY + (device % N_GY + northward) % N_GY
    opening = PART_DEV - leaving[:, 0][receiver]
    after_west = opening + to_west[receiver]
    after_east = after_west + to_east[receiver]
    after_south = after_east + to_south[receiver]
    listed = jnp.where(move_code == 0, ranks - leaving, jnp.where(move_code == 1, opening + ranks, jnp.where(move_code == 2, after_west + ranks - bound_one, jnp.where(move_code == 3, after_east + ranks - bound_two, after_south + ranks - bound_three))))
    mixing = shuffled(keys[7], devices)
    slot_index = mixing.reshape(-1)[receiver * PART_DEV + listed]
    first_x = jnp.where(move_code == 1, CX - 1, jnp.where(move_code == 2, 0, jax.random.randint(keys[8], (devices, PART_DEV), 0, CX)))
    first_y = jnp.where(move_code == 3, CY - 1, jnp.where(move_code == 4, 0, jax.random.randint(keys[9], (devices, PART_DEV), 0, CY)))
    depth_cell = jax.random.randint(keys[10], (devices, PART_DEV), 0, NZ)
    second_x = jnp.where(move_code == 1, 0, jnp.where(move_code == 2, CX - 1, first_x))
    second_y = jnp.where(move_code == 3, 0, jnp.where(move_code == 4, CY - 1, first_y))
    placed = (receiver * PART_DEV + slot_index).reshape(-1)
    cell_first = jnp.stack([first_x, first_y, depth_cell], 0).reshape(3, -1).astype(jnp.int32)
    moved_cells = jnp.stack([second_x, second_y, depth_cell], 0).reshape(3, -1).astype(jnp.int32)
    cell_second = jnp.zeros_like(cell_first).at[:, placed].set(moved_cells)
    return (move_code.reshape(-1).astype(jnp.int32), slot_index.reshape(-1).astype(jnp.int32), cell_first, cell_second)


def particle_state(key):
    move_code = move_plan(key)[0]
    keys = jax.random.split(jax.random.fold_in(key, 777), 4)
    count = move_code.shape[0]
    stay_offset = jax.random.uniform(keys[0], (3, count), jnp.float32, 0.35, 0.65)
    stay_speed = jax.random.uniform(keys[1], (3, count), jnp.float32, -0.5, 0.5)
    edge_offset = jax.random.uniform(keys[2], (3, count), jnp.float32, 0.82, 0.95)
    edge_speed = jax.random.uniform(keys[3], (3, count), jnp.float32, 1.0, 1.6)
    offsets = []
    speeds = []
    for axis_number, forward_code, backward_code in ((0, 1, 2), (1, 3, 4), (2, -1, -1)):
        ahead = move_code == forward_code
        behind = move_code == backward_code
        offsets.append(jnp.where(ahead, edge_offset[axis_number], jnp.where(behind, 1.0 - edge_offset[axis_number], stay_offset[axis_number])))
        speeds.append(jnp.where(ahead, edge_speed[axis_number], jnp.where(behind, -edge_speed[axis_number], stay_speed[axis_number])))
    return (jnp.stack(offsets, 0).astype(jnp.float32), jnp.stack(speeds, 0).astype(jnp.float32))


def draw_position(key, part):
    return particle_state(key)[0]


def draw_momentum(key, part):
    return particle_state(key)[1]


def draw_destination(key, part):
    return move_plan(key)[0]


def draw_slot_index(key, part):
    return move_plan(key)[1]


def draw_cell_first(key, part):
    return move_plan(key)[2]


def draw_cell_second(key, part):
    return move_plan(key)[3]


def steps_of(stream_key, shape, shards, low, largest):
    factor_of = 1.0
    for dim, parts in shards:
        draws = jax.random.uniform(jax.random.fold_in(jax.random.fold_in(stream_key, 6), dim), (parts,), jnp.float32, low / len(shards), largest / len(shards))
        factor_of = factor_of * jnp.repeat(jnp.exp(draws), shape[dim] // parts).reshape((-1,) + (1,) * (len(shape) - 1 - dim))
    return factor_of


def gaussian(own_key, dims, width, limit, cuts=(), held_as=jnp.bfloat16):
    result = width * jax.random.normal(own_key, dims, jnp.float32)
    if cuts:
        result = result * steps_of(own_key, dims, cuts, -0.22, 0.18)
    return jnp.clip(result, -limit, limit).astype(held_as)


def setup_inputs(seed: int = 0) -> dict:
    key_of = jax.random.split(jax.random.key(seed), 9)
    return {
        "position": draw_position(jax.random.fold_in(key_of[8], 71), 0),
        "momentum": draw_momentum(jax.random.fold_in(key_of[8], 71), 0),
        "cell_first": draw_cell_first(jax.random.fold_in(key_of[8], 71), 0),
        "cell_second": draw_cell_second(jax.random.fold_in(key_of[8], 71), 0),
        "destination": draw_destination(jax.random.fold_in(key_of[8], 71), 0),
        "slot_index": draw_slot_index(jax.random.fold_in(key_of[8], 71), 0),
        "pull_position": gaussian(key_of[6], (3, PARTICLES), 1.0, 6.0, ((1, 512),), jnp.float32),
        "pull_momentum": gaussian(key_of[7], (3, PARTICLES), 1.0, 6.0, ((1, 512),), jnp.float32),
    }


highest = lax.Precision.HIGHEST
step_size = 0.25
strength = 0.02

def kernel_matrix(extent, reach_cells):
    axis_cells = jnp.arange(extent, dtype=jnp.int32)
    distance = jnp.abs(axis_cells[:, None] - axis_cells[None, :])
    distance = jnp.minimum(distance, extent - distance)
    return jnp.exp(-distance.astype(jnp.float32) / reach_cells)

def global_cells(cell_ids):
    device = jnp.arange(cell_ids.shape[1], dtype=jnp.int32) // PART_DEV
    column_x = device // N_GY * CX + cell_ids[0]
    column_y = device % N_GY * CY + cell_ids[1]
    return (column_x, column_y, cell_ids[2])

def corner_terms(cell_ids, offsets):
    base_x, base_y, base_z = global_cells(cell_ids)
    lower = 1.0 - offsets
    terms = []
    for step_x in (0, 1):
        for step_y in (0, 1):
            for step_z in (0, 1):
                weight_x = offsets[0] if step_x == 1 else lower[0]
                weight_y = offsets[1] if step_y == 1 else lower[1]
                weight_z = offsets[2] if step_z == 1 else lower[2]
                weight = weight_x * weight_y * weight_z
                terms.append(((base_x + step_x) % NX, (base_y + step_y) % NY, (base_z + step_z) % NZ, weight))
    return terms

def particle_force(cell_ids, offsets):
    terms = corner_terms(cell_ids, offsets)
    density = jnp.zeros((NX, NY, NZ), jnp.float32)
    for index_x, index_y, index_z, weight in terms:
        density = density.at[index_x, index_y, index_z].add(weight)
    line_sums = jnp.einsum('ab,xbz->xaz', kernel_matrix(NY, NY / 4.0), density, precision=highest)
    potential = strength * jnp.einsum('xyz,zw->xyw', line_sums, kernel_matrix(NZ, NZ / 16.0), precision=highest)
    forces = []
    for direction in range(3):
        push_field = -0.5 * (jnp.roll(potential, -1, direction) - jnp.roll(potential, 1, direction))
        running = jnp.zeros_like(offsets[0])
        for index_x, index_y, index_z, weight in terms:
            running = running + weight * push_field[index_x, index_y, index_z]
        forces.append(running)
    return jnp.stack(forces, 0)

def leapfrog(position, momentum, cell_first, cell_second, destination, slot_index):
    drift_one = position + step_size * momentum
    kick_one = momentum + step_size * particle_force(cell_first, drift_one)
    device = jnp.arange(position.shape[1], dtype=jnp.int32) // PART_DEV
    eastward = (destination == 1).astype(jnp.int32) - (destination == 2).astype(jnp.int32)
    northward = (destination == 3).astype(jnp.int32) - (destination == 4).astype(jnp.int32)
    receiver = (device // N_GY + eastward) % N_GX * N_GY + (device % N_GY + northward) % N_GY
    placed = receiver * PART_DEV + slot_index
    shift_cells = jnp.stack([eastward, northward, jnp.zeros_like(eastward)], 0).astype(jnp.float32)
    moved_position = jnp.zeros_like(position).at[:, placed].set(drift_one - shift_cells)
    moved_momentum = jnp.zeros_like(momentum).at[:, placed].set(kick_one)
    drift_two = moved_position + step_size * moved_momentum
    kick_two = moved_momentum + step_size * particle_force(cell_second, drift_two)
    return (drift_two, kick_two)

def reference(position, momentum, cell_first, cell_second, destination, slot_index, pull_position, pull_momentum):

    def forward(start_position, start_momentum):
        return leapfrog(start_position, start_momentum, cell_first, cell_second, destination, slot_index)
    unused, pullback = jax.vjp(forward, position, momentum)
    grad_position, grad_momentum = pullback((pull_position, pull_momentum))
    return (grad_position, grad_momentum)
```

```python
import jax
import jax.numpy as jnp
from jax import lax
from jax.sharding import PartitionSpec as P

CX = 2
CY = 8
NZ = 256
MOVE_MOST = 256


highest = lax.Precision.HIGHEST
step_size = 0.25
strength = 0.02


def with_halo(x, sides, width):
    for axis, dim in sides:
        peers, length = (lax.axis_size(axis), x.shape[dim])
        up = [(i, (i + 1) % peers) for i in range(peers)]
        down = [(j, i) for i, j in up]
        last = lax.slice_in_dim(x, length - width, length, axis=dim)
        first = lax.slice_in_dim(x, 0, width, axis=dim)
        before = lax.ppermute(last, axis, up)
        after = lax.ppermute(first, axis, down)
        x = jnp.concatenate([before, x, after], axis=dim)
    return x


def kernel_block(targets, sources, extent, reach_cells):
    distance = jnp.abs(targets[:, None] - sources[None, :])
    distance = jnp.minimum(distance, extent - distance)
    return jnp.exp(-distance.astype(jnp.float32) / reach_cells)


def cloud_weights(cell_block, frac_block, plane_count, row_count, depth_cells):
    index_row = jnp.arange(row_count, dtype=jnp.int32)[:, None]
    corner = (cell_block[1] * plane_count + cell_block[0])[None, :]
    hit_base = (index_row == corner).astype(jnp.float32)
    hit_east = (index_row == corner + 1).astype(jnp.float32)
    hit_north = (index_row == corner + plane_count).astype(jnp.float32)
    hit_both = (index_row == corner + plane_count + 1).astype(jnp.float32)
    west_weight = (1.0 - frac_block[0])[None, :]
    east_weight = frac_block[0][None, :]
    south_weight = (1.0 - frac_block[1])[None, :]
    north_weight = frac_block[1][None, :]
    planar = (
        hit_base * (west_weight * south_weight)
        + hit_east * (east_weight * south_weight)
        + hit_north * (west_weight * north_weight)
        + hit_both * (east_weight * north_weight)
    )
    slope_east = (hit_east - hit_base) * south_weight + (hit_both - hit_north) * north_weight
    slope_north = (hit_north - hit_base) * west_weight + (hit_both - hit_east) * east_weight
    index_depth = jnp.arange(depth_cells, dtype=jnp.int32)[:, None]
    lower_hit = (index_depth == cell_block[2][None, :]).astype(jnp.float32)
    upper_hit = (index_depth == ((cell_block[2] + 1) % depth_cells)[None, :]).astype(jnp.float32)
    vertical = lower_hit * (1.0 - frac_block[2])[None, :] + upper_hit * frac_block[2][None, :]
    slope_up = upper_hit - lower_hit
    return (planar, slope_east, slope_north, vertical, slope_up)


def particle_blocks(values):
    particle_count = values.shape[1]
    block_width = min(512, particle_count)
    return values.reshape(values.shape[0], particle_count // block_width, block_width).transpose(
        1, 0, 2
    )


def deposit(scales, cell_ids, offsets):
    layers = scales.shape[0]
    row_count = (CY + 1) * (CX + 1)

    def add_block(running, pieces):
        cell_block, frac_block, scale_block = pieces
        weights = cloud_weights(cell_block, frac_block, CX + 1, row_count, NZ)
        spread = scale_block[:, None, :] * weights[0][None]
        return (running + jnp.einsum("crb,zb->crz", spread, weights[3], precision=highest), None)

    initial = jnp.zeros((layers, row_count, NZ), jnp.float32)
    running, unused = lax.scan(
        add_block,
        initial,
        (particle_blocks(cell_ids), particle_blocks(offsets), particle_blocks(scales)),
    )
    return running.reshape(layers, CY + 1, CX + 1, NZ)


def sample_fields(fields, cell_ids, offsets, slopes):
    layers = fields.shape[0]
    row_count = fields.shape[1] * fields.shape[2]
    flattened = fields.reshape(layers * row_count, NZ)

    def one_block(pieces):
        cell_block, frac_block = pieces
        block_width = cell_block.shape[1]
        weights = cloud_weights(cell_block, frac_block, fields.shape[2], row_count, NZ)
        columns = jnp.concatenate([weights[3], weights[4]], 1) if slopes else weights[3]
        contracted = jnp.dot(
            flattened, columns, precision=highest, preferred_element_type=jnp.float32
        )
        contracted = contracted.reshape(layers, row_count, -1)
        nearby = contracted[:, :, :block_width]
        results = [jnp.sum(nearby * weights[0][None], axis=1)]
        if slopes:
            results.append(jnp.sum(nearby * weights[1][None], axis=1))
            results.append(jnp.sum(nearby * weights[2][None], axis=1))
            results.append(jnp.sum(contracted[:, :, block_width:] * weights[0][None], axis=1))
        return jnp.stack(results, 0)

    blocked = lax.map(one_block, (particle_blocks(cell_ids), particle_blocks(offsets)))
    return blocked.transpose(1, 2, 0, 3).reshape(blocked.shape[1], layers, cell_ids.shape[1])


def fold_planes(slab):
    planes = slab.shape[2]
    widened = with_halo(slab, (("gx", 2),), 2)
    return jnp.concatenate(
        [
            widened[:, :, 0:1],
            widened[:, :, 1:2] + widened[:, :, 2:3],
            widened[:, :, 3 : planes + 1],
            widened[:, :, planes + 1 : planes + 2] + widened[:, :, planes + 2 : planes + 3],
            widened[:, :, planes + 3 : planes + 4],
        ],
        axis=2,
    )


def smooth_depth(field):
    depth_cells = field.shape[-1]
    axis_cells = jnp.arange(depth_cells, dtype=jnp.int32)
    matrix = kernel_block(axis_cells, axis_cells, depth_cells, depth_cells / 16.0)
    return jnp.dot(
        field.reshape(-1, depth_cells),
        matrix,
        precision=highest,
        preferred_element_type=jnp.float32,
    ).reshape(field.shape)


def sum_lines(field):
    members = lax.axis_size("gy")
    band_rows = field.shape[1]
    own_rows = band_rows - 1
    extent = own_rows * members
    reach_cells = extent / 4.0
    anchor = lax.axis_index("gy") * own_rows
    targets = (anchor + jnp.arange(-1, own_rows + 2, dtype=jnp.int32)) % extent
    initial = jnp.zeros((field.shape[0], own_rows + 3, field.shape[2], field.shape[3]), jnp.float32)
    gathered = lax.all_gather(field, "gy", axis=1, tiled=True)
    length = gathered.shape[1]
    positions = jnp.arange(length, dtype=jnp.int32)
    sources = (positions // band_rows * own_rows + positions % band_rows) % extent
    weights = kernel_block(targets, sources, extent, reach_cells)
    return initial + jnp.einsum("ab,cbxz->caxz", weights, gathered, precision=highest)


def force_field(density):
    potential = sum_lines(smooth_depth(fold_planes(density)))
    potential = strength * potential
    centre = potential[:, 1:-1, 1:-1]
    push_east = -0.5 * (potential[:, 1:-1, 2:] - potential[:, 1:-1, :-2])
    push_north = -0.5 * (potential[:, 2:, 1:-1] - potential[:, :-2, 1:-1])
    push_up = -0.5 * (jnp.roll(centre, -1, 3) - jnp.roll(centre, 1, 3))
    return jnp.concatenate([push_east, push_north, push_up], 0)


def force_pullback(pushes, cell_ids, offsets, pull_force):
    folded = fold_planes(deposit(pull_force, cell_ids, offsets))
    across = 0.5 * (folded[0:1, :, 2:] - folded[0:1, :, :-2])
    upward = folded[2:3, :, 1:-1]
    across = across + 0.5 * (jnp.roll(upward, -1, 3) - jnp.roll(upward, 1, 3))
    line_sums = sum_lines(jnp.concatenate([across, folded[1:2, :, 1:-1]], 0))
    summed = line_sums[0:1, 1:-1] + 0.5 * (line_sums[1:2, 2:] - line_sums[1:2, :-2])
    density_pull = strength * smooth_depth(summed)
    sampled = sample_fields(jnp.concatenate([pushes, density_pull], 0), cell_ids, offsets, True)
    slopes = sampled[1:]
    return jnp.sum(slopes[:, :3] * pull_force[None], axis=1) + slopes[:, 3]


def pack_moves(destination, capacity):
    particle_count = destination.shape[0]
    grouped = jnp.argsort(destination, stable=True)
    group_size = jnp.sum(
        (destination[None, :] == jnp.arange(5, dtype=jnp.int32)[:, None]).astype(jnp.int32), axis=1
    )
    earlier = jnp.arange(5, dtype=jnp.int32)[None, :] < jnp.arange(5, dtype=jnp.int32)[:, None]
    opening = jnp.sum(jnp.where(earlier, group_size[None, :], 0), axis=1)
    lane_index = jnp.arange(capacity, dtype=jnp.int32)
    chosen = jnp.stack(
        [
            grouped[jnp.minimum(opening[move_code] + lane_index, particle_count - 1)]
            for move_code in range(1, 5)
        ],
        0,
    )
    filled = lane_index[None, :] < group_size[1:5, None]
    return (chosen, filled)


def trade_pairs(outward_x, outward_y):
    widened_x = with_halo(outward_x, (("gx", 1),), 1)
    widened_y = with_halo(outward_y, (("gy", 1),), 1)
    return (widened_x[:, 0], widened_x[:, 3], widened_y[:, 0], widened_y[:, 3])


def local(
    position,
    momentum,
    cell_first,
    cell_second,
    destination,
    slot_index,
    pull_position,
    pull_momentum,
):
    particle_count = position.shape[1]
    unit_mass = jnp.ones((1, particle_count), jnp.float32)
    drift_one = position + step_size * momentum
    push_one = force_field(deposit(unit_mass, cell_first, drift_one))
    kick_one = momentum + step_size * sample_fields(push_one, cell_first, drift_one, False)[0]
    eastward = (destination == 1).astype(jnp.float32) - (destination == 2).astype(jnp.float32)
    northward = (destination == 3).astype(jnp.float32) - (destination == 4).astype(jnp.float32)
    shift_cells = jnp.stack([eastward, northward, jnp.zeros_like(eastward)], 0)
    payload = jnp.concatenate([drift_one - shift_cells, kick_one], 0)
    chosen, filled = pack_moves(destination, MOVE_MOST)
    slot_marks = jnp.where(filled, slot_index[chosen], particle_count).astype(jnp.float32)
    parcel = jnp.where(filled[None], payload[:, chosen], 0.0)
    parcel = jnp.concatenate([parcel, slot_marks[None]], 0)
    arrivals = trade_pairs(
        jnp.stack([parcel[:, 1], parcel[:, 0]], 1), jnp.stack([parcel[:, 3], parcel[:, 2]], 1)
    )
    arrivals = jnp.concatenate(arrivals, 1)
    received = arrivals[6].astype(jnp.int32)
    staying = jnp.where(destination == 0, slot_index, particle_count)
    placed = jnp.concatenate([staying, received], 0)
    arrived = (
        jnp.zeros((6, particle_count), jnp.float32)
        .at[:, placed]
        .set(jnp.concatenate([payload, arrivals[:6]], 1), mode="drop")
    )
    drift_two = arrived[:3] + step_size * arrived[3:]
    push_two = force_field(deposit(unit_mass, cell_second, drift_two))
    grad_drift_two = pull_position + force_pullback(
        push_two, cell_second, drift_two, step_size * pull_momentum
    )
    grad_kick_two = pull_momentum + step_size * grad_drift_two
    returning = jnp.concatenate([grad_drift_two, grad_kick_two], 0)
    sent_back = jnp.where(
        received[None] < particle_count,
        returning[:, jnp.minimum(received, particle_count - 1)],
        0.0,
    )
    sent_back = sent_back.reshape(6, 4, MOVE_MOST)
    homecoming = trade_pairs(sent_back[:, 0:2], sent_back[:, 2:4])
    returned = jnp.stack([homecoming[1], homecoming[0], homecoming[3], homecoming[2]], 1)
    gathered_home = jnp.where(destination[None] == 0, returning[:, slot_index], 0.0)
    home_spots = jnp.where(filled, chosen, particle_count).reshape(-1)
    gathered_home = gathered_home.at[:, home_spots].set(returned.reshape(6, -1), mode="drop")
    grad_drift_one = gathered_home[:3] + force_pullback(
        push_one, cell_first, drift_one, step_size * gathered_home[3:]
    )
    grad_momentum = gathered_home[3:] + step_size * grad_drift_one
    return (grad_drift_one, grad_momentum)


def solution(mesh):
    return jax.shard_map(
        local,
        mesh=mesh,
        in_specs=(
            P(None, ("gx", "gy")),
            P(None, ("gx", "gy")),
            P(None, ("gx", "gy")),
            P(None, ("gx", "gy")),
            P(("gx", "gy")),
            P(("gx", "gy")),
            P(None, ("gx", "gy")),
            P(None, ("gx", "gy")),
        ),
        out_specs=(P(None, ("gx", "gy")), P(None, ("gx", "gy"))),
        check_vma=False,
    )
```

```python
import functools

import jax
import jax.numpy as jnp
from jax import lax
from jax.experimental import pallas as pl
from jax.experimental.pallas import tpu as pltpu
from jax.sharding import PartitionSpec as P

CX = 2
CY = 8
NZ = 256
NQ = 4096
BLK = 256
ROWS = 16
TABLES = 5
STEP = 0.25
STRENGTH = 0.02
F32 = jnp.float32
BF16 = jnp.bfloat16
highest = lax.Precision.HIGHEST
VMEM_LIMIT = 48 * 1024 * 1024


def shape(*dims, dtype=F32):
    return jax.ShapeDtypeStruct(dims, dtype)


def call(body, outs, scratch=()):
    return pl.pallas_call(
        body,
        out_shape=outs,
        scratch_shapes=list(scratch),
        compiler_params=pltpu.CompilerParams(vmem_limit_bytes=VMEM_LIMIT),
    )


def split(x):
    high = x.astype(BF16)
    return high, (x - high.astype(F32)).astype(BF16)


def one_hot(index):
    rows = lax.broadcasted_iota(jnp.int32, (256, index.shape[1]), 0)
    return jnp.where(rows == index, 1.0, 0.0).astype(BF16)


def spread_onto(values, hot):
    return lax.dot_general(values, hot, (((1,), (1,)), ((), ())), preferred_element_type=F32)


def pick_from(table, hot):
    return jnp.dot(table, hot, preferred_element_type=F32)


def next_z(x):
    return pltpu.roll(x, NZ - 1, 1)


def prev_z(x):
    return pltpu.roll(x, 1, 1)


def diff_z(x):
    return 0.5 * (next_z(x) - prev_z(x))


def diff_row(x):
    return 0.5 * (pltpu.roll(x, ROWS - 1, 0) - pltpu.roll(x, 1, 0))


def axis_hits(rows, pitch, padded, cell_x, cell_y):
    index = lax.broadcasted_iota(jnp.int32, (padded, cell_x.shape[1]), 0)
    row_x = index // pitch
    row_y = index - row_x * pitch
    away_x = row_x - cell_x
    away_y = row_y - cell_y
    return away_x == 0, away_x == 1, away_y == 0, away_y == 1


def weights_of(hits, frac_x, frac_y):
    low_x, high_x, low_y, high_y = hits
    along_x = jnp.where(low_x, 1.0 - frac_x, jnp.where(high_x, frac_x, 0.0))
    along_y = jnp.where(low_y, 1.0 - frac_y, jnp.where(high_y, frac_y, 0.0))
    return along_x, along_y


def slopes_of(hits):
    low_x, high_x, low_y, high_y = hits
    along_x = jnp.where(low_x, -1.0, jnp.where(high_x, 1.0, 0.0))
    along_y = jnp.where(low_y, -1.0, jnp.where(high_y, 1.0, 0.0))
    return along_x, along_y


def row3(ref, at, first=0):
    return [ref[first + k : first + k + 1, at] for k in range(3)]


def line_matrix(me):
    target = lax.broadcasted_iota(jnp.int32, (ROWS, 8 * ROWS), 0)
    column = lax.broadcasted_iota(jnp.int32, (ROWS, 8 * ROWS), 1)
    device = column // ROWS
    source = column - device * ROWS
    away = (CY * (me - device) + target - source + 128) & 63
    away = jnp.minimum(away, 64 - away)
    return STRENGTH * jnp.exp(away.astype(F32) * (-1.0 / 16.0))


def depth_matrix():
    target = lax.broadcasted_iota(jnp.int32, (NZ, NZ), 0)
    source = lax.broadcasted_iota(jnp.int32, (NZ, NZ), 1)
    away = jnp.abs(target - source)
    away = jnp.minimum(away, NZ - away)
    return jnp.exp(away.astype(F32) * (-1.0 / 16.0))


def product(a, b):
    a_high, a_low = split(a)
    b_high, b_low = split(b)
    dot = functools.partial(jnp.dot, preferred_element_type=F32)
    return dot(a_high, b_high) + (dot(a_high, b_low) + dot(a_low, b_high))


def smooth(me, gathered, planes, kept):
    lines = line_matrix(me)
    for p in range(planes):
        source = gathered[:, p * ROWS : (p + 1) * ROWS, :].reshape(8 * ROWS, NZ)
        kept[p * ROWS : (p + 1) * ROWS, :] = product(lines, source)
    kept[0 : planes * ROWS, :] = product(kept[0 : planes * ROWS, :], depth_matrix())


def deposit_first_body(pos, mom, cell, pull_pos, pull_mom, own, up, down, acc):
    acc[...] = jnp.zeros_like(acc)

    def block(b, carry):
        at = pl.ds(pl.multiple_of(b * BLK, BLK), BLK)
        frac = [p + STEP * m for p, m in zip(row3(pos, at), row3(mom, at))]
        cells = row3(cell, at)
        along_x, along_y = weights_of(axis_hits(27, CY + 1, 32, cells[0], cells[1]), frac[0], frac[1])
        planar = along_x * along_y
        below = split(planar * (1.0 - frac[2]))
        above = split(planar * frac[2])
        hot = one_hot(cells[2])
        high = jnp.concatenate([below[0], above[0]], 0)
        low = jnp.concatenate([below[1], above[1]], 0)
        acc[...] += spread_onto(high, hot) + spread_onto(low, hot)
        return carry

    lax.fori_loop(0, NQ // BLK, block, 0, unroll=2)
    density = acc[0:32, :] + prev_z(acc[32:64, :])
    own[...] = jnp.zeros_like(own)
    for x in range(3):
        own[x * ROWS + 2 : x * ROWS + 11, :] = density[x * 9 : x * 9 + 9, :]
    up[0:32, :] = own[16:48, :]
    down[0:32, :] = own[0:32, :]
    for k in range(6):
        source = pull_pos if k < 3 else pull_mom
        for c in range(16):
            line = source[k % 3 : k % 3 + 1, c * 256 : (c + 1) * 256]
            at_row = 32 + k * 16 + c
            up[at_row : at_row + 1, :] = line
            down[at_row : at_row + 1, :] = line


def fold_first_body(own, left, right, pulls, out):
    out[0:16, :] = left[0:16, :]
    out[16:32, :] = own[0:16, :] + left[16:32, :]
    out[32:48, :] = own[16:32, :]
    out[48:64, :] = own[32:48, :] + right[0:16, :]
    out[64:80, :] = right[16:32, :]
    out[80:176, :] = pulls[32:128, :]


def step_body(
    place,
    pos,
    mom,
    cell,
    dest,
    slot,
    gathered,
    left,
    right,
    own,
    up,
    down,
    drift,
    pulls,
    field_high,
    field_low,
    kept,
    pack,
    table_high,
    table_low,
    acc,
    planes,
):
    me = place[0]
    smooth(me, gathered, 5, kept)
    pack[...] = jnp.zeros_like(pack)
    for x in range(3):
        mid = (x + 1) * ROWS
        east = kept[mid + 18 : mid + 27, :]
        west = kept[mid - 14 : mid - 5, :]
        pack[x * 9 : x * 9 + 9, :] = -0.5 * (east - west)
        north = kept[mid + 3 : mid + 12, :]
        south = kept[mid + 1 : mid + 10, :]
        pack[32 + x * 9 : 32 + x * 9 + 9, :] = -0.5 * (north - south)
        pack[64 + x * 9 : 64 + x * 9 + 9, :] = -diff_z(kept[mid : mid + 16, :])[2:11, :]
    for s in range(2):
        values = pack[...] if s == 0 else next_z(pack[...])
        high, low = split(values)
        field_high[s * 96 : (s + 1) * 96, :] = high
        field_low[s * 96 : (s + 1) * 96, :] = low
    ahead = lax.rem(me + 1, 8)
    behind = lax.rem(me + 7, 8)
    for t in range(TABLES):
        for k in range(6):
            first = 80 + k * 16
            if t == 0:
                values = gathered[me, first : first + 16, :]
            elif t == 1:
                values = right[first - 48 : first - 32, :]
            elif t == 2:
                values = left[first - 48 : first - 32, :]
            elif t == 3:
                values = gathered[ahead, first : first + 16, :]
            else:
                values = gathered[behind, first : first + 16, :]
            high, low = split(values)
            row = k * 80 + t * 16
            table_high[row : row + 16, :] = high
            table_low[row : row + 16, :] = low
    acc[...] = jnp.zeros_like(acc)

    def block(b, carry):
        at = pl.ds(pl.multiple_of(b * BLK, BLK), BLK)
        momentum = row3(mom, at)
        frac = [p + STEP * m for p, m in zip(row3(pos, at), momentum)]
        cells = row3(cell, at)
        moved = dest[:, at]
        where_to = slot[:, at]
        hot = one_hot(cells[2])
        along_x, along_y = weights_of(axis_hits(27, CY + 1, 32, cells[0], cells[1]), frac[0], frac[1])
        planar = along_x * along_y
        sampled = pick_from(field_high[...], hot) + pick_from(field_low[...], hot)
        below = planar * (1.0 - frac[2])
        above = planar * frac[2]
        force = [
            jnp.sum(
                below * sampled[d * 32 : d * 32 + 32, :] + above * sampled[96 + d * 32 : 128 + d * 32, :],
                axis=0,
                keepdims=True,
            )
            for d in range(3)
        ]
        to_x = jnp.where(moved == 1, 1, jnp.where(moved == 2, -1, 0))
        to_y = jnp.where(moved == 3, 1, jnp.where(moved == 4, -1, 0))
        shift = [to_x.astype(F32), to_y.astype(F32), 0.0]
        second = [frac[d] - shift[d] + STEP * (momentum[d] + STEP * force[d]) for d in range(3)]
        for d in range(3):
            drift[d : d + 1, at] = second[d]
        hot_slot = one_hot(where_to & 255)
        taken = pick_from(table_high[...], hot_slot) + pick_from(table_low[...], hot_slot)
        chosen = moved * 16 + lax.shift_right_logical(where_to, 8)
        here = lax.broadcasted_iota(jnp.int32, (80, BLK), 0) == chosen
        home = [
            jnp.sum(jnp.where(here, taken[k * 80 : k * 80 + 80, :], 0.0), axis=0, keepdims=True)
            for k in range(6)
        ]
        for k in range(6):
            pulls[k : k + 1, at] = home[k]
        along_x, along_y = weights_of(
            axis_hits(55, CY + 3, 64, cells[0] + to_x + 1, cells[1] + to_y + 1), second[0], second[1]
        )
        planar = along_x * along_y
        below = planar * (1.0 - second[2])
        above = planar * second[2]
        for c in range(4):
            scale = 1.0 if c == 0 else STEP * home[2 + c]
            high_b, low_b = split(below if c == 0 else below * scale)
            high_a, low_a = split(above if c == 0 else above * scale)
            high = jnp.concatenate([high_b, high_a], 0)
            low = jnp.concatenate([low_b, low_a], 0)
            acc[c * 128 : c * 128 + 128, :] += spread_onto(high, hot) + spread_onto(low, hot)
        return carry

    lax.fori_loop(0, NQ // BLK, block, 0)
    planes[...] = jnp.zeros_like(planes)
    for c in range(4):
        total = acc[c * 128 : c * 128 + 64, :] + prev_z(acc[c * 128 + 64 : c * 128 + 128, :])
        for x in range(5):
            planes[c, x, 1:12, :] = total[x * 11 : x * 11 + 11, :]
    for x in range(5):
        planes[2, x] = diff_row(planes[2, x]) + diff_z(planes[3, x])
    for c in range(3):
        for x in range(3):
            own[(c * 3 + x) * 16 : (c * 3 + x) * 16 + 16, :] = planes[c, x + 1]
        for x in range(2):
            up[(c * 2 + x) * 16 : (c * 2 + x) * 16 + 16, :] = planes[c, x + 3]
            down[(c * 2 + x) * 16 : (c * 2 + x) * 16 + 16, :] = planes[c, x]


def fold_body(channels, own, left, right, out):
    for c in range(channels):
        mine, theirs = c * 48, c * 32
        out[mine : mine + 16, :] = own[mine : mine + 16, :] + left[theirs : theirs + 16, :]
        out[mine + 16 : mine + 32, :] = (
            own[mine + 16 : mine + 32, :]
            + left[theirs + 16 : theirs + 32, :]
            + right[theirs : theirs + 16, :]
        )
        out[mine + 32 : mine + 48, :] = own[mine + 32 : mine + 48, :] + right[theirs + 16 : theirs + 32, :]


def lines_body(place, gathered, own, up, down):
    smooth(place[0], gathered, 9, own)
    for c in range(2):
        up[c * 32 : c * 32 + 32, :] = own[c * 48 : c * 48 + 32, :]
        down[c * 32 : c * 32 + 32, :] = own[c * 48 + 16 : c * 48 + 48, :]
    up[64:80, :] = own[112:128, :]
    down[64:80, :] = own[112:128, :]


def back_body(
    pos,
    mom,
    cell,
    dest,
    drift,
    pulls,
    mine,
    left,
    right,
    own,
    up,
    down,
    grads,
    wide,
    pack,
    field_high,
    field_low,
    acc,
    planes,
):
    for c in range(2):
        wide[c, 0:32, :] = left[c * 32 : c * 32 + 32, :]
        wide[c, 32:80, :] = mine[c * 48 : c * 48 + 48, :]
        wide[c, 80:112, :] = right[c * 32 : c * 32 + 32, :]
    wide[2, 16:32, :] = left[64:80, :]
    wide[2, 32:80, :] = mine[96:144, :]
    wide[2, 80:96, :] = right[64:80, :]
    pack[...] = jnp.zeros_like(pack)
    for x in range(5):
        mid = (x + 1) * 16
        first = x * 11
        pack[first : first + 11, :] = -0.5 * (wide[0, mid + 17 : mid + 28, :] - wide[0, mid - 15 : mid - 4, :])
        pack[64 + first : 75 + first, :] = -0.5 * (
            wide[0, mid + 2 : mid + 13, :] - wide[0, mid : mid + 11, :]
        )
        pack[128 + first : 139 + first, :] = -diff_z(wide[0, mid : mid + 16, :])[1:12, :]
        pack[192 + first : 203 + first, :] = (
            0.5 * (wide[1, mid + 17 : mid + 28, :] - wide[1, mid - 15 : mid - 4, :])
            + wide[2, mid + 1 : mid + 12, :]
        )
    for s in range(2):
        values = pack[...] if s == 0 else next_z(pack[...])
        high, low = split(values)
        field_high[s * 256 : (s + 1) * 256, :] = high
        field_low[s * 256 : (s + 1) * 256, :] = low
    acc[...] = jnp.zeros_like(acc)

    def block(b, carry):
        at = pl.ds(pl.multiple_of(b * BLK, BLK), BLK)
        cells = row3(cell, at)
        moved = dest[:, at]
        hot = one_hot(cells[2])
        second = row3(drift, at)
        pull_position = row3(pulls, at)
        pull_momentum = row3(pulls, at, 3)
        to_x = jnp.where(moved == 1, 1, jnp.where(moved == 2, -1, 0))
        to_y = jnp.where(moved == 3, 1, jnp.where(moved == 4, -1, 0))
        hits = axis_hits(55, CY + 3, 64, cells[0] + to_x + 1, cells[1] + to_y + 1)
        along_x, along_y = weights_of(hits, second[0], second[1])
        slope_x, slope_y = slopes_of(hits)
        sampled = pick_from(field_high[...], hot) + pick_from(field_low[...], hot)
        sides = []
        for s in range(2):
            mixed = sampled[s * 256 + 192 : s * 256 + 256, :]
            for d in range(3):
                mixed = mixed + (STEP * pull_momentum[d]) * sampled[s * 256 + d * 64 : s * 256 + d * 64 + 64, :]
            sides.append(mixed)
        level = sides[0] + second[2] * (sides[1] - sides[0])
        rise = sides[1] - sides[0]
        slopes = [
            jnp.sum(slope_x * (along_y * level), axis=0, keepdims=True),
            jnp.sum(slope_y * (along_x * level), axis=0, keepdims=True),
            jnp.sum(along_x * (along_y * rise), axis=0, keepdims=True),
        ]
        grad_drift = [pull_position[d] + slopes[d] for d in range(3)]
        grad_kick = [pull_momentum[d] + STEP * grad_drift[d] for d in range(3)]
        for d in range(3):
            grads[d : d + 1, at] = grad_drift[d]
            grads[d + 3 : d + 4, at] = grad_kick[d]
        frac = [p + STEP * m for p, m in zip(row3(pos, at), row3(mom, at))]
        along_x, along_y = weights_of(axis_hits(27, CY + 1, 32, cells[0], cells[1]), frac[0], frac[1])
        planar = along_x * along_y
        below = planar * (1.0 - frac[2])
        above = planar * frac[2]
        for c in range(3):
            scale = STEP * grad_kick[c]
            high_b, low_b = split(below * scale)
            high_a, low_a = split(above * scale)
            high = jnp.concatenate([high_b, high_a], 0)
            low = jnp.concatenate([low_b, low_a], 0)
            acc[c * 64 : c * 64 + 64, :] += spread_onto(high, hot) + spread_onto(low, hot)
        return carry

    lax.fori_loop(0, NQ // BLK, block, 0)
    planes[...] = jnp.zeros_like(planes)
    for c in range(3):
        total = acc[c * 64 : c * 64 + 32, :] + prev_z(acc[c * 64 + 32 : c * 64 + 64, :])
        for x in range(3):
            planes[c, x + 2, 2:11, :] = total[x * 9 : x * 9 + 9, :]
    for x in range(5):
        spread = 0.5 * (planes[0, x + 2] - planes[0, x])
        if 1 <= x <= 3:
            spread = spread + diff_row(planes[1, x + 1]) + diff_z(planes[2, x + 1])
        if 1 <= x <= 3:
            own[(x - 1) * 16 : x * 16, :] = spread
        if x >= 3:
            up[(x - 3) * 16 : (x - 2) * 16, :] = spread
        if x <= 1:
            down[x * 16 : (x + 1) * 16, :] = spread


def last_body(
    place, pos, mom, cell, grads, field_high, field_low, gathered, grad_pos, grad_mom, kept, pack, high, low
):
    smooth(place[0], gathered, 3, kept)
    pack[...] = jnp.zeros_like(pack)
    for x in range(3):
        pack[x * 9 : x * 9 + 9, :] = kept[x * 16 + 2 : x * 16 + 11, :]
    high[0:192, :] = field_high[...]
    low[0:192, :] = field_low[...]
    high[192:224, :], low[192:224, :] = split(pack[...])
    high[224:256, :], low[224:256, :] = split(next_z(pack[...]))

    def block(b, carry):
        at = pl.ds(pl.multiple_of(b * BLK, BLK), BLK)
        frac = [p + STEP * m for p, m in zip(row3(pos, at), row3(mom, at))]
        cells = row3(cell, at)
        hot = one_hot(cells[2])
        hits = axis_hits(27, CY + 1, 32, cells[0], cells[1])
        along_x, along_y = weights_of(hits, frac[0], frac[1])
        slope_x, slope_y = slopes_of(hits)
        grad_drift = row3(grads, at)
        grad_kick = row3(grads, at, 3)
        sampled = pick_from(high[...], hot) + pick_from(low[...], hot)
        sides = []
        for s in range(2):
            mixed = sampled[192 + s * 32 : 224 + s * 32, :]
            for d in range(3):
                mixed = mixed + (STEP * grad_kick[d]) * sampled[s * 96 + d * 32 : s * 96 + d * 32 + 32, :]
            sides.append(mixed)
        level = sides[0] + frac[2] * (sides[1] - sides[0])
        rise = sides[1] - sides[0]
        slopes = [
            jnp.sum(slope_x * (along_y * level), axis=0, keepdims=True),
            jnp.sum(slope_y * (along_x * level), axis=0, keepdims=True),
            jnp.sum(along_x * (along_y * rise), axis=0, keepdims=True),
        ]
        for d in range(3):
            total = grad_drift[d] + slopes[d]
            grad_pos[d : d + 1, at] = total
            grad_mom[d : d + 1, at] = grad_kick[d] + STEP * total
        return carry

    lax.fori_loop(0, NQ // BLK, block, 0, unroll=2)


def swap_x(up, down):
    peers = lax.axis_size("gx")
    forward = [(i, (i + 1) % peers) for i in range(peers)]
    backward = [((i + 1) % peers, i) for i in range(peers)]
    return lax.ppermute(up, "gx", forward), lax.ppermute(down, "gx", backward)


def gather_y(x):
    return lax.all_gather(x, "gy", axis=0, tiled=False)


def local(pos, mom, cell, cell_second, dest, slot, pull_pos, pull_mom):
    place = lax.axis_index("gy").astype(jnp.int32).reshape(1)
    dest = dest.reshape(1, NQ)
    slot = slot.reshape(1, NQ)
    scalar = pl.BlockSpec(memory_space=pltpu.SMEM)
    vmem = pl.BlockSpec(memory_space=pltpu.VMEM)

    def call_at(body, outs, scratch, operands):
        return pl.pallas_call(
            body,
            out_shape=outs,
            in_specs=[scalar] + [vmem] * operands,
            scratch_shapes=list(scratch),
            compiler_params=pltpu.CompilerParams(vmem_limit_bytes=VMEM_LIMIT),
        )

    own, up, down = call(
        deposit_first_body, (shape(48, NZ), shape(128, NZ), shape(128, NZ)), [pltpu.VMEM((64, NZ), F32)]
    )(pos, mom, cell, pull_pos, pull_mom)
    left, right = swap_x(up, down)
    gathered = gather_y(call(fold_first_body, shape(176, NZ))(own, left, right, up))
    own, up, down, drift, pulls, field_high, field_low = call_at(
        step_body,
        (
            shape(144, NZ),
            shape(96, NZ),
            shape(96, NZ),
            shape(3, NQ),
            shape(6, NQ),
            shape(192, NZ, dtype=BF16),
            shape(192, NZ, dtype=BF16),
        ),
        [
            pltpu.VMEM((80, NZ), F32),
            pltpu.VMEM((96, NZ), F32),
            pltpu.VMEM((480, NZ), BF16),
            pltpu.VMEM((480, NZ), BF16),
            pltpu.VMEM((512, NZ), F32),
            pltpu.VMEM((4, 5, ROWS, NZ), F32),
        ],
        8,
    )(place, pos, mom, cell, dest, slot, gathered, left, right)
    left, right = swap_x(up, down)
    gathered = gather_y(call(functools.partial(fold_body, 3), shape(144, NZ))(own, left, right))
    mine, up, down = call_at(lines_body, (shape(144, NZ), shape(80, NZ), shape(80, NZ)), [], 1)(
        place, gathered
    )
    left, right = swap_x(up, down)
    own, up, down, grads = call(
        back_body,
        (shape(48, NZ), shape(32, NZ), shape(32, NZ), shape(6, NQ)),
        [
            pltpu.VMEM((3, 112, NZ), F32),
            pltpu.VMEM((256, NZ), F32),
            pltpu.VMEM((512, NZ), BF16),
            pltpu.VMEM((512, NZ), BF16),
            pltpu.VMEM((192, NZ), F32),
            pltpu.VMEM((3, 7, ROWS, NZ), F32),
        ],
    )(pos, mom, cell, dest, drift, pulls, mine, left, right)
    left, right = swap_x(up, down)
    gathered = gather_y(call(functools.partial(fold_body, 1), shape(48, NZ))(own, left, right))
    return call_at(
        last_body,
        (shape(3, NQ), shape(3, NQ)),
        [
            pltpu.VMEM((48, NZ), F32),
            pltpu.VMEM((32, NZ), F32),
            pltpu.VMEM((256, NZ), BF16),
            pltpu.VMEM((256, NZ), BF16),
        ],
        7,
    )(place, pos, mom, cell, grads, field_high, field_low, gathered)


def solution(mesh):
    both = ("gx", "gy")
    return jax.shard_map(
        local,
        mesh=mesh,
        in_specs=(P(None, both), P(None, both), P(None, both), P(None, both), P(both), P(both), P(None, both), P(None, both)),
        out_specs=(P(None, both), P(None, both)),
        check_vma=False,
    )
```

```python
import functools

import jax
import jax.numpy as jnp
from jax import lax
from jax.experimental import pallas as pl
from jax.experimental.pallas import tpu as pltpu
from jax.sharding import PartitionSpec as P

CX = 2
CY = 8
NZ = 256
NQ = 4096
BLK = 4096
ROWS = 16
TABLES = 5
STEP = 0.25
STRENGTH = 0.02
F32 = jnp.float32
BF16 = jnp.bfloat16
highest = lax.Precision.HIGHEST
VMEM_LIMIT = 24 * 1024 * 1024


def shape(*dims, dtype=F32):
    return jax.ShapeDtypeStruct(dims, dtype)


def call(body, outs, scratch=()):
    return pl.pallas_call(
        body,
        out_shape=outs,
        scratch_shapes=list(scratch),
        compiler_params=pltpu.CompilerParams(vmem_limit_bytes=VMEM_LIMIT),
    )


def split(x):
    high = x.astype(BF16)
    return high, (x - high.astype(F32)).astype(BF16)


def one_hot(index):
    rows = lax.broadcasted_iota(jnp.int32, (256, index.shape[1]), 0)
    return jnp.where(rows == index, 1.0, 0.0).astype(BF16)


def one_hot_columns(index):
    width = index.shape[1]
    down = jnp.transpose(jnp.broadcast_to(index, (8, width)))[:, 0:1]
    columns = lax.broadcasted_iota(jnp.int32, (width, 256), 1)
    return jnp.where(columns == down, 1.0, 0.0).astype(BF16)


MODE_S = "rows"
MODE_D = "nt"


def put_split(ref, first, values):
    rows = values.shape[0]
    high, low = split(values)
    half = ref.shape[0] // 2
    ref[first : first + rows, :] = high
    ref[half + first : half + first + rows, :] = low


def halves(x):
    half = x.shape[0] // 2
    return x[:half] + x[half:]


def pick_from(table, hot):
    return halves(jnp.dot(table[...], hot, preferred_element_type=F32))


def spread_onto(values, index):
    if MODE_D == "nt":
        return halves(
            lax.dot_general(
                values[...], one_hot(index), (((1,), (1,)), ((), ())), preferred_element_type=F32
            )
        )
    return halves(jnp.dot(values[...], one_hot_columns(index), preferred_element_type=F32))


def next_z(x):
    return pltpu.roll(x, NZ - 1, 1)


def prev_z(x):
    return pltpu.roll(x, 1, 1)


def diff_z(x):
    return 0.5 * (next_z(x) - prev_z(x))


def diff_row(x):
    return 0.5 * (pltpu.roll(x, ROWS - 1, 0) - pltpu.roll(x, 1, 0))


def axis_hits(rows, pitch, padded, cell_x, cell_y):
    index = lax.broadcasted_iota(jnp.int32, (padded, cell_x.shape[1]), 0)
    row_x = index // pitch
    row_y = index - row_x * pitch
    away_x = row_x - cell_x
    away_y = row_y - cell_y
    return away_x == 0, away_x == 1, away_y == 0, away_y == 1


def weights_of(hits, frac_x, frac_y):
    low_x, high_x, low_y, high_y = hits
    along_x = jnp.where(low_x, 1.0 - frac_x, jnp.where(high_x, frac_x, 0.0))
    along_y = jnp.where(low_y, 1.0 - frac_y, jnp.where(high_y, frac_y, 0.0))
    return along_x, along_y


def slopes_of(hits):
    low_x, high_x, low_y, high_y = hits
    along_x = jnp.where(low_x, -1.0, jnp.where(high_x, 1.0, 0.0))
    along_y = jnp.where(low_y, -1.0, jnp.where(high_y, 1.0, 0.0))
    return along_x, along_y


def row3(ref, at, first=0):
    return [ref[first + k : first + k + 1, at] for k in range(3)]


def line_matrix(me, window, offset, rows, first_y):
    target = lax.broadcasted_iota(jnp.int32, (ROWS, 8 * window), 0)
    column = lax.broadcasted_iota(jnp.int32, (ROWS, 8 * window), 1)
    device = column // window
    source = column - device * window - offset
    away = (CY * (me - device) + target - 2 - source - first_y + 128) & 63
    away = jnp.minimum(away, 64 - away)
    weight = STRENGTH * jnp.exp(away.astype(F32) * (-1.0 / 16.0))
    return jnp.where((source >= 0) & (source < rows), weight, 0.0)


def depth_body(out):
    target = lax.broadcasted_iota(jnp.int32, (NZ, NZ), 0)
    source = lax.broadcasted_iota(jnp.int32, (NZ, NZ), 1)
    away = jnp.abs(target - source)
    away = jnp.minimum(away, NZ - away)
    put_split(out, 0, jnp.exp(away.astype(F32) * (-1.0 / 16.0)))


def product(a, b_high, b_low):
    a_high, a_low = split(a)
    dot = functools.partial(jnp.dot, preferred_element_type=F32)
    return dot(a_high, b_high) + (dot(a_high, b_low) + dot(a_low, b_high))


def smooth(me, depth, gathered, planes, rows, first_y, window, kept):
    for p in range(planes):
        first = min(p * rows // 8 * 8, gathered.shape[1] - window)
        lines = line_matrix(me, window, p * rows - first, rows, first_y)
        source = gathered[:, first : first + window, :].reshape(8 * window, NZ)
        kept[p * ROWS : (p + 1) * ROWS, :] = product(lines, *split(source))
    kept[0 : planes * ROWS, :] = product(
        kept[0 : planes * ROWS, :], depth[0:NZ, :], depth[NZ : 2 * NZ, :]
    )


def select_pulls(table, where_to, moved):
    taken = pick_from(table, one_hot(where_to & 255))
    chosen = moved * 16 + lax.shift_right_logical(where_to, 8)
    here = lax.broadcasted_iota(jnp.int32, (80, where_to.shape[1]), 0) == chosen
    return [
        jnp.sum(jnp.where(here, taken[k * 80 : k * 80 + 80, :], 0.0), axis=0, keepdims=True) for k in range(3)
    ]


def deposit_first_body(
    pos, mom, cell, dest, slot, pull_pos, pull_mom, own, up, down, state, labels, held, ints, lone, sems, lhs, acc
):
    copies = [
        pltpu.make_async_copy(pos, held.at[0], sems.at[0]),
        pltpu.make_async_copy(mom, held.at[1], sems.at[1]),
        pltpu.make_async_copy(cell, ints, sems.at[2]),
        pltpu.make_async_copy(dest, lone.at[0], sems.at[3]),
        pltpu.make_async_copy(slot, lone.at[1], sems.at[4]),
        pltpu.make_async_copy(pull_pos, held.at[2], sems.at[5]),
        pltpu.make_async_copy(pull_mom, held.at[3], sems.at[6]),
    ]
    for copy in copies:
        copy.start()
    own[...] = jnp.zeros_like(own)
    acc[...] = jnp.zeros_like(acc)
    for copy in copies:
        copy.wait()
    state[0:3, :] = held[0] + STEP * held[1]
    state[3:6, :] = held[1]
    labels[0:3, :] = ints[...]
    labels[3:4, :] = lone[0]
    labels[4:5, :] = lone[1]

    def block(b, carry):
        at = pl.ds(pl.multiple_of(b * BLK, BLK), BLK)
        frac = row3(state, at)
        cells = row3(labels, at)
        along_x, along_y = weights_of(axis_hits(27, CY + 1, 32, cells[0], cells[1]), frac[0], frac[1])
        planar = along_x * along_y
        put_split(lhs, 0, planar * (1.0 - frac[2]))
        put_split(lhs, 32, planar * frac[2])
        acc[...] += spread_onto(lhs, cells[2])
        return carry

    lax.fori_loop(0, NQ // BLK, block, 0)
    density = acc[0:32, :] + prev_z(acc[32:64, :])
    for x in range(3):
        own[x * ROWS + 2 : x * ROWS + 11, :] = density[x * 9 : x * 9 + 9, :]
    up[0:32, :] = own[16:48, :]
    down[0:32, :] = own[0:32, :]
    for k in range(6):
        source = held.at[2 + k // 3]
        for c in range(16):
            line = source[k % 3 : k % 3 + 1, c * 256 : (c + 1) * 256]
            at_row = 32 + k * 16 + c
            up[at_row : at_row + 1, :] = line
            down[at_row : at_row + 1, :] = line


def fold_first_body(own, left, right, out):
    rows = slice(2, 11)
    out[0:9, :] = left[0:16, :][rows]
    out[9:18, :] = (own[0:16, :] + left[16:32, :])[rows]
    out[18:27, :] = own[16:32, :][rows]
    out[27:36, :] = (own[32:48, :] + right[0:16, :])[rows]
    out[36:45, :] = right[16:32, :][rows]
    out[45:48, :] = jnp.zeros((3, NZ), F32)


def step_body(
    place,
    state,
    labels,
    depth,
    gathered,
    mine,
    left,
    right,
    below,
    above,
    own,
    up,
    down,
    drift,
    pulls,
    fields,
    kept,
    pack,
    table,
    lhs,
    acc,
    planes,
):
    smooth(place[0], depth, gathered, 5, 9, 0, 16, kept)
    pack[...] = jnp.zeros_like(pack)
    for x in range(3):
        mid = (x + 1) * ROWS
        east = kept[mid + 18 : mid + 27, :]
        west = kept[mid - 14 : mid - 5, :]
        pack[x * 9 : x * 9 + 9, :] = -0.5 * (east - west)
        north = kept[mid + 3 : mid + 12, :]
        south = kept[mid + 1 : mid + 10, :]
        pack[32 + x * 9 : 32 + x * 9 + 9, :] = -0.5 * (north - south)
        pack[64 + x * 9 : 64 + x * 9 + 9, :] = -diff_z(kept[mid : mid + 16, :])[2:11, :]
    put_split(fields, 0, pack[...])
    put_split(fields, 96, next_z(pack[...]))
    fill_table(table, 80, (mine, right, left, above, below))
    acc[...] = jnp.zeros_like(acc)

    def block(b, carry):
        at = pl.ds(pl.multiple_of(b * BLK, BLK), BLK)
        frac = row3(state, at)
        momentum = row3(state, at, 3)
        cells = row3(labels, at)
        moved = labels[3:4, at]
        where_to = labels[4:5, at]
        along_x, along_y = weights_of(axis_hits(27, CY + 1, 32, cells[0], cells[1]), frac[0], frac[1])
        planar = along_x * along_y
        sampled = pick_from(fields, one_hot(cells[2]))
        lower = planar * (1.0 - frac[2])
        upper = planar * frac[2]
        force = [
            jnp.sum(
                lower * sampled[d * 32 : d * 32 + 32, :] + upper * sampled[96 + d * 32 : 128 + d * 32, :],
                axis=0,
                keepdims=True,
            )
            for d in range(3)
        ]
        to_x = jnp.where(moved == 1, 1, jnp.where(moved == 2, -1, 0))
        to_y = jnp.where(moved == 3, 1, jnp.where(moved == 4, -1, 0))
        shift = [to_x.astype(F32), to_y.astype(F32), 0.0]
        second = [frac[d] - shift[d] + STEP * (momentum[d] + STEP * force[d]) for d in range(3)]
        home = select_pulls(table, where_to, moved)
        for d in range(3):
            drift[d : d + 1, at] = second[d]
            pulls[d : d + 1, at] = home[d]
        along_x, along_y = weights_of(
            axis_hits(55, CY + 3, 64, cells[0] + to_x + 1, cells[1] + to_y + 1), second[0], second[1]
        )
        planar = along_x * along_y
        upper = planar * second[2]
        lower = planar - upper
        for c in range(4):
            scale = None if c == 0 else STEP * home[c - 1]
            put_split(lhs, c * 128, lower if c == 0 else lower * scale)
            put_split(lhs, c * 128 + 64, upper if c == 0 else upper * scale)
        acc[...] += spread_onto(lhs, cells[2])
        return carry

    lax.fori_loop(0, NQ // BLK, block, 0)
    planes[...] = jnp.zeros_like(planes)
    for c in range(4):
        total = acc[c * 128 : c * 128 + 64, :] + prev_z(acc[c * 128 + 64 : c * 128 + 128, :])
        for x in range(5):
            planes[c, x, 1:12, :] = total[x * 11 : x * 11 + 11, :]
    for x in range(5):
        planes[2, x] = diff_row(planes[2, x]) + diff_z(planes[3, x])
    for c in range(3):
        for x in range(3):
            own[(c * 3 + x) * 16 : (c * 3 + x) * 16 + 16, :] = planes[c, x + 1]
        for x in range(2):
            up[(c * 2 + x) * 16 : (c * 2 + x) * 16 + 16, :] = planes[c, x + 3]
            down[(c * 2 + x) * 16 : (c * 2 + x) * 16 + 16, :] = planes[c, x]


def fill_table(table, first, sources):
    for k in range(3):
        for t, source in enumerate(sources):
            put_split(table, k * 80 + t * 16, source[first + k * 16 : first + k * 16 + 16, :])


def pulls_body(labels, mine, left, right, below, above, pulls, table):
    fill_table(table, 32, (mine, right, left, above, below))

    def block(b, carry):
        at = pl.ds(pl.multiple_of(b * BLK, BLK), BLK)
        home = select_pulls(table, labels[4:5, at], labels[3:4, at])
        for d in range(3):
            pulls[d : d + 1, at] = home[d]
        return carry

    lax.fori_loop(0, NQ // BLK, block, 0)


def fold_body(channels, own, left, right, out):
    rows = out.shape[0] // (channels * 3)
    spare = out.shape[0] - channels * 3 * rows
    if spare:
        out[channels * 3 * rows :, :] = jnp.zeros((spare, NZ), F32)
    for c in range(channels):
        mine, theirs, to = c * 48, c * 32, c * 3 * rows
        first = own[mine : mine + 16, :] + left[theirs : theirs + 16, :]
        second = (
            own[mine + 16 : mine + 32, :]
            + left[theirs + 16 : theirs + 32, :]
            + right[theirs : theirs + 16, :]
        )
        third = own[mine + 32 : mine + 48, :] + right[theirs + 16 : theirs + 32, :]
        for n, values in enumerate((first, second, third)):
            out[to + n * rows : to + (n + 1) * rows, :] = values[0:rows]


def lines_body(place, depth, gathered, own, up, down):
    smooth(place[0], depth, gathered, 9, 13, -2, 24, own)
    for c in range(2):
        up[c * 32 : c * 32 + 32, :] = own[c * 48 : c * 48 + 32, :]
        down[c * 32 : c * 32 + 32, :] = own[c * 48 + 16 : c * 48 + 48, :]
    up[64:80, :] = own[112:128, :]
    down[64:80, :] = own[112:128, :]


def back_body(
    state, labels, drift, pulls, pulls_pos, mine, left, right, own, up, down, grads, wide, pack, fields, lhs, acc, planes
):
    for c in range(2):
        wide[c, 0:32, :] = left[c * 32 : c * 32 + 32, :]
        wide[c, 32:80, :] = mine[c * 48 : c * 48 + 48, :]
        wide[c, 80:112, :] = right[c * 32 : c * 32 + 32, :]
    wide[2, 16:32, :] = left[64:80, :]
    wide[2, 32:80, :] = mine[96:144, :]
    wide[2, 80:96, :] = right[64:80, :]
    pack[...] = jnp.zeros_like(pack)
    for x in range(5):
        mid = (x + 1) * 16
        first = x * 11
        pack[first : first + 11, :] = -0.5 * (wide[0, mid + 17 : mid + 28, :] - wide[0, mid - 15 : mid - 4, :])
        pack[64 + first : 75 + first, :] = -0.5 * (
            wide[0, mid + 2 : mid + 13, :] - wide[0, mid : mid + 11, :]
        )
        pack[128 + first : 139 + first, :] = -diff_z(wide[0, mid : mid + 16, :])[1:12, :]
        pack[192 + first : 203 + first, :] = (
            0.5 * (wide[1, mid + 17 : mid + 28, :] - wide[1, mid - 15 : mid - 4, :])
            + wide[2, mid + 1 : mid + 12, :]
        )
    put_split(fields, 0, pack[...])
    put_split(fields, 256, next_z(pack[...]))
    acc[...] = jnp.zeros_like(acc)

    def block(b, carry):
        at = pl.ds(pl.multiple_of(b * BLK, BLK), BLK)
        cells = row3(labels, at)
        moved = labels[3:4, at]
        second = row3(drift, at)
        pull_position = row3(pulls_pos, at)
        pull_momentum = row3(pulls, at)
        to_x = jnp.where(moved == 1, 1, jnp.where(moved == 2, -1, 0))
        to_y = jnp.where(moved == 3, 1, jnp.where(moved == 4, -1, 0))
        hits = axis_hits(55, CY + 3, 64, cells[0] + to_x + 1, cells[1] + to_y + 1)
        along_x, along_y = weights_of(hits, second[0], second[1])
        slope_x, slope_y = slopes_of(hits)
        sampled = pick_from(fields, one_hot(cells[2]))
        sides = []
        for s in range(2):
            mixed = sampled[s * 256 + 192 : s * 256 + 256, :]
            for d in range(3):
                mixed = mixed + (STEP * pull_momentum[d]) * sampled[s * 256 + d * 64 : s * 256 + d * 64 + 64, :]
            sides.append(mixed)
        level = sides[0] + second[2] * (sides[1] - sides[0])
        rise = sides[1] - sides[0]
        slopes = [
            jnp.sum(slope_x * (along_y * level), axis=0, keepdims=True),
            jnp.sum(slope_y * (along_x * level), axis=0, keepdims=True),
            jnp.sum(along_x * (along_y * rise), axis=0, keepdims=True),
        ]
        grad_drift = [pull_position[d] + slopes[d] for d in range(3)]
        grad_kick = [pull_momentum[d] + STEP * grad_drift[d] for d in range(3)]
        for d in range(3):
            grads[d : d + 1, at] = grad_drift[d]
            grads[d + 3 : d + 4, at] = grad_kick[d]
        frac = row3(state, at)
        along_x, along_y = weights_of(axis_hits(27, CY + 1, 32, cells[0], cells[1]), frac[0], frac[1])
        planar = along_x * along_y
        above = planar * frac[2]
        below = planar - above
        for c in range(3):
            scale = STEP * grad_kick[c]
            put_split(lhs, c * 64, below * scale)
            put_split(lhs, c * 64 + 32, above * scale)
        acc[...] += spread_onto(lhs, cells[2])
        return carry

    lax.fori_loop(0, NQ // BLK, block, 0)
    planes[...] = jnp.zeros_like(planes)
    for c in range(3):
        total = acc[c * 64 : c * 64 + 32, :] + prev_z(acc[c * 64 + 32 : c * 64 + 64, :])
        for x in range(3):
            planes[c, x + 2, 2:11, :] = total[x * 9 : x * 9 + 9, :]
    for x in range(5):
        spread = 0.5 * (planes[0, x + 2] - planes[0, x])
        if 1 <= x <= 3:
            spread = spread + diff_row(planes[1, x + 1]) + diff_z(planes[2, x + 1])
        if 1 <= x <= 3:
            own[(x - 1) * 16 : x * 16, :] = spread
        if x >= 3:
            up[(x - 3) * 16 : (x - 2) * 16, :] = spread
        if x <= 1:
            down[x * 16 : (x + 1) * 16, :] = spread


def last_body(place, state, labels, depth, grads, fields, gathered, grad_pos, grad_mom, kept, pack, own_field):
    smooth(place[0], depth, gathered, 3, 16, -2, 16, kept)
    pack[...] = jnp.zeros_like(pack)
    for x in range(3):
        pack[x * 9 : x * 9 + 9, :] = kept[x * 16 + 2 : x * 16 + 11, :]
    put_split(own_field, 0, pack[...])
    put_split(own_field, 32, next_z(pack[...]))

    def block(b, carry):
        at = pl.ds(pl.multiple_of(b * BLK, BLK), BLK)
        frac = row3(state, at)
        cells = row3(labels, at)
        hot = one_hot(cells[2])
        hits = axis_hits(27, CY + 1, 32, cells[0], cells[1])
        along_x, along_y = weights_of(hits, frac[0], frac[1])
        slope_x, slope_y = slopes_of(hits)
        grad_drift = row3(grads, at)
        grad_kick = row3(grads, at, 3)
        sampled = pick_from(fields, hot)
        pulled = pick_from(own_field, hot)
        sides = []
        for s in range(2):
            mixed = pulled[s * 32 : s * 32 + 32, :]
            for d in range(3):
                mixed = mixed + (STEP * grad_kick[d]) * sampled[s * 96 + d * 32 : s * 96 + d * 32 + 32, :]
            sides.append(mixed)
        level = sides[0] + frac[2] * (sides[1] - sides[0])
        rise = sides[1] - sides[0]
        slopes = [
            jnp.sum(slope_x * (along_y * level), axis=0, keepdims=True),
            jnp.sum(slope_y * (along_x * level), axis=0, keepdims=True),
            jnp.sum(along_x * (along_y * rise), axis=0, keepdims=True),
        ]
        for d in range(3):
            total = grad_drift[d] + slopes[d]
            grad_pos[d : d + 1, at] = total
            grad_mom[d : d + 1, at] = grad_kick[d] + STEP * total
        return carry

    lax.fori_loop(0, NQ // BLK, block, 0)


def swap(up, down, axis):
    peers = lax.axis_size(axis)
    forward = [(i, (i + 1) % peers) for i in range(peers)]
    backward = [((i + 1) % peers, i) for i in range(peers)]
    return lax.ppermute(up, axis, forward), lax.ppermute(down, axis, backward)


def gather_y(x):
    return lax.all_gather(x, "gy", axis=0, tiled=False)


def local(pos, mom, cell, cell_second, dest, slot, pull_pos, pull_mom):
    place = lax.axis_index("gy").astype(jnp.int32).reshape(1)
    dest = dest.reshape(1, NQ)
    slot = slot.reshape(1, NQ)
    scalar = pl.BlockSpec(memory_space=pltpu.SMEM)
    vmem = pl.BlockSpec(memory_space=pltpu.VMEM)

    def call_at(body, outs, scratch, operands):
        return pl.pallas_call(
            body,
            out_shape=outs,
            in_specs=[scalar] + [vmem] * operands,
            scratch_shapes=list(scratch),
            compiler_params=pltpu.CompilerParams(vmem_limit_bytes=VMEM_LIMIT),
        )

    depth = pl.pallas_call(
        depth_body,
        out_shape=shape(2 * NZ, NZ, dtype=BF16),
        compiler_params=pltpu.CompilerParams(vmem_limit_bytes=VMEM_LIMIT),
        cost_estimate=pl.CostEstimate(flops=10**9, bytes_accessed=10**7, transcendentals=10**6),
    )()
    in_hbm = [
        pltpu.with_memory_space_constraint(x, pltpu.HBM)
        for x in (pos, mom, cell, dest, slot, pull_pos, pull_mom)
    ]
    own, up, down, state, labels = pl.pallas_call(
        deposit_first_body,
        out_shape=(
            shape(48, NZ),
            shape(128, NZ),
            shape(128, NZ),
            shape(6, NQ),
            shape(5, NQ, dtype=jnp.int32),
        ),
        in_specs=[pl.BlockSpec(memory_space=pltpu.HBM)] * 7,
        scratch_shapes=[
            pltpu.VMEM((4, 3, NQ), F32),
            pltpu.VMEM((3, NQ), jnp.int32),
            pltpu.VMEM((2, 1, NQ), jnp.int32),
            pltpu.SemaphoreType.DMA((7,)),
            pltpu.VMEM((128, BLK), BF16),
            pltpu.VMEM((64, NZ), F32),
        ],
        compiler_params=pltpu.CompilerParams(vmem_limit_bytes=VMEM_LIMIT),
    )(*in_hbm)
    mine, (left, right) = up, swap(up, down, "gx")
    below, above = swap(up, up, "gy")
    first_left, first_right = left, right
    gathered = gather_y(call(fold_first_body, shape(48, NZ))(own, left, right))
    own, up, down, drift, pulls, fields = call_at(
        step_body,
        (
            shape(144, NZ),
            shape(96, NZ),
            shape(96, NZ),
            shape(3, NQ),
            shape(3, NQ),
            shape(384, NZ, dtype=BF16),
        ),
        [
            pltpu.VMEM((80, NZ), F32),
            pltpu.VMEM((96, NZ), F32),
            pltpu.VMEM((480, NZ), BF16),
            pltpu.VMEM((1024, BLK), BF16),
            pltpu.VMEM((512, NZ), F32),
            pltpu.VMEM((4, 5, ROWS, NZ), F32),
        ],
        9,
    )(place, state, labels, depth, gathered, mine, left, right, below, above)
    left, right = swap(up, down, "gx")
    gathered = gather_y(call(functools.partial(fold_body, 3), shape(120, NZ))(own, left, right))
    own, up, down = call_at(lines_body, (shape(144, NZ), shape(80, NZ), shape(80, NZ)), [], 2)(
        place, depth, gathered
    )
    left, right = swap(up, down, "gx")
    pulls_pos = call(pulls_body, shape(3, NQ), [pltpu.VMEM((480, NZ), BF16)])(
        labels, mine, first_left, first_right, below, above
    )
    own, up, down, grads = call(
        back_body,
        (shape(48, NZ), shape(32, NZ), shape(32, NZ), shape(6, NQ)),
        [
            pltpu.VMEM((3, 112, NZ), F32),
            pltpu.VMEM((256, NZ), F32),
            pltpu.VMEM((1024, NZ), BF16),
            pltpu.VMEM((384, BLK), BF16),
            pltpu.VMEM((192, NZ), F32),
            pltpu.VMEM((3, 7, ROWS, NZ), F32),
        ],
    )(state, labels, drift, pulls, pulls_pos, own, left, right)
    left, right = swap(up, down, "gx")
    gathered = gather_y(call(functools.partial(fold_body, 1), shape(48, NZ))(own, left, right))
    return call_at(
        last_body,
        (shape(3, NQ), shape(3, NQ)),
        [pltpu.VMEM((48, NZ), F32), pltpu.VMEM((32, NZ), F32), pltpu.VMEM((128, NZ), BF16)],
        6,
    )(place, state, labels, depth, grads, fields, gathered)


def solution(mesh):
    both = ("gx", "gy")
    return jax.shard_map(
        local,
        mesh=mesh,
        in_specs=(P(None, both), P(None, both), P(None, both), P(None, both), P(both), P(both), P(None, both), P(None, both)),
        out_specs=(P(None, both), P(None, both)),
        check_vma=False,
    )
```

```python
import functools

import jax
import jax.numpy as jnp
from jax import lax
from jax.experimental import pallas as pl
from jax.experimental.pallas import tpu as pltpu
from jax.sharding import PartitionSpec as P

CX = 2
CY = 8
NZ = 256
NQ = 4096
BLK = 4096
ROWS = 16
TABLES = 5
STEP = 0.25
STRENGTH = 0.02
F32 = jnp.float32
BF16 = jnp.bfloat16
highest = lax.Precision.HIGHEST
SECOND_SPANS = [(11 * p, 11, -1) for p in range(6)] + [(66 + 13 * p, 13, -2) for p in range(3)]
REPLIES = 105
VMEM_LIMIT = 24 * 1024 * 1024


def shape(*dims, dtype=F32):
    return jax.ShapeDtypeStruct(dims, dtype)


def call(body, outs, scratch=()):
    return pl.pallas_call(
        body,
        out_shape=outs,
        scratch_shapes=list(scratch),
        compiler_params=pltpu.CompilerParams(vmem_limit_bytes=VMEM_LIMIT),
    )


def split(x):
    high = x.astype(BF16)
    return high, (x - high.astype(F32)).astype(BF16)


def one_hot(index):
    rows = lax.broadcasted_iota(jnp.int32, (256, index.shape[1]), 0)
    return jnp.where(rows == index, 1.0, 0.0).astype(BF16)


def one_hot_columns(index):
    width = index.shape[1]
    down = jnp.transpose(jnp.broadcast_to(index, (8, width)))[:, 0:1]
    columns = lax.broadcasted_iota(jnp.int32, (width, 256), 1)
    return jnp.where(columns == down, 1.0, 0.0).astype(BF16)


MODE_S = "rows"
MODE_D = "nt"


def put_split(ref, first, values):
    rows = values.shape[0]
    high, low = split(values)
    half = ref.shape[0] // 2
    ref[first : first + rows, :] = high
    ref[half + first : half + first + rows, :] = low


def halves(x):
    half = x.shape[0] // 2
    return x[:half] + x[half:]


def pick_from(table, hot):
    return halves(jnp.dot(table[...], hot, preferred_element_type=F32))


def spread_onto(values, hot):
    return halves(
        lax.dot_general(values[...], hot, (((1,), (1,)), ((), ())), preferred_element_type=F32)
    )


def next_z(x):
    return pltpu.roll(x, NZ - 1, 1)


def prev_z(x):
    return pltpu.roll(x, 1, 1)


def diff_z(x):
    return 0.5 * (next_z(x) - prev_z(x))


def diff_row(x):
    return 0.5 * (pltpu.roll(x, ROWS - 1, 0) - pltpu.roll(x, 1, 0))


def axis_hits(rows, pitch, padded, cell_x, cell_y):
    index = lax.broadcasted_iota(jnp.int32, (padded, 1), 0)
    row_x = index // pitch
    row_y = index - row_x * pitch
    return row_x == cell_x, row_x - 1 == cell_x, row_y == cell_y, row_y - 1 == cell_y


def weights_of(hits, frac_x, frac_y):
    low_x, high_x, low_y, high_y = hits
    along_x = jnp.where(low_x, 1.0 - frac_x, jnp.where(high_x, frac_x, 0.0))
    along_y = jnp.where(low_y, 1.0 - frac_y, jnp.where(high_y, frac_y, 0.0))
    return along_x, along_y


def slopes_of(hits):
    low_x, high_x, low_y, high_y = hits
    along_x = jnp.where(low_x, -1.0, jnp.where(high_x, 1.0, 0.0))
    along_y = jnp.where(low_y, -1.0, jnp.where(high_y, 1.0, 0.0))
    return along_x, along_y


def row3(ref, at, first=0):
    return [ref[first + k : first + k + 1, at] for k in range(3)]


def line_matrix(me, window, offset, rows, first_y):
    target = lax.broadcasted_iota(jnp.int32, (ROWS, 8 * window), 0)
    column = lax.broadcasted_iota(jnp.int32, (ROWS, 8 * window), 1)
    device = column // window
    source = column - device * window - offset
    away = (CY * (me - device) + target - 2 - source - first_y + 128) & 63
    away = jnp.minimum(away, 64 - away)
    weight = STRENGTH * jnp.exp(away.astype(F32) * (-1.0 / 16.0))
    return jnp.where((source >= 0) & (source < rows), weight, 0.0)


def depth_body(out):
    target = lax.broadcasted_iota(jnp.int32, (NZ, NZ), 0)
    source = lax.broadcasted_iota(jnp.int32, (NZ, NZ), 1)
    away = jnp.abs(target - source)
    away = jnp.minimum(away, NZ - away)
    put_split(out, 0, jnp.exp(away.astype(F32) * (-1.0 / 16.0)))


def product(a, b_high, b_low):
    a_high, a_low = split(a)
    dot = functools.partial(jnp.dot, preferred_element_type=F32)
    return dot(a_high, b_high) + (dot(a_high, b_low) + dot(a_low, b_high))


def smooth(me, depth, gathered, spans, window, kept):
    for p, (start, rows, first_y) in enumerate(spans):
        first = min(start // 8 * 8, gathered.shape[1] - window)
        lines = line_matrix(me, window, start - first, rows, first_y)
        source = gathered[:, first : first + window, :].reshape(8 * window, NZ)
        kept[p * ROWS : (p + 1) * ROWS, :] = product(lines, *split(source))
    kept[0 : len(spans) * ROWS, :] = product(
        kept[0 : len(spans) * ROWS, :], depth[0:NZ, :], depth[NZ : 2 * NZ, :]
    )


def select_pulls(table, where_to, moved):
    taken = pick_from(table, one_hot(where_to & 255))
    rows = taken.shape[0] // 3
    chosen = moved * 16 + lax.shift_right_logical(where_to, 8)
    here = lax.broadcasted_iota(jnp.int32, (rows, where_to.shape[1]), 0) == chosen
    return [
        jnp.sum(jnp.where(here, taken[k * rows : k * rows + rows, :], 0.0), axis=0, keepdims=True)
        for k in range(3)
    ]


def requests_body(labels, wanted, ranks, marks, lists):
    for c in range(16):
        part = labels[3:4, c * 256 : (c + 1) * 256]
        marks[c : c + 1, :] = jnp.where(part == 3, 1.0, 0.0)
        marks[16 + c : 17 + c, :] = jnp.where(part == 4, 1.0, 0.0)
    row = lax.broadcasted_iota(jnp.int32, (256, 256), 0)
    column = lax.broadcasted_iota(jnp.int32, (256, 256), 1)
    earlier = jnp.where(row < column, 1.0, 0.0).astype(BF16)
    within = jnp.dot(marks[...].astype(BF16), earlier, preferred_element_type=F32)
    totals = jnp.broadcast_to(jnp.sum(marks[...], axis=1, keepdims=True), (32, 256))
    row = lax.broadcasted_iota(jnp.int32, (32, 32), 0)
    column = lax.broadcasted_iota(jnp.int32, (32, 32), 1)
    earlier = jnp.where((column < row) & (row // 16 == column // 16), 1.0, 0.0).astype(BF16)
    marks[...] = within + jnp.dot(earlier, totals.astype(BF16), preferred_element_type=F32)
    for c in range(16):
        part = labels[3:4, c * 256 : (c + 1) * 256]
        place = jnp.where(part == 3, marks[c : c + 1, :], jnp.where(part == 4, marks[16 + c : 17 + c, :], -1.0))
        ranks[0:1, c * 256 : (c + 1) * 256] = place.astype(jnp.int32)
    moved = labels[3:4, :]
    where_to = labels[4:5, :]
    upper = lax.shift_right_logical(where_to, 8).astype(F32)
    lower = (where_to & 255).astype(F32)
    lists[...] = jnp.zeros_like(lists)
    lists[0:1, :] = jnp.where(moved == 3, upper, 0.0)
    lists[1:2, :] = jnp.where(moved == 3, lower, 0.0)
    lists[2:3, :] = jnp.where(moved == 4, upper, 0.0)
    lists[3:4, :] = jnp.where(moved == 4, lower, 0.0)
    placed = lax.dot_general(
        lists[...].astype(BF16), one_hot(ranks[...]), (((1,), (1,)), ((), ())), preferred_element_type=F32
    )
    wanted[...] = jnp.zeros_like(wanted)
    wanted[0:1, :] = placed[0:1, :] * 256.0 + placed[1:2, :]
    wanted[1:2, :] = placed[2:3, :] * 256.0 + placed[3:4, :]


def replies_body(place, gathered, lent, out, table):
    put_split(table, 0, lent[...])
    out[...] = jnp.zeros_like(out)
    for n, side in enumerate((lax.rem(place[0] + 7, 8), lax.rem(place[0] + 1, 8))):
        wanted = gathered[side, 45 + n : 46 + n, :].astype(jnp.int32)
        taken = pick_from(table, one_hot(wanted & 255))
        here = lax.broadcasted_iota(jnp.int32, (16, 256), 0) == lax.shift_right_logical(wanted, 8)
        for k in range(3):
            row = n * 3 + k
            out[row : row + 1, :] = jnp.sum(
                jnp.where(here, taken[k * 16 : k * 16 + 16, :], 0.0), axis=0, keepdims=True
            )


def deposit_first_body(
    pos, mom, cell, dest, slot, pull_pos, pull_mom, own, up, down, lent, state, labels, hot, held, ints, lone, sems, lhs, acc
):
    copies = [
        pltpu.make_async_copy(pos, held.at[0], sems.at[0]),
        pltpu.make_async_copy(mom, held.at[1], sems.at[1]),
        pltpu.make_async_copy(cell, ints, sems.at[2]),
        pltpu.make_async_copy(dest, lone.at[0], sems.at[3]),
        pltpu.make_async_copy(slot, lone.at[1], sems.at[4]),
        pltpu.make_async_copy(pull_pos, held.at[2], sems.at[5]),
        pltpu.make_async_copy(pull_mom, held.at[3], sems.at[6]),
    ]
    for copy in copies:
        copy.start()
    own[...] = jnp.zeros_like(own)
    acc[...] = jnp.zeros_like(acc)
    for copy in copies:
        copy.wait()
    state[0:3, :] = held[0] + STEP * held[1]
    state[3:6, :] = held[1]
    labels[0:3, :] = ints[...]
    labels[3:4, :] = lone[0]
    labels[4:5, :] = lone[1]
    hot[...] = one_hot(ints[2:3, :])

    def block(b, carry):
        at = pl.ds(pl.multiple_of(b * BLK, BLK), BLK)
        frac = row3(state, at)
        cells = row3(labels, at)
        along_x, along_y = weights_of(axis_hits(27, CY + 1, 32, cells[0], cells[1]), frac[0], frac[1])
        planar = along_x * along_y
        put_split(lhs, 0, planar * (1.0 - frac[2]))
        put_split(lhs, 32, planar * frac[2])
        acc[...] += spread_onto(lhs, hot[...])
        return carry

    lax.fori_loop(0, NQ // BLK, block, 0)
    density = acc[0:32, :] + prev_z(acc[32:64, :])
    for x in range(3):
        own[x * ROWS + 2 : x * ROWS + 11, :] = density[x * 9 : x * 9 + 9, :]
    up[0:32, :] = own[16:48, :]
    down[0:32, :] = own[0:32, :]
    for k in range(6):
        source = held.at[2 + k // 3]
        for c in range(16):
            line = source[k % 3 : k % 3 + 1, c * 256 : (c + 1) * 256]
            at_row = 32 + k * 16 + c
            up[at_row : at_row + 1, :] = line
            down[at_row : at_row + 1, :] = line
            if k < 3:
                lent[at_row - 32 : at_row - 31, :] = line


def fold_first_body(own, left, right, pulls, wanted, out):
    rows = slice(2, 11)
    out[0:9, :] = left[0:16, :][rows]
    out[9:18, :] = (own[0:16, :] + left[16:32, :])[rows]
    out[18:27, :] = own[16:32, :][rows]
    out[27:36, :] = (own[32:48, :] + right[0:16, :])[rows]
    out[36:45, :] = right[16:32, :][rows]
    out[45:48, :] = wanted[0:3, :]
    out[48:96, :] = pulls[80:128, :]


def step_body(
    place,
    state,
    labels,
    hot,
    depth,
    gathered,
    mine,
    left,
    right,
    own,
    up,
    down,
    drift,
    pulls,
    fields,
    kept,
    pack,
    table,
    lhs,
    acc,
    planes,
):
    smooth(place[0], depth, gathered, [(9 * p, 9, 0) for p in range(5)], 16, kept)
    pack[...] = jnp.zeros_like(pack)
    for x in range(3):
        mid = (x + 1) * ROWS
        east = kept[mid + 18 : mid + 27, :]
        west = kept[mid - 14 : mid - 5, :]
        pack[x * 9 : x * 9 + 9, :] = -0.5 * (east - west)
        north = kept[mid + 3 : mid + 12, :]
        south = kept[mid + 1 : mid + 10, :]
        pack[32 + x * 9 : 32 + x * 9 + 9, :] = -0.5 * (north - south)
        pack[64 + x * 9 : 64 + x * 9 + 9, :] = -diff_z(kept[mid : mid + 16, :])[2:11, :]
    put_split(fields, 0, pack[...])
    put_split(fields, 96, next_z(pack[...]))
    ahead = lax.rem(place[0] + 1, 8)
    behind = lax.rem(place[0] + 7, 8)

    def rows_of(device):
        return lambda row: gathered[device, 48 + row : 64 + row, :]

    fill_table(
        table, [rows_at(mine, 80), rows_at(right, 80), rows_at(left, 80), rows_of(ahead), rows_of(behind)]
    )
    acc[...] = jnp.zeros_like(acc)

    def block(b, carry):
        at = pl.ds(pl.multiple_of(b * BLK, BLK), BLK)
        frac = row3(state, at)
        momentum = row3(state, at, 3)
        cells = row3(labels, at)
        moved = labels[3:4, at]
        where_to = labels[4:5, at]
        along_x, along_y = weights_of(axis_hits(27, CY + 1, 32, cells[0], cells[1]), frac[0], frac[1])
        planar = along_x * along_y
        sampled = pick_from(fields, hot[...])
        lower = planar * (1.0 - frac[2])
        upper = planar * frac[2]
        force = [
            jnp.sum(
                lower * sampled[d * 32 : d * 32 + 32, :] + upper * sampled[96 + d * 32 : 128 + d * 32, :],
                axis=0,
                keepdims=True,
            )
            for d in range(3)
        ]
        to_x = jnp.where(moved == 1, 1, jnp.where(moved == 2, -1, 0))
        to_y = jnp.where(moved == 3, 1, jnp.where(moved == 4, -1, 0))
        shift = [to_x.astype(F32), to_y.astype(F32), 0.0]
        second = [frac[d] - shift[d] + STEP * (momentum[d] + STEP * force[d]) for d in range(3)]
        home = select_pulls(table, where_to, moved)
        for d in range(3):
            drift[d : d + 1, at] = second[d]
            pulls[d : d + 1, at] = home[d]
        along_x, along_y = weights_of(
            axis_hits(55, CY + 3, 64, cells[0] + to_x + 1, cells[1] + to_y + 1), second[0], second[1]
        )
        planar = along_x * along_y
        upper = planar * second[2]
        lower = planar - upper
        for c in range(4):
            scale = None if c == 0 else STEP * home[c - 1]
            put_split(lhs, c * 128, lower if c == 0 else lower * scale)
            put_split(lhs, c * 128 + 64, upper if c == 0 else upper * scale)
        acc[...] += spread_onto(lhs, hot[...])
        return carry

    lax.fori_loop(0, NQ // BLK, block, 0)
    planes[...] = jnp.zeros_like(planes)
    for c in range(4):
        total = acc[c * 128 : c * 128 + 64, :] + prev_z(acc[c * 128 + 64 : c * 128 + 128, :])
        for x in range(5):
            planes[c, x, 1:12, :] = total[x * 11 : x * 11 + 11, :]
    for x in range(5):
        planes[2, x] = diff_row(planes[2, x]) + diff_z(planes[3, x])
    for c in range(3):
        for x in range(3):
            own[(c * 3 + x) * 16 : (c * 3 + x) * 16 + 16, :] = planes[c, x + 1]
        for x in range(2):
            up[(c * 2 + x) * 16 : (c * 2 + x) * 16 + 16, :] = planes[c, x + 3]
            down[(c * 2 + x) * 16 : (c * 2 + x) * 16 + 16, :] = planes[c, x]


def fill_table(table, sources):
    for k in range(3):
        for t, source in enumerate(sources):
            put_split(table, (k * len(sources) + t) * 16, source(k * 16))


def rows_at(ref, first):
    return lambda row: ref[first + row : first + row + 16, :]


def pulls_body(place, labels, ranks, mine, left, right, gathered, pulls, table, lists, replied):
    fill_table(table, [rows_at(mine, 0), rows_at(right, 32), rows_at(left, 32)])
    moved = labels[3:4, :]
    home = select_pulls(table, labels[4:5, :], moved)
    lists[...] = jnp.zeros_like(lists)
    lists[0:3, :] = gathered[lax.rem(place[0] + 1, 8), REPLIES : REPLIES + 3, :]
    lists[3:6, :] = gathered[lax.rem(place[0] + 7, 8), REPLIES + 3 : REPLIES + 6, :]
    put_split(replied, 0, lists[...])
    taken = pick_from(replied, one_hot(ranks[...]))
    for d in range(3):
        from_y = jnp.where(moved == 3, taken[d : d + 1, :], jnp.where(moved == 4, taken[d + 3 : d + 4, :], 0.0))
        pulls[d : d + 1, :] = home[d] + from_y


def fold_planes(own, left, right, channel):
    mine, theirs = channel * 48, channel * 32
    first = own[mine : mine + 16, :] + left[theirs : theirs + 16, :]
    second = (
        own[mine + 16 : mine + 32, :] + left[theirs + 16 : theirs + 32, :] + right[theirs : theirs + 16, :]
    )
    third = own[mine + 32 : mine + 48, :] + right[theirs + 16 : theirs + 32, :]
    return first, second, third


def fold_second_body(own, left, right, replies, out):
    for c in range(3):
        for n, values in enumerate(fold_planes(own, left, right, c)):
            start, rows, first_y = SECOND_SPANS[c * 3 + n]
            out[start : start + rows, :] = values[first_y + 2 : first_y + 2 + rows]
    out[REPLIES : REPLIES + 7, :] = replies[0:7, :]


def fold_third_body(own, left, right, out):
    for n, values in enumerate(fold_planes(own, left, right, 0)):
        out[n * 16 : n * 16 + 16, :] = values


def lines_body(place, depth, gathered, own, up, down):
    smooth(place[0], depth, gathered, SECOND_SPANS, 24, own)
    for c in range(2):
        up[c * 32 : c * 32 + 32, :] = own[c * 48 : c * 48 + 32, :]
        down[c * 32 : c * 32 + 32, :] = own[c * 48 + 16 : c * 48 + 48, :]
    up[64:80, :] = own[112:128, :]
    down[64:80, :] = own[112:128, :]


def back_body(
    state, labels, hot, drift, pulls, pulls_pos, mine, left, right, own, up, down, grads, wide, pack, fields, lhs, acc, planes
):
    for c in range(2):
        wide[c, 0:32, :] = left[c * 32 : c * 32 + 32, :]
        wide[c, 32:80, :] = mine[c * 48 : c * 48 + 48, :]
        wide[c, 80:112, :] = right[c * 32 : c * 32 + 32, :]
    wide[2, 16:32, :] = left[64:80, :]
    wide[2, 32:80, :] = mine[96:144, :]
    wide[2, 80:96, :] = right[64:80, :]
    pack[...] = jnp.zeros_like(pack)
    for x in range(5):
        mid = (x + 1) * 16
        first = x * 11
        pack[first : first + 11, :] = -0.5 * (wide[0, mid + 17 : mid + 28, :] - wide[0, mid - 15 : mid - 4, :])
        pack[64 + first : 75 + first, :] = -0.5 * (
            wide[0, mid + 2 : mid + 13, :] - wide[0, mid : mid + 11, :]
        )
        pack[128 + first : 139 + first, :] = -diff_z(wide[0, mid : mid + 16, :])[1:12, :]
        pack[192 + first : 203 + first, :] = (
            0.5 * (wide[1, mid + 17 : mid + 28, :] - wide[1, mid - 15 : mid - 4, :])
            + wide[2, mid + 1 : mid + 12, :]
        )
    put_split(fields, 0, pack[...])
    put_split(fields, 256, next_z(pack[...]))
    acc[...] = jnp.zeros_like(acc)

    def block(b, carry):
        at = pl.ds(pl.multiple_of(b * BLK, BLK), BLK)
        cells = row3(labels, at)
        moved = labels[3:4, at]
        second = row3(drift, at)
        pull_position = row3(pulls_pos, at)
        pull_momentum = row3(pulls, at)
        to_x = jnp.where(moved == 1, 1, jnp.where(moved == 2, -1, 0))
        to_y = jnp.where(moved == 3, 1, jnp.where(moved == 4, -1, 0))
        hits = axis_hits(55, CY + 3, 64, cells[0] + to_x + 1, cells[1] + to_y + 1)
        along_x, along_y = weights_of(hits, second[0], second[1])
        slope_x, slope_y = slopes_of(hits)
        sampled = pick_from(fields, hot[...])
        sides = []
        for s in range(2):
            mixed = sampled[s * 256 + 192 : s * 256 + 256, :]
            for d in range(3):
                mixed = mixed + (STEP * pull_momentum[d]) * sampled[s * 256 + d * 64 : s * 256 + d * 64 + 64, :]
            sides.append(mixed)
        level = sides[0] + second[2] * (sides[1] - sides[0])
        rise = sides[1] - sides[0]
        slopes = [
            jnp.sum(slope_x * (along_y * level), axis=0, keepdims=True),
            jnp.sum(slope_y * (along_x * level), axis=0, keepdims=True),
            jnp.sum(along_x * (along_y * rise), axis=0, keepdims=True),
        ]
        grad_drift = [pull_position[d] + slopes[d] for d in range(3)]
        grad_kick = [pull_momentum[d] + STEP * grad_drift[d] for d in range(3)]
        for d in range(3):
            grads[d : d + 1, at] = grad_drift[d]
            grads[d + 3 : d + 4, at] = grad_kick[d]
        frac = row3(state, at)
        along_x, along_y = weights_of(axis_hits(27, CY + 1, 32, cells[0], cells[1]), frac[0], frac[1])
        planar = along_x * along_y
        above = planar * frac[2]
        below = planar - above
        for c in range(3):
            scale = STEP * grad_kick[c]
            put_split(lhs, c * 64, below * scale)
            put_split(lhs, c * 64 + 32, above * scale)
        acc[...] += spread_onto(lhs, hot[...])
        return carry

    lax.fori_loop(0, NQ // BLK, block, 0)
    planes[...] = jnp.zeros_like(planes)
    for c in range(3):
        total = acc[c * 64 : c * 64 + 32, :] + prev_z(acc[c * 64 + 32 : c * 64 + 64, :])
        for x in range(3):
            planes[c, x + 2, 2:11, :] = total[x * 9 : x * 9 + 9, :]
    for x in range(5):
        spread = 0.5 * (planes[0, x + 2] - planes[0, x])
        if 1 <= x <= 3:
            spread = spread + diff_row(planes[1, x + 1]) + diff_z(planes[2, x + 1])
        if 1 <= x <= 3:
            own[(x - 1) * 16 : x * 16, :] = spread
        if x >= 3:
            up[(x - 3) * 16 : (x - 2) * 16, :] = spread
        if x <= 1:
            down[x * 16 : (x + 1) * 16, :] = spread


def mix_slopes(hits, frac, sides):
    along_x, along_y = weights_of(hits, frac[0], frac[1])
    slope_x, slope_y = slopes_of(hits)
    rise = sides[1] - sides[0]
    level = sides[0] + frac[2] * rise
    return [
        jnp.sum(slope_x * (along_y * level), axis=0, keepdims=True),
        jnp.sum(slope_y * (along_x * level), axis=0, keepdims=True),
        jnp.sum(along_x * (along_y * rise), axis=0, keepdims=True),
    ]


def push_body(state, labels, hot, grads, fields, out):
    frac = row3(state, slice(None))
    cells = row3(labels, slice(None))
    grad_kick = row3(grads, slice(None), 3)
    sampled = pick_from(fields, hot[...])
    sides = []
    for s in range(2):
        mixed = (STEP * grad_kick[0]) * sampled[s * 96 : s * 96 + 32, :]
        for d in range(1, 3):
            mixed = mixed + (STEP * grad_kick[d]) * sampled[s * 96 + d * 32 : s * 96 + d * 32 + 32, :]
        sides.append(mixed)
    slopes = mix_slopes(axis_hits(27, CY + 1, 32, cells[0], cells[1]), frac, sides)
    for d in range(3):
        out[d : d + 1, :] = grads[d : d + 1, :] + slopes[d]


def last_body(place, state, labels, hot, depth, grads, partial, gathered, grad_pos, grad_mom, kept, pack, own_field):
    smooth(place[0], depth, gathered, [(16 * p, 16, -2) for p in range(3)], 16, kept)
    pack[...] = jnp.zeros_like(pack)
    for x in range(3):
        pack[x * 9 : x * 9 + 9, :] = kept[x * 16 + 2 : x * 16 + 11, :]
    put_split(own_field, 0, pack[...])
    put_split(own_field, 32, next_z(pack[...]))
    frac = row3(state, slice(None))
    cells = row3(labels, slice(None))
    sampled = pick_from(own_field, hot[...])
    slopes = mix_slopes(
        axis_hits(27, CY + 1, 32, cells[0], cells[1]), frac, [sampled[0:32, :], sampled[32:64, :]]
    )
    for d in range(3):
        total = partial[d : d + 1, :] + slopes[d]
        grad_pos[d : d + 1, :] = total
        grad_mom[d : d + 1, :] = grads[d + 3 : d + 4, :] + STEP * total


def swap(up, down, axis):
    peers = lax.axis_size(axis)
    forward = [(i, (i + 1) % peers) for i in range(peers)]
    backward = [((i + 1) % peers, i) for i in range(peers)]
    return lax.ppermute(up, axis, forward), lax.ppermute(down, axis, backward)


def gather_y(x):
    return lax.all_gather(x, "gy", axis=0, tiled=False)


def local(pos, mom, cell, cell_second, dest, slot, pull_pos, pull_mom):
    place = lax.axis_index("gy").astype(jnp.int32).reshape(1)
    dest = dest.reshape(1, NQ)
    slot = slot.reshape(1, NQ)
    scalar = pl.BlockSpec(memory_space=pltpu.SMEM)
    vmem = pl.BlockSpec(memory_space=pltpu.VMEM)

    def call_at(body, outs, scratch, operands):
        return pl.pallas_call(
            body,
            out_shape=outs,
            in_specs=[scalar] + [vmem] * operands,
            scratch_shapes=list(scratch),
            compiler_params=pltpu.CompilerParams(vmem_limit_bytes=VMEM_LIMIT),
        )

    depth = pl.pallas_call(
        depth_body,
        out_shape=shape(2 * NZ, NZ, dtype=BF16),
        compiler_params=pltpu.CompilerParams(vmem_limit_bytes=VMEM_LIMIT),
        cost_estimate=pl.CostEstimate(flops=10**9, bytes_accessed=10**7, transcendentals=10**6),
    )()
    in_hbm = [
        pltpu.with_memory_space_constraint(x, pltpu.HBM)
        for x in (pos, mom, cell, dest, slot, pull_pos, pull_mom)
    ]
    own, up, down, lent, state, labels, hot = pl.pallas_call(
        deposit_first_body,
        out_shape=(
            shape(48, NZ),
            shape(128, NZ),
            shape(128, NZ),
            shape(48, NZ),
            shape(6, NQ),
            shape(5, NQ, dtype=jnp.int32),
            shape(NZ, NQ, dtype=BF16),
        ),
        in_specs=[pl.BlockSpec(memory_space=pltpu.HBM)] * 7,
        scratch_shapes=[
            pltpu.VMEM((4, 3, NQ), F32),
            pltpu.VMEM((3, NQ), jnp.int32),
            pltpu.VMEM((2, 1, NQ), jnp.int32),
            pltpu.SemaphoreType.DMA((7,)),
            pltpu.VMEM((128, BLK), BF16),
            pltpu.VMEM((64, NZ), F32),
        ],
        compiler_params=pltpu.CompilerParams(vmem_limit_bytes=VMEM_LIMIT),
    )(*in_hbm)
    mine, (left, right) = up, swap(up, down, "gx")
    first_left, first_right = left, right
    wanted, ranks = call(
        requests_body,
        (shape(8, NZ), shape(1, NQ, dtype=jnp.int32)),
        [pltpu.VMEM((32, NZ), F32), pltpu.VMEM((16, NQ), F32)],
    )(labels)
    gathered = gather_y(call(fold_first_body, shape(96, NZ))(own, left, right, up, wanted))
    replies = call_at(replies_body, shape(8, NZ), [pltpu.VMEM((96, NZ), BF16)], 2)(place, gathered, lent)
    own, up, down, drift, pulls, fields = call_at(
        step_body,
        (
            shape(144, NZ),
            shape(96, NZ),
            shape(96, NZ),
            shape(3, NQ),
            shape(3, NQ),
            shape(384, NZ, dtype=BF16),
        ),
        [
            pltpu.VMEM((80, NZ), F32),
            pltpu.VMEM((96, NZ), F32),
            pltpu.VMEM((480, NZ), BF16),
            pltpu.VMEM((1024, BLK), BF16),
            pltpu.VMEM((512, NZ), F32),
            pltpu.VMEM((4, 5, ROWS, NZ), F32),
        ],
        8,
    )(place, state, labels, hot, depth, gathered, mine, left, right)
    left, right = swap(up, down, "gx")
    gathered = gather_y(call(fold_second_body, shape(112, NZ))(own, left, right, replies))
    own, up, down = call_at(lines_body, (shape(144, NZ), shape(80, NZ), shape(80, NZ)), [], 2)(
        place, depth, gathered
    )
    left, right = swap(up, down, "gx")
    pulls_pos = call_at(
        pulls_body,
        shape(3, NQ),
        [pltpu.VMEM((288, NZ), BF16), pltpu.VMEM((16, NZ), F32), pltpu.VMEM((32, NZ), BF16)],
        6,
    )(place, labels, ranks, lent, first_left, first_right, gathered)
    own, up, down, grads = call(
        back_body,
        (shape(48, NZ), shape(32, NZ), shape(32, NZ), shape(6, NQ)),
        [
            pltpu.VMEM((3, 112, NZ), F32),
            pltpu.VMEM((256, NZ), F32),
            pltpu.VMEM((1024, NZ), BF16),
            pltpu.VMEM((384, BLK), BF16),
            pltpu.VMEM((192, NZ), F32),
            pltpu.VMEM((3, 7, ROWS, NZ), F32),
        ],
    )(state, labels, hot, drift, pulls, pulls_pos, own, left, right)
    left, right = swap(up, down, "gx")
    gathered = gather_y(call(fold_third_body, shape(48, NZ))(own, left, right))
    partial = call(push_body, shape(3, NQ))(state, labels, hot, grads, fields)
    return call_at(
        last_body,
        (shape(3, NQ), shape(3, NQ)),
        [pltpu.VMEM((48, NZ), F32), pltpu.VMEM((32, NZ), F32), pltpu.VMEM((128, NZ), BF16)],
        7,
    )(place, state, labels, hot, depth, grads, partial, gathered)


def solution(mesh):
    both = ("gx", "gy")
    return jax.shard_map(
        local,
        mesh=mesh,
        in_specs=(P(None, both), P(None, both), P(None, both), P(None, both), P(both), P(both), P(None, both), P(None, both)),
        out_specs=(P(None, both), P(None, both)),
        check_vma=False,
    )
```

```python
import functools

import jax
import jax.numpy as jnp
from jax import lax
from jax.experimental import pallas as pl
from jax.experimental.pallas import tpu as pltpu
from jax.sharding import PartitionSpec as P

CX = 2
CY = 8
NZ = 256
NQ = 4096
BLK = 4096
ROWS = 16
TABLES = 5
STEP = 0.25
STRENGTH = 0.02
F32 = jnp.float32
BF16 = jnp.bfloat16
highest = lax.Precision.HIGHEST
SECOND_SPANS = [(11 * p, 11, -1) for p in range(6)] + [(66 + 13 * p, 13, -2) for p in range(3)]
REPLIES = 105
VMEM_LIMIT = 24 * 1024 * 1024


def shape(*dims, dtype=F32):
    return jax.ShapeDtypeStruct(dims, dtype)


def call(body, outs, scratch=()):
    return pl.pallas_call(
        body,
        out_shape=outs,
        scratch_shapes=list(scratch),
        compiler_params=pltpu.CompilerParams(vmem_limit_bytes=VMEM_LIMIT),
    )


def split(x):
    high = x.astype(BF16)
    return high, (x - high.astype(F32)).astype(BF16)


def one_hot(index):
    rows = lax.broadcasted_iota(jnp.int32, (256, index.shape[1]), 0)
    return jnp.where(rows == index, 1.0, 0.0).astype(BF16)


def one_hot_columns(index):
    width = index.shape[1]
    down = jnp.transpose(jnp.broadcast_to(index, (8, width)))[:, 0:1]
    columns = lax.broadcasted_iota(jnp.int32, (width, 256), 1)
    return jnp.where(columns == down, 1.0, 0.0).astype(BF16)


MODE_S = "rows"
MODE_D = "nt"


def put_split(ref, first, values):
    rows = values.shape[0]
    high, low = split(values)
    half = ref.shape[0] // 2
    ref[first : first + rows, :] = high
    ref[half + first : half + first + rows, :] = low


def halves(x):
    half = x.shape[0] // 2
    return x[:half] + x[half:]


def pick_from(table, hot):
    return halves(jnp.dot(table[...], hot, preferred_element_type=F32))


def spread_onto(values, hot):
    return halves(
        lax.dot_general(values[...], hot, (((1,), (1,)), ((), ())), preferred_element_type=F32)
    )


def next_z(x):
    return pltpu.roll(x, NZ - 1, 1)


def prev_z(x):
    return pltpu.roll(x, 1, 1)


def diff_z(x):
    return 0.5 * (next_z(x) - prev_z(x))


def diff_row(x):
    return 0.5 * (pltpu.roll(x, ROWS - 1, 0) - pltpu.roll(x, 1, 0))


def axis_hits(rows, pitch, padded, cell_x, cell_y):
    index = lax.broadcasted_iota(jnp.int32, (padded, 1), 0)
    row_x = index // pitch
    row_y = index - row_x * pitch
    return row_x == cell_x, row_x - 1 == cell_x, row_y == cell_y, row_y - 1 == cell_y


def weights_of(hits, frac_x, frac_y):
    low_x, high_x, low_y, high_y = hits
    along_x = jnp.where(low_x, 1.0 - frac_x, jnp.where(high_x, frac_x, 0.0))
    along_y = jnp.where(low_y, 1.0 - frac_y, jnp.where(high_y, frac_y, 0.0))
    return along_x, along_y


def slopes_of(hits):
    low_x, high_x, low_y, high_y = hits
    along_x = jnp.where(low_x, -1.0, jnp.where(high_x, 1.0, 0.0))
    along_y = jnp.where(low_y, -1.0, jnp.where(high_y, 1.0, 0.0))
    return along_x, along_y


def row3(ref, at, first=0):
    return [ref[first + k : first + k + 1, at] for k in range(3)]


def line_matrix(me, window, offset, rows, first_y):
    target = lax.broadcasted_iota(jnp.int32, (ROWS, 8 * window), 0)
    column = lax.broadcasted_iota(jnp.int32, (ROWS, 8 * window), 1)
    device = column // window
    source = column - device * window - offset
    away = (CY * (me - device) + target - 2 - source - first_y + 128) & 63
    away = jnp.minimum(away, 64 - away)
    weight = STRENGTH * jnp.exp(away.astype(F32) * (-1.0 / 16.0))
    return jnp.where((source >= 0) & (source < rows), weight, 0.0)


def depth_body(out):
    target = lax.broadcasted_iota(jnp.int32, (NZ, NZ), 0)
    source = lax.broadcasted_iota(jnp.int32, (NZ, NZ), 1)
    away = jnp.abs(target - source)
    away = jnp.minimum(away, NZ - away)
    put_split(out, 0, jnp.exp(away.astype(F32) * (-1.0 / 16.0)))


def product(a, b_high, b_low):
    a_high, a_low = split(a)
    dot = functools.partial(jnp.dot, preferred_element_type=F32)
    return dot(a_high, b_high) + (dot(a_high, b_low) + dot(a_low, b_high))


def smooth(me, depth, gathered, spans, window, kept):
    for p, (start, rows, first_y) in enumerate(spans):
        first = min(start // 8 * 8, gathered.shape[1] - window)
        lines = line_matrix(me, window, start - first, rows, first_y)
        source = gathered[:, first : first + window, :].reshape(8 * window, NZ)
        kept[p * ROWS : (p + 1) * ROWS, :] = product(lines, *split(source))
    kept[0 : len(spans) * ROWS, :] = product(
        kept[0 : len(spans) * ROWS, :], depth[0:NZ, :], depth[NZ : 2 * NZ, :]
    )


def select_pulls(table, where_to, moved):
    taken = pick_from(table, one_hot(where_to & 255))
    rows = taken.shape[0] // 3
    chosen = moved * 16 + lax.shift_right_logical(where_to, 8)
    here = lax.broadcasted_iota(jnp.int32, (rows, where_to.shape[1]), 0) == chosen
    return [
        jnp.sum(jnp.where(here, taken[k * rows : k * rows + rows, :], 0.0), axis=0, keepdims=True)
        for k in range(3)
    ]


def requests_body(labels, wanted, ranks, marks, lists):
    for c in range(16):
        part = labels[3:4, c * 256 : (c + 1) * 256]
        marks[c : c + 1, :] = jnp.where(part == 3, 1.0, 0.0)
        marks[16 + c : 17 + c, :] = jnp.where(part == 4, 1.0, 0.0)
    row = lax.broadcasted_iota(jnp.int32, (256, 256), 0)
    column = lax.broadcasted_iota(jnp.int32, (256, 256), 1)
    earlier = jnp.where(row < column, 1.0, 0.0).astype(BF16)
    within = jnp.dot(marks[...].astype(BF16), earlier, preferred_element_type=F32)
    totals = jnp.broadcast_to(jnp.sum(marks[...], axis=1, keepdims=True), (32, 256))
    row = lax.broadcasted_iota(jnp.int32, (32, 32), 0)
    column = lax.broadcasted_iota(jnp.int32, (32, 32), 1)
    earlier = jnp.where((column < row) & (row // 16 == column // 16), 1.0, 0.0).astype(BF16)
    marks[...] = within + jnp.dot(earlier, totals.astype(BF16), preferred_element_type=F32)
    for c in range(16):
        part = labels[3:4, c * 256 : (c + 1) * 256]
        place = jnp.where(part == 3, marks[c : c + 1, :], jnp.where(part == 4, marks[16 + c : 17 + c, :], -1.0))
        ranks[0:1, c * 256 : (c + 1) * 256] = place.astype(jnp.int32)
    moved = labels[3:4, :]
    where_to = labels[4:5, :]
    upper = lax.shift_right_logical(where_to, 8).astype(F32)
    lower = (where_to & 255).astype(F32)
    lists[...] = jnp.zeros_like(lists)
    lists[0:1, :] = jnp.where(moved == 3, upper, 0.0)
    lists[1:2, :] = jnp.where(moved == 3, lower, 0.0)
    lists[2:3, :] = jnp.where(moved == 4, upper, 0.0)
    lists[3:4, :] = jnp.where(moved == 4, lower, 0.0)
    placed = lax.dot_general(
        lists[...].astype(BF16), one_hot(ranks[...]), (((1,), (1,)), ((), ())), preferred_element_type=F32
    )
    wanted[...] = jnp.zeros_like(wanted)
    wanted[0:1, :] = placed[0:1, :] * 256.0 + placed[1:2, :]
    wanted[1:2, :] = placed[2:3, :] * 256.0 + placed[3:4, :]


def replies_body(place, gathered, lent, out, table):
    put_split(table, 0, lent[...])
    out[...] = jnp.zeros_like(out)
    for n, side in enumerate((lax.rem(place[0] + 7, 8), lax.rem(place[0] + 1, 8))):
        wanted = gathered[side, 45 + n : 46 + n, :].astype(jnp.int32)
        taken = pick_from(table, one_hot(wanted & 255))
        here = lax.broadcasted_iota(jnp.int32, (16, 256), 0) == lax.shift_right_logical(wanted, 8)
        for k in range(3):
            row = n * 3 + k
            out[row : row + 1, :] = jnp.sum(
                jnp.where(here, taken[k * 16 : k * 16 + 16, :], 0.0), axis=0, keepdims=True
            )


def deposit_first_body(
    pos, mom, cell, dest, slot, pull_pos, pull_mom, own, up, down, lent, state, labels, hot, held, ints, lone, sems, lhs, acc
):
    copies = [
        pltpu.make_async_copy(pos, held.at[0], sems.at[0]),
        pltpu.make_async_copy(mom, held.at[1], sems.at[1]),
        pltpu.make_async_copy(cell, ints, sems.at[2]),
        pltpu.make_async_copy(dest, lone.at[0], sems.at[3]),
        pltpu.make_async_copy(slot, lone.at[1], sems.at[4]),
        pltpu.make_async_copy(pull_pos, held.at[2], sems.at[5]),
        pltpu.make_async_copy(pull_mom, held.at[3], sems.at[6]),
    ]
    for copy in copies:
        copy.start()
    own[...] = jnp.zeros_like(own)
    acc[...] = jnp.zeros_like(acc)
    for copy in copies:
        copy.wait()
    state[0:3, :] = held[0] + STEP * held[1]
    state[3:6, :] = held[1]
    labels[0:3, :] = ints[...]
    labels[3:4, :] = lone[0]
    labels[4:5, :] = lone[1]
    hot[...] = one_hot(ints[2:3, :])

    def block(b, carry):
        at = pl.ds(pl.multiple_of(b * BLK, BLK), BLK)
        frac = row3(state, at)
        cells = row3(labels, at)
        along_x, along_y = weights_of(axis_hits(27, CY + 1, 32, cells[0], cells[1]), frac[0], frac[1])
        planar = along_x * along_y
        put_split(lhs, 0, planar * (1.0 - frac[2]))
        put_split(lhs, 32, planar * frac[2])
        acc[...] += spread_onto(lhs, hot[...])
        return carry

    lax.fori_loop(0, NQ // BLK, block, 0)
    density = acc[0:32, :] + prev_z(acc[32:64, :])
    for x in range(3):
        own[x * ROWS + 2 : x * ROWS + 11, :] = density[x * 9 : x * 9 + 9, :]
    up[0:32, :] = own[16:48, :]
    down[0:32, :] = own[0:32, :]
    for k in range(6):
        source = held.at[2 + k // 3]
        for c in range(16):
            line = source[k % 3 : k % 3 + 1, c * 256 : (c + 1) * 256]
            at_row = 32 + k * 16 + c
            up[at_row : at_row + 1, :] = line
            down[at_row : at_row + 1, :] = line
            if k < 3:
                lent[at_row - 32 : at_row - 31, :] = line


def fold_first_body(own, left, right, pulls, wanted, out):
    rows = slice(2, 11)
    out[0:9, :] = left[0:16, :][rows]
    out[9:18, :] = (own[0:16, :] + left[16:32, :])[rows]
    out[18:27, :] = own[16:32, :][rows]
    out[27:36, :] = (own[32:48, :] + right[0:16, :])[rows]
    out[36:45, :] = right[16:32, :][rows]
    out[45:48, :] = wanted[0:3, :]
    out[48:96, :] = pulls[80:128, :]


def step_body(
    place,
    state,
    labels,
    hot,
    depth,
    gathered,
    mine,
    left,
    right,
    own,
    up,
    down,
    drift,
    pulls,
    fields,
    kept,
    pack,
    table,
    lhs,
    acc,
    planes,
):
    smooth(place[0], depth, gathered, [(9 * p, 9, 0) for p in range(5)], 16, kept)
    pack[...] = jnp.zeros_like(pack)
    for x in range(3):
        mid = (x + 1) * ROWS
        east = kept[mid + 18 : mid + 27, :]
        west = kept[mid - 14 : mid - 5, :]
        pack[x * 9 : x * 9 + 9, :] = -0.5 * (east - west)
        north = kept[mid + 3 : mid + 12, :]
        south = kept[mid + 1 : mid + 10, :]
        pack[32 + x * 9 : 32 + x * 9 + 9, :] = -0.5 * (north - south)
        pack[64 + x * 9 : 64 + x * 9 + 9, :] = -diff_z(kept[mid : mid + 16, :])[2:11, :]
    put_split(fields, 0, pack[...])
    put_split(fields, 96, next_z(pack[...]))
    ahead = lax.rem(place[0] + 1, 8)
    behind = lax.rem(place[0] + 7, 8)

    def rows_of(device):
        return lambda row: gathered[device, 48 + row : 64 + row, :]

    fill_table(
        table, [rows_at(mine, 80), rows_at(right, 80), rows_at(left, 80), rows_of(ahead), rows_of(behind)]
    )
    acc[...] = jnp.zeros_like(acc)

    def block(b, carry):
        at = pl.ds(pl.multiple_of(b * BLK, BLK), BLK)
        frac = row3(state, at)
        momentum = row3(state, at, 3)
        cells = row3(labels, at)
        moved = labels[3:4, at]
        where_to = labels[4:5, at]
        along_x, along_y = weights_of(axis_hits(27, CY + 1, 32, cells[0], cells[1]), frac[0], frac[1])
        planar = along_x * along_y
        sampled = pick_from(fields, hot[...])
        lower = planar * (1.0 - frac[2])
        upper = planar * frac[2]
        force = [
            jnp.sum(
                lower * sampled[d * 32 : d * 32 + 32, :] + upper * sampled[96 + d * 32 : 128 + d * 32, :],
                axis=0,
                keepdims=True,
            )
            for d in range(3)
        ]
        to_x = jnp.where(moved == 1, 1, jnp.where(moved == 2, -1, 0))
        to_y = jnp.where(moved == 3, 1, jnp.where(moved == 4, -1, 0))
        shift = [to_x.astype(F32), to_y.astype(F32), 0.0]
        second = [frac[d] - shift[d] + STEP * (momentum[d] + STEP * force[d]) for d in range(3)]
        home = select_pulls(table, where_to, moved)
        for d in range(3):
            drift[d : d + 1, at] = second[d]
            pulls[d : d + 1, at] = home[d]
        along_x, along_y = weights_of(
            axis_hits(55, CY + 3, 64, cells[0] + to_x + 1, cells[1] + to_y + 1), second[0], second[1]
        )
        planar = along_x * along_y
        upper = planar * second[2]
        lower = planar - upper
        for c in range(4):
            scale = None if c == 0 else STEP * home[c - 1]
            put_split(lhs, c * 128, lower if c == 0 else lower * scale)
            put_split(lhs, c * 128 + 64, upper if c == 0 else upper * scale)
        acc[...] += spread_onto(lhs, hot[...])
        return carry

    lax.fori_loop(0, NQ // BLK, block, 0)
    planes[...] = jnp.zeros_like(planes)
    for c in range(4):
        total = acc[c * 128 : c * 128 + 64, :] + prev_z(acc[c * 128 + 64 : c * 128 + 128, :])
        for x in range(5):
            planes[c, x, 1:12, :] = total[x * 11 : x * 11 + 11, :]
    for x in range(5):
        planes[2, x] = diff_row(planes[2, x]) + diff_z(planes[3, x])
    for c in range(3):
        for x in range(3):
            own[(c * 3 + x) * 16 : (c * 3 + x) * 16 + 16, :] = planes[c, x + 1]
        for x in range(2):
            up[(c * 2 + x) * 16 : (c * 2 + x) * 16 + 16, :] = planes[c, x + 3]
            down[(c * 2 + x) * 16 : (c * 2 + x) * 16 + 16, :] = planes[c, x]


def fill_table(table, sources):
    for k in range(3):
        for t, source in enumerate(sources):
            put_split(table, (k * len(sources) + t) * 16, source(k * 16))


def rows_at(ref, first):
    return lambda row: ref[first + row : first + row + 16, :]


def pulls_body(place, labels, ranks, mine, left, right, gathered, pulls, table, lists, replied):
    fill_table(table, [rows_at(mine, 0), rows_at(right, 32), rows_at(left, 32)])
    moved = labels[3:4, :]
    home = select_pulls(table, labels[4:5, :], moved)
    lists[...] = jnp.zeros_like(lists)
    lists[0:3, :] = gathered[lax.rem(place[0] + 1, 8), REPLIES : REPLIES + 3, :]
    lists[3:6, :] = gathered[lax.rem(place[0] + 7, 8), REPLIES + 3 : REPLIES + 6, :]
    put_split(replied, 0, lists[...])
    taken = pick_from(replied, one_hot(ranks[...]))
    for d in range(3):
        from_y = jnp.where(moved == 3, taken[d : d + 1, :], jnp.where(moved == 4, taken[d + 3 : d + 4, :], 0.0))
        pulls[d : d + 1, :] = home[d] + from_y


def fold_planes(own, left, right, channel):
    mine, theirs = channel * 48, channel * 32
    first = own[mine : mine + 16, :] + left[theirs : theirs + 16, :]
    second = (
        own[mine + 16 : mine + 32, :] + left[theirs + 16 : theirs + 32, :] + right[theirs : theirs + 16, :]
    )
    third = own[mine + 32 : mine + 48, :] + right[theirs + 16 : theirs + 32, :]
    return first, second, third


def fold_second_body(own, left, right, replies, out):
    for c in range(3):
        for n, values in enumerate(fold_planes(own, left, right, c)):
            start, rows, first_y = SECOND_SPANS[c * 3 + n]
            out[start : start + rows, :] = values[first_y + 2 : first_y + 2 + rows]
    out[REPLIES : REPLIES + 7, :] = replies[0:7, :]


def fold_third_body(own, left, right, out):
    for n, values in enumerate(fold_planes(own, left, right, 0)):
        out[n * 16 : n * 16 + 16, :] = values


def lines_body(place, depth, gathered, own, up, down):
    smooth(place[0], depth, gathered, SECOND_SPANS, 24, own)
    for c in range(2):
        up[c * 32 : c * 32 + 32, :] = own[c * 48 : c * 48 + 32, :]
        down[c * 32 : c * 32 + 32, :] = own[c * 48 + 16 : c * 48 + 48, :]
    up[64:80, :] = own[112:128, :]
    down[64:80, :] = own[112:128, :]


def back_body(
    state, labels, hot, drift, pulls, pulls_pos, mine, left, right, own, up, down, grads, wide, pack, fields, lhs, acc, planes
):
    for c in range(2):
        wide[c, 0:32, :] = left[c * 32 : c * 32 + 32, :]
        wide[c, 32:80, :] = mine[c * 48 : c * 48 + 48, :]
        wide[c, 80:112, :] = right[c * 32 : c * 32 + 32, :]
    wide[2, 16:32, :] = left[64:80, :]
    wide[2, 32:80, :] = mine[96:144, :]
    wide[2, 80:96, :] = right[64:80, :]
    pack[...] = jnp.zeros_like(pack)
    for x in range(5):
        mid = (x + 1) * 16
        first = x * 11
        pack[first : first + 11, :] = -0.5 * (wide[0, mid + 17 : mid + 28, :] - wide[0, mid - 15 : mid - 4, :])
        pack[64 + first : 75 + first, :] = -0.5 * (
            wide[0, mid + 2 : mid + 13, :] - wide[0, mid : mid + 11, :]
        )
        pack[128 + first : 139 + first, :] = -diff_z(wide[0, mid : mid + 16, :])[1:12, :]
        pack[192 + first : 203 + first, :] = (
            0.5 * (wide[1, mid + 17 : mid + 28, :] - wide[1, mid - 15 : mid - 4, :])
            + wide[2, mid + 1 : mid + 12, :]
        )
    put_split(fields, 0, pack[...])
    put_split(fields, 256, next_z(pack[...]))
    acc[...] = jnp.zeros_like(acc)

    def block(b, carry):
        at = pl.ds(pl.multiple_of(b * BLK, BLK), BLK)
        cells = row3(labels, at)
        moved = labels[3:4, at]
        second = row3(drift, at)
        pull_position = row3(pulls_pos, at)
        pull_momentum = row3(pulls, at)
        to_x = jnp.where(moved == 1, 1, jnp.where(moved == 2, -1, 0))
        to_y = jnp.where(moved == 3, 1, jnp.where(moved == 4, -1, 0))
        hits = axis_hits(55, CY + 3, 64, cells[0] + to_x + 1, cells[1] + to_y + 1)
        along_x, along_y = weights_of(hits, second[0], second[1])
        slope_x, slope_y = slopes_of(hits)
        sampled = pick_from(fields, hot[...])
        sides = []
        for s in range(2):
            mixed = sampled[s * 256 + 192 : s * 256 + 256, :]
            for d in range(3):
                mixed = mixed + (STEP * pull_momentum[d]) * sampled[s * 256 + d * 64 : s * 256 + d * 64 + 64, :]
            sides.append(mixed)
        level = sides[0] + second[2] * (sides[1] - sides[0])
        rise = sides[1] - sides[0]
        slopes = [
            jnp.sum(slope_x * (along_y * level), axis=0, keepdims=True),
            jnp.sum(slope_y * (along_x * level), axis=0, keepdims=True),
            jnp.sum(along_x * (along_y * rise), axis=0, keepdims=True),
        ]
        grad_drift = [pull_position[d] + slopes[d] for d in range(3)]
        grad_kick = [pull_momentum[d] + STEP * grad_drift[d] for d in range(3)]
        for d in range(3):
            grads[d : d + 1, at] = grad_drift[d]
            grads[d + 3 : d + 4, at] = grad_kick[d]
        frac = row3(state, at)
        along_x, along_y = weights_of(axis_hits(27, CY + 1, 32, cells[0], cells[1]), frac[0], frac[1])
        planar = along_x * along_y
        above = planar * frac[2]
        below = planar - above
        for c in range(3):
            scale = STEP * grad_kick[c]
            put_split(lhs, c * 64, below * scale)
            put_split(lhs, c * 64 + 32, above * scale)
        acc[...] += spread_onto(lhs, hot[...])
        return carry

    lax.fori_loop(0, NQ // BLK, block, 0)
    planes[...] = jnp.zeros_like(planes)
    for c in range(3):
        total = acc[c * 64 : c * 64 + 32, :] + prev_z(acc[c * 64 + 32 : c * 64 + 64, :])
        for x in range(3):
            planes[c, x + 2, 2:11, :] = total[x * 9 : x * 9 + 9, :]
    for x in range(5):
        spread = 0.5 * (planes[0, x + 2] - planes[0, x])
        if 1 <= x <= 3:
            spread = spread + diff_row(planes[1, x + 1]) + diff_z(planes[2, x + 1])
        if 1 <= x <= 3:
            own[(x - 1) * 16 : x * 16, :] = spread
        if x >= 3:
            up[(x - 3) * 16 : (x - 2) * 16, :] = spread
        if x <= 1:
            down[x * 16 : (x + 1) * 16, :] = spread


def mix_slopes(hits, frac, sides):
    along_x, along_y = weights_of(hits, frac[0], frac[1])
    slope_x, slope_y = slopes_of(hits)
    rise = sides[1] - sides[0]
    level = sides[0] + frac[2] * rise
    return [
        jnp.sum(slope_x * (along_y * level), axis=0, keepdims=True),
        jnp.sum(slope_y * (along_x * level), axis=0, keepdims=True),
        jnp.sum(along_x * (along_y * rise), axis=0, keepdims=True),
    ]


def push_body(state, labels, hot, grads, fields, out):
    frac = row3(state, slice(None))
    cells = row3(labels, slice(None))
    grad_kick = row3(grads, slice(None), 3)
    sampled = pick_from(fields, hot[...])
    sides = []
    for s in range(2):
        mixed = (STEP * grad_kick[0]) * sampled[s * 96 : s * 96 + 32, :]
        for d in range(1, 3):
            mixed = mixed + (STEP * grad_kick[d]) * sampled[s * 96 + d * 32 : s * 96 + d * 32 + 32, :]
        sides.append(mixed)
    slopes = mix_slopes(axis_hits(27, CY + 1, 32, cells[0], cells[1]), frac, sides)
    for d in range(3):
        out[d : d + 1, :] = grads[d : d + 1, :] + slopes[d]


def last_body(place, state, labels, hot, depth, grads, partial, gathered, grad_pos, grad_mom, kept, pack, own_field):
    smooth(place[0], depth, gathered, [(16 * p, 16, -2) for p in range(3)], 16, kept)
    pack[...] = jnp.zeros_like(pack)
    for x in range(3):
        pack[x * 9 : x * 9 + 9, :] = kept[x * 16 + 2 : x * 16 + 11, :]
    put_split(own_field, 0, pack[...])
    put_split(own_field, 32, next_z(pack[...]))
    frac = row3(state, slice(None))
    cells = row3(labels, slice(None))
    sampled = pick_from(own_field, hot[...])
    slopes = mix_slopes(
        axis_hits(27, CY + 1, 32, cells[0], cells[1]), frac, [sampled[0:32, :], sampled[32:64, :]]
    )
    for d in range(3):
        total = partial[d : d + 1, :] + slopes[d]
        grad_pos[d : d + 1, :] = total
        grad_mom[d : d + 1, :] = grads[d + 3 : d + 4, :] + STEP * total


def trade_x(first, second):
    peers = lax.axis_size("gx")
    inner = [(i, i ^ 1) for i in range(peers)]
    outer = [(i, (i + 1 if i % 2 else i - 1) % peers) for i in range(peers)]
    return lax.ppermute(first, "gx", inner), lax.ppermute(second, "gx", outer)


def put_pair(odd, ones, others):
    for flag in range(2):

        @pl.when(odd == flag)
        def _():
            ones[0][...] = others[flag][...]
            ones[1][...] = others[1 - flag][...]


def sided(body, placed, arrived=None, sent=None):
    def wrapped(place, *refs):
        refs = list(refs)
        odd = lax.shift_right_logical(place[0], 3) & 1
        if sent is not None:
            pair = refs[sent : sent + 2]
            made = refs[-2:]
            refs = refs[:-2]
            refs[sent : sent + 2] = made
        if arrived is not None:
            came = refs[arrived : arrived + 2]
            sides = refs[-2:]
            refs = refs[:-2]
            put_pair(odd, (sides[1], sides[0]), came)
            refs[arrived : arrived + 2] = sides
        if placed:
            body(place, *refs)
        else:
            body(*refs)
        if sent is not None:
            put_pair(odd, pair, made)

    return wrapped


def gather_y(x):
    return lax.all_gather(x, "gy", axis=0, tiled=False)


def local(pos, mom, cell, cell_second, dest, slot, pull_pos, pull_mom):
    place = lax.axis_index(("gx", "gy")).astype(jnp.int32).reshape(1)
    dest = dest.reshape(1, NQ)
    slot = slot.reshape(1, NQ)
    scalar = pl.BlockSpec(memory_space=pltpu.SMEM)
    vmem = pl.BlockSpec(memory_space=pltpu.VMEM)

    def call_at(body, outs, scratch, operands):
        return pl.pallas_call(
            body,
            out_shape=outs,
            in_specs=[scalar] + [vmem] * operands,
            scratch_shapes=list(scratch),
            compiler_params=pltpu.CompilerParams(vmem_limit_bytes=VMEM_LIMIT),
        )

    depth = pl.pallas_call(
        depth_body,
        out_shape=shape(2 * NZ, NZ, dtype=BF16),
        compiler_params=pltpu.CompilerParams(vmem_limit_bytes=VMEM_LIMIT),
        cost_estimate=pl.CostEstimate(flops=10**9, bytes_accessed=10**7, transcendentals=10**6),
    )()
    in_hbm = [
        pltpu.with_memory_space_constraint(x, pltpu.HBM)
        for x in (pos, mom, cell, dest, slot, pull_pos, pull_mom)
    ]
    own, up, down, lent, state, labels, hot = pl.pallas_call(
        sided(deposit_first_body, False, sent=8),
        out_shape=(
            shape(48, NZ),
            shape(128, NZ),
            shape(128, NZ),
            shape(48, NZ),
            shape(6, NQ),
            shape(5, NQ, dtype=jnp.int32),
            shape(NZ, NQ, dtype=BF16),
        ),
        in_specs=[scalar] + [pl.BlockSpec(memory_space=pltpu.HBM)] * 7,
        scratch_shapes=[
            pltpu.VMEM((4, 3, NQ), F32),
            pltpu.VMEM((3, NQ), jnp.int32),
            pltpu.VMEM((2, 1, NQ), jnp.int32),
            pltpu.SemaphoreType.DMA((7,)),
            pltpu.VMEM((128, BLK), BF16),
            pltpu.VMEM((64, NZ), F32),
            pltpu.VMEM((128, NZ), F32),
            pltpu.VMEM((128, NZ), F32),
        ],
        compiler_params=pltpu.CompilerParams(vmem_limit_bytes=VMEM_LIMIT),
    )(place, *in_hbm)
    mine, (left, right) = up, trade_x(up, down)
    first_left, first_right = left, right
    wanted, ranks = call(
        requests_body,
        (shape(8, NZ), shape(1, NQ, dtype=jnp.int32)),
        [pltpu.VMEM((32, NZ), F32), pltpu.VMEM((16, NQ), F32)],
    )(labels)
    gathered = gather_y(call_at(
            sided(fold_first_body, False, arrived=1), shape(96, NZ), [pltpu.VMEM((128, NZ), F32)] * 2, 5
        )(place, own, left, right, up, wanted))
    replies = call_at(replies_body, shape(8, NZ), [pltpu.VMEM((96, NZ), BF16)], 2)(place, gathered, lent)
    own, up, down, drift, pulls, fields = call_at(
        sided(step_body, True, arrived=6, sent=9),
        (
            shape(144, NZ),
            shape(96, NZ),
            shape(96, NZ),
            shape(3, NQ),
            shape(3, NQ),
            shape(384, NZ, dtype=BF16),
        ),
        [
            pltpu.VMEM((80, NZ), F32),
            pltpu.VMEM((96, NZ), F32),
            pltpu.VMEM((480, NZ), BF16),
            pltpu.VMEM((1024, BLK), BF16),
            pltpu.VMEM((512, NZ), F32),
            pltpu.VMEM((4, 5, ROWS, NZ), F32),
        ]
        + [pltpu.VMEM((128, NZ), F32)] * 2
        + [pltpu.VMEM((96, NZ), F32)] * 2,
        8,
    )(place, state, labels, hot, depth, gathered, mine, left, right)
    left, right = trade_x(up, down)
    gathered = gather_y(call_at(
            sided(fold_second_body, False, arrived=1), shape(112, NZ), [pltpu.VMEM((96, NZ), F32)] * 2, 4
        )(place, own, left, right, replies))
    own, up, down = call_at(
        sided(lines_body, True, sent=3),
        (shape(144, NZ), shape(80, NZ), shape(80, NZ)),
        [pltpu.VMEM((80, NZ), F32)] * 2,
        2,
    )(
        place, depth, gathered
    )
    left, right = trade_x(up, down)
    pulls_pos = call_at(
        sided(pulls_body, True, arrived=3),
        shape(3, NQ),
        [pltpu.VMEM((288, NZ), BF16), pltpu.VMEM((16, NZ), F32), pltpu.VMEM((32, NZ), BF16)]
        + [pltpu.VMEM((128, NZ), F32)] * 2,
        6,
    )(place, labels, ranks, lent, first_left, first_right, gathered)
    own, up, down, grads = call_at(
        sided(back_body, False, arrived=7, sent=10),
        (shape(48, NZ), shape(32, NZ), shape(32, NZ), shape(6, NQ)),
        [
            pltpu.VMEM((3, 112, NZ), F32),
            pltpu.VMEM((256, NZ), F32),
            pltpu.VMEM((1024, NZ), BF16),
            pltpu.VMEM((384, BLK), BF16),
            pltpu.VMEM((192, NZ), F32),
            pltpu.VMEM((3, 7, ROWS, NZ), F32),
        ]
        + [pltpu.VMEM((80, NZ), F32)] * 2
        + [pltpu.VMEM((32, NZ), F32)] * 2,
        9,
    )(place, state, labels, hot, drift, pulls, pulls_pos, own, left, right)
    left, right = trade_x(up, down)
    gathered = gather_y(call_at(
            sided(fold_third_body, False, arrived=1), shape(48, NZ), [pltpu.VMEM((32, NZ), F32)] * 2, 3
        )(place, own, left, right))
    partial = call(push_body, shape(3, NQ))(state, labels, hot, grads, fields)
    return call_at(
        last_body,
        (shape(3, NQ), shape(3, NQ)),
        [pltpu.VMEM((48, NZ), F32), pltpu.VMEM((32, NZ), F32), pltpu.VMEM((128, NZ), BF16)],
        7,
    )(place, state, labels, hot, depth, grads, partial, gathered)


def solution(mesh):
    both = ("gx", "gy")
    return jax.shard_map(
        local,
        mesh=mesh,
        in_specs=(P(None, both), P(None, both), P(None, both), P(None, both), P(both), P(both), P(None, both), P(None, both)),
        out_specs=(P(None, both), P(None, both)),
        check_vma=False,
    )
```

```python
import functools

import jax
import jax.numpy as jnp
from jax import lax
from jax.experimental import pallas as pl
from jax.experimental.pallas import tpu as pltpu
from jax.sharding import PartitionSpec as P

CX = 2
CY = 8
NZ = 256
NQ = 4096
BLK = 4096
ROWS = 16
TABLES = 5
STEP = 0.25
STRENGTH = 0.02
F32 = jnp.float32
BF16 = jnp.bfloat16
highest = lax.Precision.HIGHEST
SECOND_SPANS = [(11 * p, 11, -1) for p in range(6)] + [(66 + 13 * p, 13, -2) for p in range(3)]
REPLIES = 105
PHASES = [
    ([(9 * p, 9, 0) for p in range(5)], 16, 96),
    (SECOND_SPANS, 24, 112),
    ([(16 * p, 16, -2) for p in range(3)], 16, 48),
]
LINES = 32 * sum(len(spans) for spans, _, _ in PHASES)
VMEM_LIMIT = 24 * 1024 * 1024


def shape(*dims, dtype=F32):
    return jax.ShapeDtypeStruct(dims, dtype)


def call(body, outs, scratch=()):
    return pl.pallas_call(
        body,
        out_shape=outs,
        scratch_shapes=list(scratch),
        compiler_params=pltpu.CompilerParams(vmem_limit_bytes=VMEM_LIMIT),
    )


def split(x):
    high = x.astype(BF16)
    return high, (x - high.astype(F32)).astype(BF16)


def one_hot(index):
    rows = lax.broadcasted_iota(jnp.int32, (256, index.shape[1]), 0)
    return jnp.where(rows == index, 1.0, 0.0).astype(BF16)


def one_hot_columns(index):
    width = index.shape[1]
    down = jnp.transpose(jnp.broadcast_to(index, (8, width)))[:, 0:1]
    columns = lax.broadcasted_iota(jnp.int32, (width, 256), 1)
    return jnp.where(columns == down, 1.0, 0.0).astype(BF16)


MODE_S = "rows"
MODE_D = "nt"


def put_split(ref, first, values):
    rows = values.shape[0]
    high, low = split(values)
    half = ref.shape[0] // 2
    ref[first : first + rows, :] = high
    ref[half + first : half + first + rows, :] = low


def halves(x):
    half = x.shape[0] // 2
    return x[:half] + x[half:]


def pick_from(table, hot):
    return halves(jnp.dot(table[...], hot, preferred_element_type=F32))


def spread_onto(values, hot):
    return halves(
        lax.dot_general(values[...], hot, (((1,), (1,)), ((), ())), preferred_element_type=F32)
    )


def next_z(x):
    return pltpu.roll(x, NZ - 1, 1)


def prev_z(x):
    return pltpu.roll(x, 1, 1)


def diff_z(x):
    return 0.5 * (next_z(x) - prev_z(x))


def diff_row(x):
    return 0.5 * (pltpu.roll(x, ROWS - 1, 0) - pltpu.roll(x, 1, 0))


def axis_hits(rows, pitch, padded, cell_x, cell_y):
    index = lax.broadcasted_iota(jnp.int32, (padded, 1), 0)
    row_x = index // pitch
    row_y = index - row_x * pitch
    return row_x == cell_x, row_x - 1 == cell_x, row_y == cell_y, row_y - 1 == cell_y


def weights_of(hits, frac_x, frac_y):
    low_x, high_x, low_y, high_y = hits
    along_x = jnp.where(low_x, 1.0 - frac_x, jnp.where(high_x, frac_x, 0.0))
    along_y = jnp.where(low_y, 1.0 - frac_y, jnp.where(high_y, frac_y, 0.0))
    return along_x, along_y


def slopes_of(hits):
    low_x, high_x, low_y, high_y = hits
    along_x = jnp.where(low_x, -1.0, jnp.where(high_x, 1.0, 0.0))
    along_y = jnp.where(low_y, -1.0, jnp.where(high_y, 1.0, 0.0))
    return along_x, along_y


def row3(ref, at, first=0):
    return [ref[first + k : first + k + 1, at] for k in range(3)]


def line_matrix(me, window, offset, rows, first_y):
    target = lax.broadcasted_iota(jnp.int32, (ROWS, 8 * window), 0)
    column = lax.broadcasted_iota(jnp.int32, (ROWS, 8 * window), 1)
    device = column // window
    source = column - device * window - offset
    away = (CY * (me - device) + target - 2 - source - first_y + 128) & 63
    away = jnp.minimum(away, 64 - away)
    weight = STRENGTH * jnp.exp(away.astype(F32) * (-1.0 / 16.0))
    return jnp.where((source >= 0) & (source < rows), weight, 0.0)


def depth_body(place, out, lines):
    target = lax.broadcasted_iota(jnp.int32, (NZ, NZ), 0)
    source = lax.broadcasted_iota(jnp.int32, (NZ, NZ), 1)
    away = jnp.abs(target - source)
    away = jnp.minimum(away, NZ - away)
    put_split(out, 0, jnp.exp(away.astype(F32) * (-1.0 / 16.0)))
    at = 0
    for spans, window, total in PHASES:
        for start, rows, first_y in spans:
            matrix = line_matrix(place[0], window, start - window_start(start, window, total), rows, first_y)
            high, low = split(matrix)
            lines[at : at + 16, 0 : 8 * window] = high
            lines[at + 16 : at + 32, 0 : 8 * window] = low
            at += 32


def window_start(start, window, total):
    return min(start // 8 * 8, total - window)


def product(a_high, a_low, b_high, b_low):
    dot = functools.partial(jnp.dot, preferred_element_type=F32)
    return dot(a_high, b_high) + (dot(a_high, b_low) + dot(a_low, b_high))


def smooth(depth, lines, gathered, phase, kept):
    spans, window, total = PHASES[phase]
    at = 32 * sum(len(PHASES[n][0]) for n in range(phase))
    for p, (start, _, _) in enumerate(spans):
        first = window_start(start, window, total)
        source = gathered[:, first : first + window, :].reshape(8 * window, NZ)
        along = lines[at : at + 16, 0 : 8 * window], lines[at + 16 : at + 32, 0 : 8 * window]
        kept[p * ROWS : (p + 1) * ROWS, :] = product(*along, *split(source))
        at += 32
    kept[0 : len(spans) * ROWS, :] = product(
        *split(kept[0 : len(spans) * ROWS, :]), depth[0:NZ, :], depth[NZ : 2 * NZ, :]
    )


def select_pulls(table, where_to, moved):
    taken = pick_from(table, one_hot(where_to & 255))
    rows = taken.shape[0] // 3
    chosen = moved * 16 + lax.shift_right_logical(where_to, 8)
    here = lax.broadcasted_iota(jnp.int32, (rows, where_to.shape[1]), 0) == chosen
    return [
        jnp.sum(jnp.where(here, taken[k * rows : k * rows + rows, :], 0.0), axis=0, keepdims=True)
        for k in range(3)
    ]


def requests_body(labels, wanted, ranks, marks, lists):
    for c in range(16):
        part = labels[3:4, c * 256 : (c + 1) * 256]
        marks[c : c + 1, :] = jnp.where(part == 3, 1.0, 0.0)
        marks[16 + c : 17 + c, :] = jnp.where(part == 4, 1.0, 0.0)
    row = lax.broadcasted_iota(jnp.int32, (256, 256), 0)
    column = lax.broadcasted_iota(jnp.int32, (256, 256), 1)
    earlier = jnp.where(row < column, 1.0, 0.0).astype(BF16)
    within = jnp.dot(marks[...].astype(BF16), earlier, preferred_element_type=F32)
    totals = jnp.broadcast_to(jnp.sum(marks[...], axis=1, keepdims=True), (32, 256))
    row = lax.broadcasted_iota(jnp.int32, (32, 32), 0)
    column = lax.broadcasted_iota(jnp.int32, (32, 32), 1)
    earlier = jnp.where((column < row) & (row // 16 == column // 16), 1.0, 0.0).astype(BF16)
    marks[...] = within + jnp.dot(earlier, totals.astype(BF16), preferred_element_type=F32)
    for c in range(16):
        part = labels[3:4, c * 256 : (c + 1) * 256]
        place = jnp.where(part == 3, marks[c : c + 1, :], jnp.where(part == 4, marks[16 + c : 17 + c, :], -1.0))
        ranks[0:1, c * 256 : (c + 1) * 256] = place.astype(jnp.int32)
    moved = labels[3:4, :]
    where_to = labels[4:5, :]
    upper = lax.shift_right_logical(where_to, 8).astype(F32)
    lower = (where_to & 255).astype(F32)
    lists[...] = jnp.zeros_like(lists)
    lists[0:1, :] = jnp.where(moved == 3, upper, 0.0)
    lists[1:2, :] = jnp.where(moved == 3, lower, 0.0)
    lists[2:3, :] = jnp.where(moved == 4, upper, 0.0)
    lists[3:4, :] = jnp.where(moved == 4, lower, 0.0)
    placed = lax.dot_general(
        lists[...].astype(BF16), one_hot(ranks[...]), (((1,), (1,)), ((), ())), preferred_element_type=F32
    )
    wanted[...] = jnp.zeros_like(wanted)
    wanted[0:1, :] = placed[0:1, :] * 256.0 + placed[1:2, :]
    wanted[1:2, :] = placed[2:3, :] * 256.0 + placed[3:4, :]


def replies_body(place, gathered, lent, out, table):
    put_split(table, 0, lent[...])
    out[...] = jnp.zeros_like(out)
    for n, side in enumerate((lax.rem(place[0] + 7, 8), lax.rem(place[0] + 1, 8))):
        wanted = gathered[side, 45 + n : 46 + n, :].astype(jnp.int32)
        taken = pick_from(table, one_hot(wanted & 255))
        here = lax.broadcasted_iota(jnp.int32, (16, 256), 0) == lax.shift_right_logical(wanted, 8)
        for k in range(3):
            row = n * 3 + k
            out[row : row + 1, :] = jnp.sum(
                jnp.where(here, taken[k * 16 : k * 16 + 16, :], 0.0), axis=0, keepdims=True
            )


def deposit_first_body(
    pos, mom, cell, dest, slot, pull_pos, pull_mom, own, up, down, lent, state, labels, hot, held, ints, lone, sems, lhs, acc
):
    copies = [
        pltpu.make_async_copy(pos, held.at[0], sems.at[0]),
        pltpu.make_async_copy(mom, held.at[1], sems.at[1]),
        pltpu.make_async_copy(cell, ints, sems.at[2]),
        pltpu.make_async_copy(dest, lone.at[0], sems.at[3]),
        pltpu.make_async_copy(slot, lone.at[1], sems.at[4]),
        pltpu.make_async_copy(pull_pos, held.at[2], sems.at[5]),
        pltpu.make_async_copy(pull_mom, held.at[3], sems.at[6]),
    ]
    for copy in copies:
        copy.start()
    own[...] = jnp.zeros_like(own)
    acc[...] = jnp.zeros_like(acc)
    copies[0].wait()
    copies[1].wait()
    state[0:3, :] = held[0] + STEP * held[1]
    state[3:6, :] = held[1]
    copies[2].wait()
    labels[0:3, :] = ints[...]
    hot[...] = one_hot(ints[2:3, :])

    def block(b, carry):
        at = pl.ds(pl.multiple_of(b * BLK, BLK), BLK)
        frac = row3(state, at)
        cells = row3(labels, at)
        along_x, along_y = weights_of(axis_hits(27, CY + 1, 32, cells[0], cells[1]), frac[0], frac[1])
        planar = along_x * along_y
        put_split(lhs, 0, planar * (1.0 - frac[2]))
        put_split(lhs, 32, planar * frac[2])
        acc[...] += spread_onto(lhs, hot[...])
        return carry

    lax.fori_loop(0, NQ // BLK, block, 0)
    density = acc[0:32, :] + prev_z(acc[32:64, :])
    for x in range(3):
        own[x * ROWS + 2 : x * ROWS + 11, :] = density[x * 9 : x * 9 + 9, :]
    up[0:32, :] = own[16:48, :]
    down[0:32, :] = own[0:32, :]
    for copy in copies[3:]:
        copy.wait()
    labels[3:4, :] = lone[0]
    labels[4:5, :] = lone[1]
    for k in range(6):
        source = held.at[2 + k // 3]
        for c in range(16):
            line = source[k % 3 : k % 3 + 1, c * 256 : (c + 1) * 256]
            at_row = 32 + k * 16 + c
            up[at_row : at_row + 1, :] = line
            down[at_row : at_row + 1, :] = line
            if k < 3:
                lent[at_row - 32 : at_row - 31, :] = line


def fold_first_body(own, left, right, pulls, wanted, out):
    rows = slice(2, 11)
    out[0:9, :] = left[0:16, :][rows]
    out[9:18, :] = (own[0:16, :] + left[16:32, :])[rows]
    out[18:27, :] = own[16:32, :][rows]
    out[27:36, :] = (own[32:48, :] + right[0:16, :])[rows]
    out[36:45, :] = right[16:32, :][rows]
    out[45:48, :] = wanted[0:3, :]
    out[48:96, :] = pulls[80:128, :]


def step_body(
    place,
    state,
    labels,
    hot,
    depth,
    lines,
    gathered,
    mine,
    left,
    right,
    own,
    up,
    down,
    drift,
    pulls,
    fields,
    kept,
    pack,
    table,
    lhs,
    acc,
    planes,
):
    smooth(depth, lines, gathered, 0, kept)
    pack[...] = jnp.zeros_like(pack)
    for x in range(3):
        mid = (x + 1) * ROWS
        east = kept[mid + 18 : mid + 27, :]
        west = kept[mid - 14 : mid - 5, :]
        pack[x * 9 : x * 9 + 9, :] = -0.5 * (east - west)
        north = kept[mid + 3 : mid + 12, :]
        south = kept[mid + 1 : mid + 10, :]
        pack[32 + x * 9 : 32 + x * 9 + 9, :] = -0.5 * (north - south)
        pack[64 + x * 9 : 64 + x * 9 + 9, :] = -diff_z(kept[mid : mid + 16, :])[2:11, :]
    put_split(fields, 0, pack[...])
    put_split(fields, 96, next_z(pack[...]))
    ahead = lax.rem(place[0] + 1, 8)
    behind = lax.rem(place[0] + 7, 8)

    def rows_of(device):
        return lambda row: gathered[device, 48 + row : 64 + row, :]

    fill_table(
        table, [rows_at(mine, 80), rows_at(right, 80), rows_at(left, 80), rows_of(ahead), rows_of(behind)]
    )
    acc[...] = jnp.zeros_like(acc)

    def block(b, carry):
        at = pl.ds(pl.multiple_of(b * BLK, BLK), BLK)
        frac = row3(state, at)
        momentum = row3(state, at, 3)
        cells = row3(labels, at)
        moved = labels[3:4, at]
        where_to = labels[4:5, at]
        along_x, along_y = weights_of(axis_hits(27, CY + 1, 32, cells[0], cells[1]), frac[0], frac[1])
        planar = along_x * along_y
        sampled = pick_from(fields, hot[...])
        lower = planar * (1.0 - frac[2])
        upper = planar * frac[2]
        force = [
            jnp.sum(
                lower * sampled[d * 32 : d * 32 + 32, :] + upper * sampled[96 + d * 32 : 128 + d * 32, :],
                axis=0,
                keepdims=True,
            )
            for d in range(3)
        ]
        to_x = jnp.where(moved == 1, 1, jnp.where(moved == 2, -1, 0))
        to_y = jnp.where(moved == 3, 1, jnp.where(moved == 4, -1, 0))
        shift = [to_x.astype(F32), to_y.astype(F32), 0.0]
        second = [frac[d] - shift[d] + STEP * (momentum[d] + STEP * force[d]) for d in range(3)]
        home = select_pulls(table, where_to, moved)
        for d in range(3):
            drift[d : d + 1, at] = second[d]
            pulls[d : d + 1, at] = home[d]
        along_x, along_y = weights_of(
            axis_hits(55, CY + 3, 56, cells[0] + to_x + 1, cells[1] + to_y + 1), second[0], second[1]
        )
        planar = along_x * along_y
        upper = planar * second[2]
        lower = planar - upper
        for c in range(4):
            scale = None if c == 0 else STEP * home[c - 1]
            both = jnp.concatenate([lower, upper], 0)
            put_split(lhs, c * 112, both if c == 0 else both * scale)
        acc[...] += spread_onto(lhs, hot[...])
        return carry

    lax.fori_loop(0, NQ // BLK, block, 0)
    planes[...] = jnp.zeros_like(planes)
    for c in range(4):
        total = acc[c * 112 : c * 112 + 56, :] + prev_z(acc[c * 112 + 56 : c * 112 + 112, :])
        for x in range(5):
            planes[c, x, 1:12, :] = total[x * 11 : x * 11 + 11, :]
    for x in range(5):
        planes[2, x] = diff_row(planes[2, x]) + diff_z(planes[3, x])
    for c in range(3):
        for x in range(3):
            own[(c * 3 + x) * 16 : (c * 3 + x) * 16 + 16, :] = planes[c, x + 1]
        for x in range(2):
            up[(c * 2 + x) * 16 : (c * 2 + x) * 16 + 16, :] = planes[c, x + 3]
            down[(c * 2 + x) * 16 : (c * 2 + x) * 16 + 16, :] = planes[c, x]


def fill_table(table, sources):
    for k in range(3):
        for t, source in enumerate(sources):
            put_split(table, (k * len(sources) + t) * 16, source(k * 16))


def rows_at(ref, first):
    return lambda row: ref[first + row : first + row + 16, :]


def pulls_body(place, labels, ranks, mine, left, right, gathered, pulls, table, lists, replied):
    fill_table(table, [rows_at(mine, 0), rows_at(right, 32), rows_at(left, 32)])
    moved = labels[3:4, :]
    home = select_pulls(table, labels[4:5, :], moved)
    lists[...] = jnp.zeros_like(lists)
    lists[0:3, :] = gathered[lax.rem(place[0] + 1, 8), REPLIES : REPLIES + 3, :]
    lists[3:6, :] = gathered[lax.rem(place[0] + 7, 8), REPLIES + 3 : REPLIES + 6, :]
    put_split(replied, 0, lists[...])
    taken = pick_from(replied, one_hot(ranks[...]))
    for d in range(3):
        from_y = jnp.where(moved == 3, taken[d : d + 1, :], jnp.where(moved == 4, taken[d + 3 : d + 4, :], 0.0))
        pulls[d : d + 1, :] = home[d] + from_y


def fold_planes(own, left, right, channel):
    mine, theirs = channel * 48, channel * 32
    first = own[mine : mine + 16, :] + left[theirs : theirs + 16, :]
    second = (
        own[mine + 16 : mine + 32, :] + left[theirs + 16 : theirs + 32, :] + right[theirs : theirs + 16, :]
    )
    third = own[mine + 32 : mine + 48, :] + right[theirs + 16 : theirs + 32, :]
    return first, second, third


def fold_second_body(own, left, right, replies, out):
    for c in range(3):
        for n, values in enumerate(fold_planes(own, left, right, c)):
            start, rows, first_y = SECOND_SPANS[c * 3 + n]
            out[start : start + rows, :] = values[first_y + 2 : first_y + 2 + rows]
    out[REPLIES : REPLIES + 7, :] = replies[0:7, :]


def fold_third_body(own, left, right, out):
    for n, values in enumerate(fold_planes(own, left, right, 0)):
        out[n * 16 : n * 16 + 16, :] = values


def lines_body(depth, lines, gathered, own, up, down):
    smooth(depth, lines, gathered, 1, own)
    for c in range(2):
        up[c * 32 : c * 32 + 32, :] = own[c * 48 : c * 48 + 32, :]
        down[c * 32 : c * 32 + 32, :] = own[c * 48 + 16 : c * 48 + 48, :]
    up[64:80, :] = own[112:128, :]
    down[64:80, :] = own[112:128, :]


def back_body(
    state, labels, hot, drift, pulls, pulls_pos, mine, left, right, own, up, down, grads, wide, pack, fields, lhs, acc, planes
):
    for c in range(2):
        wide[c, 0:32, :] = left[c * 32 : c * 32 + 32, :]
        wide[c, 32:80, :] = mine[c * 48 : c * 48 + 48, :]
        wide[c, 80:112, :] = right[c * 32 : c * 32 + 32, :]
    wide[2, 16:32, :] = left[64:80, :]
    wide[2, 32:80, :] = mine[96:144, :]
    wide[2, 80:96, :] = right[64:80, :]
    pack[...] = jnp.zeros_like(pack)
    for x in range(5):
        mid = (x + 1) * 16
        first = x * 11
        pack[first : first + 11, :] = -0.5 * (wide[0, mid + 17 : mid + 28, :] - wide[0, mid - 15 : mid - 4, :])
        pack[56 + first : 67 + first, :] = -0.5 * (
            wide[0, mid + 2 : mid + 13, :] - wide[0, mid : mid + 11, :]
        )
        pack[112 + first : 123 + first, :] = -diff_z(wide[0, mid : mid + 16, :])[1:12, :]
        pack[168 + first : 179 + first, :] = (
            0.5 * (wide[1, mid + 17 : mid + 28, :] - wide[1, mid - 15 : mid - 4, :])
            + wide[2, mid + 1 : mid + 12, :]
        )
    put_split(fields, 0, pack[...])
    put_split(fields, 224, next_z(pack[...]))
    acc[...] = jnp.zeros_like(acc)

    def block(b, carry):
        at = pl.ds(pl.multiple_of(b * BLK, BLK), BLK)
        cells = row3(labels, at)
        moved = labels[3:4, at]
        second = row3(drift, at)
        pull_position = row3(pulls_pos, at)
        pull_momentum = row3(pulls, at)
        to_x = jnp.where(moved == 1, 1, jnp.where(moved == 2, -1, 0))
        to_y = jnp.where(moved == 3, 1, jnp.where(moved == 4, -1, 0))
        hits = axis_hits(55, CY + 3, 56, cells[0] + to_x + 1, cells[1] + to_y + 1)
        along_x, along_y = weights_of(hits, second[0], second[1])
        slope_x, slope_y = slopes_of(hits)
        sampled = pick_from(fields, hot[...])
        sides = []
        for s in range(2):
            mixed = sampled[s * 224 + 168 : s * 224 + 224, :]
            for d in range(3):
                mixed = mixed + (STEP * pull_momentum[d]) * sampled[s * 224 + d * 56 : s * 224 + d * 56 + 56, :]
            sides.append(mixed)
        level = sides[0] + second[2] * (sides[1] - sides[0])
        rise = sides[1] - sides[0]
        slopes = [
            jnp.sum(slope_x * (along_y * level), axis=0, keepdims=True),
            jnp.sum(slope_y * (along_x * level), axis=0, keepdims=True),
            jnp.sum(along_x * (along_y * rise), axis=0, keepdims=True),
        ]
        grad_drift = [pull_position[d] + slopes[d] for d in range(3)]
        grad_kick = [pull_momentum[d] + STEP * grad_drift[d] for d in range(3)]
        for d in range(3):
            grads[d : d + 1, at] = grad_drift[d]
            grads[d + 3 : d + 4, at] = grad_kick[d]
        frac = row3(state, at)
        along_x, along_y = weights_of(axis_hits(27, CY + 1, 32, cells[0], cells[1]), frac[0], frac[1])
        planar = along_x * along_y
        above = planar * frac[2]
        below = planar - above
        for c in range(3):
            scale = STEP * grad_kick[c]
            put_split(lhs, c * 64, below * scale)
            put_split(lhs, c * 64 + 32, above * scale)
        acc[...] += spread_onto(lhs, hot[...])
        return carry

    lax.fori_loop(0, NQ // BLK, block, 0)
    planes[...] = jnp.zeros_like(planes)
    for c in range(3):
        total = acc[c * 64 : c * 64 + 32, :] + prev_z(acc[c * 64 + 32 : c * 64 + 64, :])
        for x in range(3):
            planes[c, x + 2, 2:11, :] = total[x * 9 : x * 9 + 9, :]
    for x in range(5):
        spread = 0.5 * (planes[0, x + 2] - planes[0, x])
        if 1 <= x <= 3:
            spread = spread + diff_row(planes[1, x + 1]) + diff_z(planes[2, x + 1])
        if 1 <= x <= 3:
            own[(x - 1) * 16 : x * 16, :] = spread
        if x >= 3:
            up[(x - 3) * 16 : (x - 2) * 16, :] = spread
        if x <= 1:
            down[x * 16 : (x + 1) * 16, :] = spread


def mix_slopes(hits, frac, sides):
    along_x, along_y = weights_of(hits, frac[0], frac[1])
    slope_x, slope_y = slopes_of(hits)
    rise = sides[1] - sides[0]
    level = sides[0] + frac[2] * rise
    return [
        jnp.sum(slope_x * (along_y * level), axis=0, keepdims=True),
        jnp.sum(slope_y * (along_x * level), axis=0, keepdims=True),
        jnp.sum(along_x * (along_y * rise), axis=0, keepdims=True),
    ]


def push_body(state, labels, hot, grads, fields, out):
    frac = row3(state, slice(None))
    cells = row3(labels, slice(None))
    grad_kick = row3(grads, slice(None), 3)
    sampled = pick_from(fields, hot[...])
    sides = []
    for s in range(2):
        mixed = (STEP * grad_kick[0]) * sampled[s * 96 : s * 96 + 32, :]
        for d in range(1, 3):
            mixed = mixed + (STEP * grad_kick[d]) * sampled[s * 96 + d * 32 : s * 96 + d * 32 + 32, :]
        sides.append(mixed)
    slopes = mix_slopes(axis_hits(27, CY + 1, 32, cells[0], cells[1]), frac, sides)
    for d in range(3):
        out[d : d + 1, :] = grads[d : d + 1, :] + slopes[d]


def last_body(state, labels, hot, depth, lines, grads, partial, gathered, grad_pos, grad_mom, kept, pack, own_field):
    smooth(depth, lines, gathered, 2, kept)
    pack[...] = jnp.zeros_like(pack)
    for x in range(3):
        pack[x * 9 : x * 9 + 9, :] = kept[x * 16 + 2 : x * 16 + 11, :]
    put_split(own_field, 0, pack[...])
    put_split(own_field, 32, next_z(pack[...]))
    frac = row3(state, slice(None))
    cells = row3(labels, slice(None))
    sampled = pick_from(own_field, hot[...])
    slopes = mix_slopes(
        axis_hits(27, CY + 1, 32, cells[0], cells[1]), frac, [sampled[0:32, :], sampled[32:64, :]]
    )
    for d in range(3):
        total = partial[d : d + 1, :] + slopes[d]
        grad_pos[d : d + 1, :] = total
        grad_mom[d : d + 1, :] = grads[d + 3 : d + 4, :] + STEP * total


def swap(up, down, axis):
    peers = lax.axis_size(axis)
    forward = [(i, (i + 1) % peers) for i in range(peers)]
    backward = [((i + 1) % peers, i) for i in range(peers)]
    return lax.ppermute(up, axis, forward), lax.ppermute(down, axis, backward)


def gather_y(x):
    return lax.all_gather(x, "gy", axis=0, tiled=False)


def local(pos, mom, cell, cell_second, dest, slot, pull_pos, pull_mom):
    place = lax.axis_index("gy").astype(jnp.int32).reshape(1)
    dest = dest.reshape(1, NQ)
    slot = slot.reshape(1, NQ)
    scalar = pl.BlockSpec(memory_space=pltpu.SMEM)
    vmem = pl.BlockSpec(memory_space=pltpu.VMEM)

    def call_at(body, outs, scratch, operands):
        return pl.pallas_call(
            body,
            out_shape=outs,
            in_specs=[scalar] + [vmem] * operands,
            scratch_shapes=list(scratch),
            compiler_params=pltpu.CompilerParams(vmem_limit_bytes=VMEM_LIMIT),
        )

    depth, lines = call_at(
        depth_body, (shape(2 * NZ, NZ, dtype=BF16), shape(LINES, 192, dtype=BF16)), [], 0
    )(place)
    in_hbm = [
        pltpu.with_memory_space_constraint(x, pltpu.HBM)
        for x in (pos, mom, cell, dest, slot, pull_pos, pull_mom)
    ]
    own, up, down, lent, state, labels, hot = pl.pallas_call(
        deposit_first_body,
        out_shape=(
            shape(48, NZ),
            shape(128, NZ),
            shape(128, NZ),
            shape(48, NZ),
            shape(6, NQ),
            shape(5, NQ, dtype=jnp.int32),
            shape(NZ, NQ, dtype=BF16),
        ),
        in_specs=[pl.BlockSpec(memory_space=pltpu.HBM)] * 7,
        scratch_shapes=[
            pltpu.VMEM((4, 3, NQ), F32),
            pltpu.VMEM((3, NQ), jnp.int32),
            pltpu.VMEM((2, 1, NQ), jnp.int32),
            pltpu.SemaphoreType.DMA((7,)),
            pltpu.VMEM((128, BLK), BF16),
            pltpu.VMEM((64, NZ), F32),
        ],
        compiler_params=pltpu.CompilerParams(vmem_limit_bytes=VMEM_LIMIT),
    )(*in_hbm)
    mine, (left, right) = up, swap(up, down, "gx")
    first_left, first_right = left, right
    wanted, ranks = call(
        requests_body,
        (shape(8, NZ), shape(1, NQ, dtype=jnp.int32)),
        [pltpu.VMEM((32, NZ), F32), pltpu.VMEM((16, NQ), F32)],
    )(labels)
    gathered = gather_y(call(fold_first_body, shape(96, NZ))(own, left, right, up, wanted))
    replies = call_at(replies_body, shape(8, NZ), [pltpu.VMEM((96, NZ), BF16)], 2)(place, gathered, lent)
    own, up, down, drift, pulls, fields = call_at(
        step_body,
        (
            shape(144, NZ),
            shape(96, NZ),
            shape(96, NZ),
            shape(3, NQ),
            shape(3, NQ),
            shape(384, NZ, dtype=BF16),
        ),
        [
            pltpu.VMEM((80, NZ), F32),
            pltpu.VMEM((96, NZ), F32),
            pltpu.VMEM((480, NZ), BF16),
            pltpu.VMEM((896, BLK), BF16),
            pltpu.VMEM((448, NZ), F32),
            pltpu.VMEM((4, 5, ROWS, NZ), F32),
        ],
        9,
    )(place, state, labels, hot, depth, lines, gathered, mine, left, right)
    left, right = swap(up, down, "gx")
    gathered = gather_y(call(fold_second_body, shape(112, NZ))(own, left, right, replies))
    own, up, down = call(lines_body, (shape(144, NZ), shape(80, NZ), shape(80, NZ)))(depth, lines, gathered)
    left, right = swap(up, down, "gx")
    pulls_pos = call_at(
        pulls_body,
        shape(3, NQ),
        [pltpu.VMEM((288, NZ), BF16), pltpu.VMEM((16, NZ), F32), pltpu.VMEM((32, NZ), BF16)],
        6,
    )(place, labels, ranks, lent, first_left, first_right, gathered)
    own, up, down, grads = call(
        back_body,
        (shape(48, NZ), shape(32, NZ), shape(32, NZ), shape(6, NQ)),
        [
            pltpu.VMEM((3, 112, NZ), F32),
            pltpu.VMEM((224, NZ), F32),
            pltpu.VMEM((896, NZ), BF16),
            pltpu.VMEM((384, BLK), BF16),
            pltpu.VMEM((192, NZ), F32),
            pltpu.VMEM((3, 7, ROWS, NZ), F32),
        ],
    )(state, labels, hot, drift, pulls, pulls_pos, own, left, right)
    left, right = swap(up, down, "gx")
    gathered = gather_y(call(fold_third_body, shape(48, NZ))(own, left, right))
    partial = call(push_body, shape(3, NQ))(state, labels, hot, grads, fields)
    return call(
        last_body,
        (shape(3, NQ), shape(3, NQ)),
        [pltpu.VMEM((48, NZ), F32), pltpu.VMEM((32, NZ), F32), pltpu.VMEM((128, NZ), BF16)],
    )(state, labels, hot, depth, lines, grads, partial, gathered)


def solution(mesh):
    both = ("gx", "gy")
    return jax.shard_map(
        local,
        mesh=mesh,
        in_specs=(P(None, both), P(None, both), P(None, both), P(None, both), P(both), P(both), P(None, both), P(None, both)),
        out_specs=(P(None, both), P(None, both)),
        check_vma=False,
    )
```

```python
import functools

import jax
import jax.numpy as jnp
from jax import lax
from jax.experimental import pallas as pl
from jax.experimental.pallas import tpu as pltpu
from jax.sharding import PartitionSpec as P

CX = 2
CY = 8
NZ = 256
NQ = 4096
BLK = 4096
ROWS = 16
TABLES = 5
STEP = 0.25
STRENGTH = 0.02
F32 = jnp.float32
BF16 = jnp.bfloat16
highest = lax.Precision.HIGHEST
SECOND_SPANS = [(11 * p, 11, -1) for p in range(6)] + [(66 + 13 * p, 13, -2) for p in range(3)]
REPLIES = 105
PHASES = [
    ([(9 * p, 9, 0) for p in range(5)], 16, 96),
    (SECOND_SPANS, 24, 112),
    ([(16 * p, 16, -2) for p in range(3)], 16, 48),
]
LINES = 32 * sum(len(spans) for spans, _, _ in PHASES)
VMEM_LIMIT = 24 * 1024 * 1024


def shape(*dims, dtype=F32):
    return jax.ShapeDtypeStruct(dims, dtype)


def call(body, outs, scratch=()):
    return pl.pallas_call(
        body,
        out_shape=outs,
        scratch_shapes=list(scratch),
        compiler_params=pltpu.CompilerParams(vmem_limit_bytes=VMEM_LIMIT),
    )


def split(x):
    high = x.astype(BF16)
    return high, (x - high.astype(F32)).astype(BF16)


def one_hot(index):
    rows = lax.broadcasted_iota(jnp.int32, (256, index.shape[1]), 0)
    return jnp.where(rows == index, 1.0, 0.0).astype(BF16)


def one_hot_columns(index):
    width = index.shape[1]
    down = jnp.transpose(jnp.broadcast_to(index, (8, width)))[:, 0:1]
    columns = lax.broadcasted_iota(jnp.int32, (width, 256), 1)
    return jnp.where(columns == down, 1.0, 0.0).astype(BF16)


MODE_S = "rows"
MODE_D = "nt"


def put_split(ref, first, values):
    rows = values.shape[0]
    high, low = split(values)
    half = ref.shape[0] // 2
    ref[first : first + rows, :] = high
    ref[half + first : half + first + rows, :] = low


def halves(x):
    half = x.shape[0] // 2
    return x[:half] + x[half:]


def pick_from(table, hot):
    return halves(jnp.dot(table[...], hot, preferred_element_type=F32))


def spread_onto(values, hot):
    return halves(
        lax.dot_general(values[...], hot, (((1,), (1,)), ((), ())), preferred_element_type=F32)
    )


def next_z(x):
    return pltpu.roll(x, NZ - 1, 1)


def prev_z(x):
    return pltpu.roll(x, 1, 1)


def diff_z(x):
    return 0.5 * (next_z(x) - prev_z(x))


def diff_row(x):
    return 0.5 * (pltpu.roll(x, ROWS - 1, 0) - pltpu.roll(x, 1, 0))


def axis_hits(rows, pitch, padded, cell_x, cell_y):
    index = lax.broadcasted_iota(jnp.int32, (padded, 1), 0)
    row_x = index // pitch
    row_y = index - row_x * pitch
    return row_x == cell_x, row_x - 1 == cell_x, row_y == cell_y, row_y - 1 == cell_y


def weights_of(hits, frac_x, frac_y):
    low_x, high_x, low_y, high_y = hits
    along_x = jnp.where(low_x, 1.0 - frac_x, jnp.where(high_x, frac_x, 0.0))
    along_y = jnp.where(low_y, 1.0 - frac_y, jnp.where(high_y, frac_y, 0.0))
    return along_x, along_y


def slopes_of(hits):
    low_x, high_x, low_y, high_y = hits
    along_x = jnp.where(low_x, -1.0, jnp.where(high_x, 1.0, 0.0))
    along_y = jnp.where(low_y, -1.0, jnp.where(high_y, 1.0, 0.0))
    return along_x, along_y


def row3(ref, at, first=0):
    return [ref[first + k : first + k + 1, at] for k in range(3)]


def line_matrix(me, window, offset, rows, first_y):
    target = lax.broadcasted_iota(jnp.int32, (ROWS, 8 * window), 0)
    column = lax.broadcasted_iota(jnp.int32, (ROWS, 8 * window), 1)
    device = column // window
    source = column - device * window - offset
    away = (CY * (me - device) + target - 2 - source - first_y + 128) & 63
    away = jnp.minimum(away, 64 - away)
    weight = STRENGTH * jnp.exp(away.astype(F32) * (-1.0 / 16.0))
    return jnp.where((source >= 0) & (source < rows), weight, 0.0)


def depth_body(place, out, lines):
    target = lax.broadcasted_iota(jnp.int32, (NZ, NZ), 0)
    source = lax.broadcasted_iota(jnp.int32, (NZ, NZ), 1)
    away = jnp.abs(target - source)
    away = jnp.minimum(away, NZ - away)
    put_split(out, 0, jnp.exp(away.astype(F32) * (-1.0 / 16.0)))
    at = 0
    for spans, window, total in PHASES:
        for start, rows, first_y in spans:
            matrix = line_matrix(place[0], window, start - window_start(start, window, total), rows, first_y)
            high, low = split(matrix)
            lines[at : at + 16, 0 : 8 * window] = high
            lines[at + 16 : at + 32, 0 : 8 * window] = low
            at += 32


def window_start(start, window, total):
    return min(start // 8 * 8, total - window)


def product(a_high, a_low, b_high, b_low):
    dot = functools.partial(jnp.dot, preferred_element_type=F32)
    return dot(a_high, b_high) + (dot(a_high, b_low) + dot(a_low, b_high))


def smooth(depth, lines, gathered, phase, kept):
    spans, window, total = PHASES[phase]
    at = 32 * sum(len(PHASES[n][0]) for n in range(phase))
    for p, (start, _, _) in enumerate(spans):
        first = window_start(start, window, total)
        source = gathered[:, first : first + window, :].reshape(8 * window, NZ)
        along = lines[at : at + 16, 0 : 8 * window], lines[at + 16 : at + 32, 0 : 8 * window]
        kept[p * ROWS : (p + 1) * ROWS, :] = product(*along, *split(source))
        at += 32
    kept[0 : len(spans) * ROWS, :] = product(
        *split(kept[0 : len(spans) * ROWS, :]), depth[0:NZ, :], depth[NZ : 2 * NZ, :]
    )


def select_pulls(table, where_to, moved):
    taken = pick_from(table, one_hot(where_to & 255))
    rows = taken.shape[0] // 3
    chosen = moved * 16 + lax.shift_right_logical(where_to, 8)
    here = lax.broadcasted_iota(jnp.int32, (rows, where_to.shape[1]), 0) == chosen
    return [
        jnp.sum(jnp.where(here, taken[k * rows : k * rows + rows, :], 0.0), axis=0, keepdims=True)
        for k in range(3)
    ]


def requests_body(labels, wanted, ranks, marks, lists):
    for c in range(16):
        part = labels[3:4, c * 256 : (c + 1) * 256]
        marks[c : c + 1, :] = jnp.where(part == 3, 1.0, 0.0)
        marks[16 + c : 17 + c, :] = jnp.where(part == 4, 1.0, 0.0)
    row = lax.broadcasted_iota(jnp.int32, (256, 256), 0)
    column = lax.broadcasted_iota(jnp.int32, (256, 256), 1)
    earlier = jnp.where(row < column, 1.0, 0.0).astype(BF16)
    within = jnp.dot(marks[...].astype(BF16), earlier, preferred_element_type=F32)
    totals = jnp.broadcast_to(jnp.sum(marks[...], axis=1, keepdims=True), (32, 256))
    row = lax.broadcasted_iota(jnp.int32, (32, 32), 0)
    column = lax.broadcasted_iota(jnp.int32, (32, 32), 1)
    earlier = jnp.where((column < row) & (row // 16 == column // 16), 1.0, 0.0).astype(BF16)
    marks[...] = within + jnp.dot(earlier, totals.astype(BF16), preferred_element_type=F32)
    for c in range(16):
        part = labels[3:4, c * 256 : (c + 1) * 256]
        place = jnp.where(part == 3, marks[c : c + 1, :], jnp.where(part == 4, marks[16 + c : 17 + c, :], -1.0))
        ranks[0:1, c * 256 : (c + 1) * 256] = place.astype(jnp.int32)
    moved = labels[3:4, :]
    where_to = labels[4:5, :]
    upper = lax.shift_right_logical(where_to, 8).astype(F32)
    lower = (where_to & 255).astype(F32)
    lists[...] = jnp.zeros_like(lists)
    lists[0:1, :] = jnp.where(moved == 3, upper, 0.0)
    lists[1:2, :] = jnp.where(moved == 3, lower, 0.0)
    lists[2:3, :] = jnp.where(moved == 4, upper, 0.0)
    lists[3:4, :] = jnp.where(moved == 4, lower, 0.0)
    placed = lax.dot_general(
        lists[...].astype(BF16), one_hot(ranks[...]), (((1,), (1,)), ((), ())), preferred_element_type=F32
    )
    wanted[...] = jnp.zeros_like(wanted)
    wanted[0:1, :] = placed[0:1, :] * 256.0 + placed[1:2, :]
    wanted[1:2, :] = placed[2:3, :] * 256.0 + placed[3:4, :]


def replies_body(place, gathered, lent, out, table):
    put_split(table, 0, lent[...])
    out[...] = jnp.zeros_like(out)
    for n, side in enumerate((lax.rem(place[0] + 7, 8), lax.rem(place[0] + 1, 8))):
        wanted = gathered[side, 45 + n : 46 + n, :].astype(jnp.int32)
        taken = pick_from(table, one_hot(wanted & 255))
        here = lax.broadcasted_iota(jnp.int32, (16, 256), 0) == lax.shift_right_logical(wanted, 8)
        for k in range(3):
            row = n * 3 + k
            out[row : row + 1, :] = jnp.sum(
                jnp.where(here, taken[k * 16 : k * 16 + 16, :], 0.0), axis=0, keepdims=True
            )


def deposit_first_body(
    pos, mom, cell, dest, slot, pull_pos, pull_mom, own, up, down, lent, state, labels, hot, held, ints, lone, sems, lhs, acc
):
    copies = [
        pltpu.make_async_copy(pos, held.at[0], sems.at[0]),
        pltpu.make_async_copy(mom, held.at[1], sems.at[1]),
        pltpu.make_async_copy(cell, ints, sems.at[2]),
        pltpu.make_async_copy(dest, lone.at[0], sems.at[3]),
        pltpu.make_async_copy(slot, lone.at[1], sems.at[4]),
        pltpu.make_async_copy(pull_pos, held.at[2], sems.at[5]),
        pltpu.make_async_copy(pull_mom, held.at[3], sems.at[6]),
    ]
    for copy in copies:
        copy.start()
    own[...] = jnp.zeros_like(own)
    acc[...] = jnp.zeros_like(acc)
    copies[0].wait()
    copies[1].wait()
    state[0:3, :] = held[0] + STEP * held[1]
    state[3:6, :] = held[1]
    copies[2].wait()
    labels[0:3, :] = ints[...]
    hot[...] = one_hot(ints[2:3, :])

    def block(b, carry):
        at = pl.ds(pl.multiple_of(b * BLK, BLK), BLK)
        frac = row3(state, at)
        cells = row3(labels, at)
        along_x, along_y = weights_of(axis_hits(27, CY + 1, 32, cells[0], cells[1]), frac[0], frac[1])
        planar = along_x * along_y
        put_split(lhs, 0, planar * (1.0 - frac[2]))
        put_split(lhs, 32, planar * frac[2])
        acc[...] += spread_onto(lhs, hot[...])
        return carry

    lax.fori_loop(0, NQ // BLK, block, 0)
    density = acc[0:32, :] + prev_z(acc[32:64, :])
    for x in range(3):
        own[x * ROWS + 2 : x * ROWS + 11, :] = density[x * 9 : x * 9 + 9, :]
    up[0:32, :] = own[16:48, :]
    down[0:32, :] = own[0:32, :]
    for copy in copies[3:]:
        copy.wait()
    labels[3:4, :] = lone[0]
    labels[4:5, :] = lone[1]
    for k in range(6):
        source = held.at[2 + k // 3]
        for c in range(16):
            line = source[k % 3 : k % 3 + 1, c * 256 : (c + 1) * 256]
            at_row = 32 + k * 16 + c
            up[at_row : at_row + 1, :] = line
            down[at_row : at_row + 1, :] = line
            if k < 3:
                lent[at_row - 32 : at_row - 31, :] = line


def fold_first_body(own, left, right, pulls, wanted, out):
    rows = slice(2, 11)
    out[0:9, :] = left[0:16, :][rows]
    out[9:18, :] = (own[0:16, :] + left[16:32, :])[rows]
    out[18:27, :] = own[16:32, :][rows]
    out[27:36, :] = (own[32:48, :] + right[0:16, :])[rows]
    out[36:45, :] = right[16:32, :][rows]
    out[45:48, :] = wanted[0:3, :]
    out[48:96, :] = pulls[80:128, :]


def step_body(
    place,
    state,
    labels,
    hot,
    depth,
    lines,
    gathered,
    mine,
    left,
    right,
    own,
    up,
    down,
    drift,
    pulls,
    fields,
    kept,
    pack,
    table,
    lhs,
    acc,
    planes,
):
    smooth(depth, lines, gathered, 0, kept)
    pack[...] = jnp.zeros_like(pack)
    for x in range(3):
        mid = (x + 1) * ROWS
        east = kept[mid + 18 : mid + 27, :]
        west = kept[mid - 14 : mid - 5, :]
        pack[x * 9 : x * 9 + 9, :] = -0.5 * (east - west)
        north = kept[mid + 3 : mid + 12, :]
        south = kept[mid + 1 : mid + 10, :]
        pack[32 + x * 9 : 32 + x * 9 + 9, :] = -0.5 * (north - south)
        pack[64 + x * 9 : 64 + x * 9 + 9, :] = -diff_z(kept[mid : mid + 16, :])[2:11, :]
    put_split(fields, 0, pack[...])
    put_split(fields, 96, next_z(pack[...]))
    ahead = lax.rem(place[0] + 1, 8)
    behind = lax.rem(place[0] + 7, 8)

    def rows_of(device):
        return lambda row: gathered[device, 48 + row : 64 + row, :]

    fill_table(
        table, [rows_at(mine, 80), rows_at(right, 80), rows_at(left, 80), rows_of(ahead), rows_of(behind)]
    )
    acc[...] = jnp.zeros_like(acc)

    def block(b, carry):
        at = pl.ds(pl.multiple_of(b * BLK, BLK), BLK)
        frac = row3(state, at)
        momentum = row3(state, at, 3)
        cells = row3(labels, at)
        moved = labels[3:4, at]
        where_to = labels[4:5, at]
        along_x, along_y = weights_of(axis_hits(27, CY + 1, 32, cells[0], cells[1]), frac[0], frac[1])
        planar = along_x * along_y
        sampled = pick_from(fields, hot[...])
        lower = planar * (1.0 - frac[2])
        upper = planar * frac[2]
        force = [
            jnp.sum(
                lower * sampled[d * 32 : d * 32 + 32, :] + upper * sampled[96 + d * 32 : 128 + d * 32, :],
                axis=0,
                keepdims=True,
            )
            for d in range(3)
        ]
        to_x = jnp.where(moved == 1, 1, jnp.where(moved == 2, -1, 0))
        to_y = jnp.where(moved == 3, 1, jnp.where(moved == 4, -1, 0))
        shift = [to_x.astype(F32), to_y.astype(F32), 0.0]
        second = [frac[d] - shift[d] + STEP * (momentum[d] + STEP * force[d]) for d in range(3)]
        home = select_pulls(table, where_to, moved)
        for d in range(3):
            drift[d : d + 1, at] = second[d]
            pulls[d : d + 1, at] = home[d]
        along_x, along_y = weights_of(
            axis_hits(55, CY + 3, 56, cells[0] + to_x + 1, cells[1] + to_y + 1), second[0], second[1]
        )
        planar = along_x * along_y
        upper = planar * second[2]
        lower = planar - upper
        for c in range(4):
            scale = None if c == 0 else STEP * home[c - 1]
            both = jnp.concatenate([lower, upper], 0)
            put_split(lhs, c * 112, both if c == 0 else both * scale)
        acc[...] += spread_onto(lhs, hot[...])
        return carry

    lax.fori_loop(0, NQ // BLK, block, 0)
    planes[...] = jnp.zeros_like(planes)
    for c in range(4):
        total = acc[c * 112 : c * 112 + 56, :] + prev_z(acc[c * 112 + 56 : c * 112 + 112, :])
        for x in range(5):
            planes[c, x, 1:12, :] = total[x * 11 : x * 11 + 11, :]
    for x in range(5):
        planes[2, x] = diff_row(planes[2, x]) + diff_z(planes[3, x])
    for c in range(3):
        for x in range(3):
            own[(c * 3 + x) * 16 : (c * 3 + x) * 16 + 16, :] = planes[c, x + 1]
        for x in range(2):
            up[(c * 2 + x) * 16 : (c * 2 + x) * 16 + 16, :] = planes[c, x + 3]
            down[(c * 2 + x) * 16 : (c * 2 + x) * 16 + 16, :] = planes[c, x]


def fill_table(table, sources):
    for k in range(3):
        for t, source in enumerate(sources):
            put_split(table, (k * len(sources) + t) * 16, source(k * 16))


def rows_at(ref, first):
    return lambda row: ref[first + row : first + row + 16, :]


def pulls_body(place, labels, ranks, mine, left, right, gathered, pulls, table, lists, replied):
    fill_table(table, [rows_at(mine, 0), rows_at(right, 32), rows_at(left, 32)])
    moved = labels[3:4, :]
    home = select_pulls(table, labels[4:5, :], moved)
    lists[...] = jnp.zeros_like(lists)
    lists[0:3, :] = gathered[lax.rem(place[0] + 1, 8), REPLIES : REPLIES + 3, :]
    lists[3:6, :] = gathered[lax.rem(place[0] + 7, 8), REPLIES + 3 : REPLIES + 6, :]
    put_split(replied, 0, lists[...])
    taken = pick_from(replied, one_hot(ranks[...]))
    for d in range(3):
        from_y = jnp.where(moved == 3, taken[d : d + 1, :], jnp.where(moved == 4, taken[d + 3 : d + 4, :], 0.0))
        pulls[d : d + 1, :] = home[d] + from_y


def fold_planes(own, left, right, channel):
    mine, theirs = channel * 48, channel * 32
    first = own[mine : mine + 16, :] + left[theirs : theirs + 16, :]
    second = (
        own[mine + 16 : mine + 32, :] + left[theirs + 16 : theirs + 32, :] + right[theirs : theirs + 16, :]
    )
    third = own[mine + 32 : mine + 48, :] + right[theirs + 16 : theirs + 32, :]
    return first, second, third


def fold_second_body(own, left, right, replies, out):
    for c in range(3):
        for n, values in enumerate(fold_planes(own, left, right, c)):
            start, rows, first_y = SECOND_SPANS[c * 3 + n]
            out[start : start + rows, :] = values[first_y + 2 : first_y + 2 + rows]
    out[REPLIES : REPLIES + 7, :] = replies[0:7, :]


def fold_third_body(own, left, right, out):
    for n, values in enumerate(fold_planes(own, left, right, 0)):
        out[n * 16 : n * 16 + 16, :] = values


def lines_body(depth, lines, gathered, own, up, down):
    smooth(depth, lines, gathered, 1, own)
    for c in range(2):
        up[c * 32 : c * 32 + 32, :] = own[c * 48 : c * 48 + 32, :]
        down[c * 32 : c * 32 + 32, :] = own[c * 48 + 16 : c * 48 + 48, :]
    up[64:80, :] = own[112:128, :]
    down[64:80, :] = own[112:128, :]


def slope_weights(hits, frac_x, frac_y):
    along_x, along_y = weights_of(hits, frac_x, frac_y)
    slope_x, slope_y = slopes_of(hits)
    return slope_x * along_y, slope_y * along_x, along_x * along_y


def back_body(
    state, labels, hot, drift, pulls, pulls_pos, mine, left, right, own, up, down, grads, wide, pack, fields, lhs, acc, planes
):
    for c in range(2):
        wide[c, 0:32, :] = left[c * 32 : c * 32 + 32, :]
        wide[c, 32:80, :] = mine[c * 48 : c * 48 + 48, :]
        wide[c, 80:112, :] = right[c * 32 : c * 32 + 32, :]
    wide[2, 16:32, :] = left[64:80, :]
    wide[2, 32:80, :] = mine[96:144, :]
    wide[2, 80:96, :] = right[64:80, :]
    pack[...] = jnp.zeros_like(pack)
    for x in range(5):
        mid = (x + 1) * 16
        first = x * 11
        pack[first : first + 11, :] = -0.5 * (wide[0, mid + 17 : mid + 28, :] - wide[0, mid - 15 : mid - 4, :])
        pack[56 + first : 67 + first, :] = -0.5 * (
            wide[0, mid + 2 : mid + 13, :] - wide[0, mid : mid + 11, :]
        )
        pack[112 + first : 123 + first, :] = -diff_z(wide[0, mid : mid + 16, :])[1:12, :]
        pack[168 + first : 179 + first, :] = (
            0.5 * (wide[1, mid + 17 : mid + 28, :] - wide[1, mid - 15 : mid - 4, :])
            + wide[2, mid + 1 : mid + 12, :]
        )
    put_split(fields, 0, pack[...])
    put_split(fields, 224, next_z(pack[...]))
    acc[...] = jnp.zeros_like(acc)

    def block(b, carry):
        at = pl.ds(pl.multiple_of(b * BLK, BLK), BLK)
        cells = row3(labels, at)
        moved = labels[3:4, at]
        second = row3(drift, at)
        pull_position = row3(pulls_pos, at)
        pull_momentum = row3(pulls, at)
        to_x = jnp.where(moved == 1, 1, jnp.where(moved == 2, -1, 0))
        to_y = jnp.where(moved == 3, 1, jnp.where(moved == 4, -1, 0))
        hits = axis_hits(55, CY + 3, 56, cells[0] + to_x + 1, cells[1] + to_y + 1)
        along_x, along_y = weights_of(hits, second[0], second[1])
        slope_x, slope_y = slopes_of(hits)
        sampled = pick_from(fields, hot[...])
        sides = []
        for s in range(2):
            mixed = sampled[s * 224 + 168 : s * 224 + 224, :]
            for d in range(3):
                mixed = mixed + (STEP * pull_momentum[d]) * sampled[s * 224 + d * 56 : s * 224 + d * 56 + 56, :]
            sides.append(mixed)
        level = sides[0] + second[2] * (sides[1] - sides[0])
        rise = sides[1] - sides[0]
        slopes = [
            jnp.sum(slope_x * (along_y * level), axis=0, keepdims=True),
            jnp.sum(slope_y * (along_x * level), axis=0, keepdims=True),
            jnp.sum(along_x * (along_y * rise), axis=0, keepdims=True),
        ]
        grad_drift = [pull_position[d] + slopes[d] for d in range(3)]
        grad_kick = [pull_momentum[d] + STEP * grad_drift[d] for d in range(3)]
        for d in range(3):
            grads[d : d + 1, at] = grad_drift[d]
            grads[d + 3 : d + 4, at] = grad_kick[d]
        frac = row3(state, at)
        along_x, along_y = weights_of(axis_hits(27, CY + 1, 32, cells[0], cells[1]), frac[0], frac[1])
        planar = along_x * along_y
        above = planar * frac[2]
        below = planar - above
        for c in range(3):
            scale = STEP * grad_kick[c]
            put_split(lhs, c * 64, below * scale)
            put_split(lhs, c * 64 + 32, above * scale)
        acc[...] += spread_onto(lhs, hot[...])
        return carry

    lax.fori_loop(0, NQ // BLK, block, 0)
    planes[...] = jnp.zeros_like(planes)
    for c in range(3):
        total = acc[c * 64 : c * 64 + 32, :] + prev_z(acc[c * 64 + 32 : c * 64 + 64, :])
        for x in range(3):
            planes[c, x + 2, 2:11, :] = total[x * 9 : x * 9 + 9, :]
    for x in range(5):
        spread = 0.5 * (planes[0, x + 2] - planes[0, x])
        if 1 <= x <= 3:
            spread = spread + diff_row(planes[1, x + 1]) + diff_z(planes[2, x + 1])
        if 1 <= x <= 3:
            own[(x - 1) * 16 : x * 16, :] = spread
        if x >= 3:
            up[(x - 3) * 16 : (x - 2) * 16, :] = spread
        if x <= 1:
            down[x * 16 : (x + 1) * 16, :] = spread


def mix_slopes(weights, frac_z, sides):
    rise = sides[1] - sides[0]
    level = sides[0] + frac_z * rise
    return [
        jnp.sum(weights[d] * (level if d < 2 else rise), axis=0, keepdims=True) for d in range(3)
    ]


def push_body(state, labels, hot, grads, fields, out, weights):
    frac = row3(state, slice(None))
    cells = row3(labels, slice(None))
    grad_kick = row3(grads, slice(None), 3)
    sampled = pick_from(fields, hot[...])
    sides = []
    for s in range(2):
        mixed = (STEP * grad_kick[0]) * sampled[s * 96 : s * 96 + 32, :]
        for d in range(1, 3):
            mixed = mixed + (STEP * grad_kick[d]) * sampled[s * 96 + d * 32 : s * 96 + d * 32 + 32, :]
        sides.append(mixed)
    hits = axis_hits(27, CY + 1, 32, cells[0], cells[1])
    for n, values in enumerate(slope_weights(hits, frac[0], frac[1])):
        weights[n] = values
    slopes = mix_slopes(weights, frac[2], sides)
    for d in range(3):
        out[d : d + 1, :] = grads[d : d + 1, :] + slopes[d]


def last_body(state, weights, hot, depth, lines, grads, partial, gathered, grad_pos, grad_mom, kept, pack, own_field):
    smooth(depth, lines, gathered, 2, kept)
    pack[...] = jnp.zeros_like(pack)
    for x in range(3):
        pack[x * 9 : x * 9 + 9, :] = kept[x * 16 + 2 : x * 16 + 11, :]
    put_split(own_field, 0, pack[...])
    put_split(own_field, 32, next_z(pack[...]))
    sampled = pick_from(own_field, hot[...])
    slopes = mix_slopes(weights, state[2:3, :], [sampled[0:32, :], sampled[32:64, :]])
    for d in range(3):
        total = partial[d : d + 1, :] + slopes[d]
        grad_pos[d : d + 1, :] = total
        grad_mom[d : d + 1, :] = grads[d + 3 : d + 4, :] + STEP * total


def swap(up, down, axis):
    peers = lax.axis_size(axis)
    forward = [(i, (i + 1) % peers) for i in range(peers)]
    backward = [((i + 1) % peers, i) for i in range(peers)]
    return lax.ppermute(up, axis, forward), lax.ppermute(down, axis, backward)


def gather_y(x):
    return lax.all_gather(x, "gy", axis=0, tiled=False)


def local(pos, mom, cell, cell_second, dest, slot, pull_pos, pull_mom):
    place = lax.axis_index("gy").astype(jnp.int32).reshape(1)
    dest = dest.reshape(1, NQ)
    slot = slot.reshape(1, NQ)
    scalar = pl.BlockSpec(memory_space=pltpu.SMEM)
    vmem = pl.BlockSpec(memory_space=pltpu.VMEM)

    def call_at(body, outs, scratch, operands):
        return pl.pallas_call(
            body,
            out_shape=outs,
            in_specs=[scalar] + [vmem] * operands,
            scratch_shapes=list(scratch),
            compiler_params=pltpu.CompilerParams(vmem_limit_bytes=VMEM_LIMIT),
        )

    depth, lines = call_at(
        depth_body, (shape(2 * NZ, NZ, dtype=BF16), shape(LINES, 192, dtype=BF16)), [], 0
    )(place)
    in_hbm = [
        pltpu.with_memory_space_constraint(x, pltpu.HBM)
        for x in (pos, mom, cell, dest, slot, pull_pos, pull_mom)
    ]
    own, up, down, lent, state, labels, hot = pl.pallas_call(
        deposit_first_body,
        out_shape=(
            shape(48, NZ),
            shape(128, NZ),
            shape(128, NZ),
            shape(48, NZ),
            shape(6, NQ),
            shape(5, NQ, dtype=jnp.int32),
            shape(NZ, NQ, dtype=BF16),
        ),
        in_specs=[pl.BlockSpec(memory_space=pltpu.HBM)] * 7,
        scratch_shapes=[
            pltpu.VMEM((4, 3, NQ), F32),
            pltpu.VMEM((3, NQ), jnp.int32),
            pltpu.VMEM((2, 1, NQ), jnp.int32),
            pltpu.SemaphoreType.DMA((7,)),
            pltpu.VMEM((128, BLK), BF16),
            pltpu.VMEM((64, NZ), F32),
        ],
        compiler_params=pltpu.CompilerParams(vmem_limit_bytes=VMEM_LIMIT),
    )(*in_hbm)
    mine, (left, right) = up, swap(up, down, "gx")
    first_left, first_right = left, right
    wanted, ranks = call(
        requests_body,
        (shape(8, NZ), shape(1, NQ, dtype=jnp.int32)),
        [pltpu.VMEM((32, NZ), F32), pltpu.VMEM((16, NQ), F32)],
    )(labels)
    gathered = gather_y(call(fold_first_body, shape(96, NZ))(own, left, right, up, wanted))
    replies = call_at(replies_body, shape(8, NZ), [pltpu.VMEM((96, NZ), BF16)], 2)(place, gathered, lent)
    own, up, down, drift, pulls, fields = call_at(
        step_body,
        (
            shape(144, NZ),
            shape(96, NZ),
            shape(96, NZ),
            shape(3, NQ),
            shape(3, NQ),
            shape(384, NZ, dtype=BF16),
        ),
        [
            pltpu.VMEM((80, NZ), F32),
            pltpu.VMEM((96, NZ), F32),
            pltpu.VMEM((480, NZ), BF16),
            pltpu.VMEM((896, BLK), BF16),
            pltpu.VMEM((448, NZ), F32),
            pltpu.VMEM((4, 5, ROWS, NZ), F32),
        ],
        9,
    )(place, state, labels, hot, depth, lines, gathered, mine, left, right)
    left, right = swap(up, down, "gx")
    gathered = gather_y(call(fold_second_body, shape(112, NZ))(own, left, right, replies))
    own, up, down = call(lines_body, (shape(144, NZ), shape(80, NZ), shape(80, NZ)))(depth, lines, gathered)
    left, right = swap(up, down, "gx")
    pulls_pos = call_at(
        pulls_body,
        shape(3, NQ),
        [pltpu.VMEM((288, NZ), BF16), pltpu.VMEM((16, NZ), F32), pltpu.VMEM((32, NZ), BF16)],
        6,
    )(place, labels, ranks, lent, first_left, first_right, gathered)
    own, up, down, grads = call(
        back_body,
        (shape(48, NZ), shape(32, NZ), shape(32, NZ), shape(6, NQ)),
        [
            pltpu.VMEM((3, 112, NZ), F32),
            pltpu.VMEM((224, NZ), F32),
            pltpu.VMEM((896, NZ), BF16),
            pltpu.VMEM((384, BLK), BF16),
            pltpu.VMEM((192, NZ), F32),
            pltpu.VMEM((3, 7, ROWS, NZ), F32),
        ],
    )(state, labels, hot, drift, pulls, pulls_pos, own, left, right)
    left, right = swap(up, down, "gx")
    gathered = gather_y(call(fold_third_body, shape(48, NZ))(own, left, right))
    partial, near_weights = call(push_body, (shape(3, NQ), shape(3, 32, NQ)))(state, labels, hot, grads, fields)
    return call(
        last_body,
        (shape(3, NQ), shape(3, NQ)),
        [pltpu.VMEM((48, NZ), F32), pltpu.VMEM((32, NZ), F32), pltpu.VMEM((128, NZ), BF16)],
    )(state, near_weights, hot, depth, lines, grads, partial, gathered)


def solution(mesh):
    both = ("gx", "gy")
    return jax.shard_map(
        local,
        mesh=mesh,
        in_specs=(P(None, both), P(None, both), P(None, both), P(None, both), P(both), P(both), P(None, both), P(None, both)),
        out_specs=(P(None, both), P(None, both)),
        check_vma=False,
    )
```
